32 devices in a mesh: dp: 16 (over z, y, x), tensor: 2 (over core).
Axes of the slice: x: 2, y: 2, z: 4, core: 2. Of those that a mesh axis runs over, the one named last changes fastest.
Arguments:
- inputs: bfloat16 [32, 1024, 768], P('dp'), may hold values from -6 to 6
- segments: int32 [32, 1024], P('dp'), may hold values from 0 to 1, as said below
- token_marks: int32 [32, 1024], P('dp'), may hold values from 0 to 1, as said below
- cotangent: bfloat16 [32, 1024, 768], P('dp', 'tensor'), may hold values from -6 to 6
- heads_weight: float32 [3, 768, 768], P(None, 'dp', 'tensor')
- merge_weight: float32 [768, 768], P('tensor', 'dp')
- expand_weight: float32 [768, 3072], P('dp', 'tensor')
- reduce_weight: float32 [3072, 768], P('tensor', 'dp')
- norm_params: float32 [4, 768], P(None, ('dp', 'tensor'))
- first_heads: float32 [3, 768, 768], P(None, 'dp', 'tensor')
- first_merge: float32 [768, 768], P('tensor', 'dp')
- first_expand: float32 [768, 3072], P('dp', 'tensor')
- first_reduce: float32 [3072, 768], P('tensor', 'dp')
- first_norm: float32 [4, 768], P(None, ('dp', 'tensor')), may hold values from -4 to 4
- second_heads: float32 [3, 768, 768], P(None, 'dp', 'tensor'), may hold values from 0.01 to 1
- second_merge: float32 [768, 768], P('tensor', 'dp'), may hold values from 0.01 to 1
- second_expand: float32 [768, 3072], P('dp', 'tensor'), may hold values from 0.01 to 1
- second_reduce: float32 [3072, 768], P('tensor', 'dp'), may hold values from 0.01 to 1
- second_norm: float32 [4, 768], P(None, ('dp', 'tensor')), may hold values from 0.01 to 1
- step_count: int32 [], replicated, may hold values from 1 to 99
Outputs:
- layer_output: bfloat16 [32, 1024, 768], P('dp', 'tensor')
- input_grad: float32 [32, 1024, 768], P('dp', 'tensor')
- grad_heads: float32 [3, 768, 768], P(None, 'dp', 'tensor')
- grad_merge: float32 [768, 768], P('tensor', 'dp')
- grad_expand: float32 [768, 3072], P('dp', 'tensor')
- grad_reduce: float32 [3072, 768], P('tensor', 'dp')
- grad_norm: float32 [4, 768], P(None, ('dp', 'tensor'))
- next_first_heads: float32 [3, 768, 768], P(None, 'dp', 'tensor')
- next_first_merge: float32 [768, 768], P('tensor', 'dp')
- next_first_expand: float32 [768, 3072], P('dp', 'tensor')
- next_first_reduce: float32 [3072, 768], P('tensor', 'dp')
- next_first_norm: float32 [4, 768], P(None, ('dp', 'tensor'))
- next_second_heads: float32 [3, 768, 768], P(None, 'dp', 'tensor')
- next_second_merge: float32 [768, 768], P('tensor', 'dp')
- next_second_expand: float32 [768, 3072], P('dp', 'tensor')
- next_second_reduce: float32 [3072, 768], P('tensor', 'dp')
- next_second_norm: float32 [4, 768], P(None, ('dp', 'tensor'))
- next_heads_weight: float32 [3, 768, 768], P(None, 'dp', 'tensor')
- next_merge_weight: float32 [768, 768], P('tensor', 'dp')
- next_expand_weight: float32 [768, 3072], P('dp', 'tensor')
- next_reduce_weight: float32 [3072, 768], P('tensor', 'dp')
- next_norm_params: float32 [4, 768], P(None, ('dp', 'tensor'))
- trust_ratios: float32 [10], replicated
The draws below stay inside these ranges and needn't reach their ends.
Inputs may be any that keep to these rules, and one draw needn't show every extreme that they name: `segments`: each row holds segment 0, its first 256 to 511 tokens, then segment 1 up to the row's end. `token_marks`: in each row one to 78 positions are 1, in runs of one to three; some row holds exactly 78 of them, all among its first 512 tokens.
All inputs are finite; a program needn't handle non-finite values.
Results may differ from the reference program's by a relative error of at most 0.018.
The reference program's roundings to bfloat16 on the way count: a program that leaves them out, or rounds other values in their place, can miss the bound.
Values may be sent and summed in bfloat16 or wider, within the bound.
No kernel may reach another device: no remote copies, remote signals or barrier semaphores. Data moves between devices by JAX's collectives and lax.ppermute only.
A program may use at most 192 MiB of HBM per device.

```python
import math
from functools import partial
import jax
import jax.numpy as jnp
from jax import lax

D = 768
HEADS = 12
HEAD = 64
FF = 3072
SEQ = 1024
RUNS = 26
ROWS = 32


def ramp(length, spread):
    along = jnp.arange(length, dtype=jnp.float32) / (length - 1)
    factor = spread ** (along - 0.5)
    return factor / math.sqrt((spread - 1.0 / spread) / (2.0 * math.log(spread)))


def draw_heads_weight(key, part):
    key = jax.random.fold_in(key, 1)
    noise_draw = jax.random.normal(key, (3, D, D), jnp.float32)
    spread = 10.0
    heads_factor = jnp.array([1.5, 1.0, 1.0], jnp.float32)
    return noise_draw * ramp(D, spread)[None, :, None] * heads_factor[:, None, None] * D ** (-0.5)


def draw_merge_weight(key, part):
    key = jax.random.fold_in(key, 2)
    noise_draw = jax.random.normal(key, (D, D), jnp.float32)
    spread = 10.0
    return noise_draw * ramp(D, spread)[None, :] * (D // 16) ** (-0.5)


def draw_expand_weight(key, part):
    key = jax.random.fold_in(key, 3)
    noise_draw = jax.random.normal(key, (D, FF), jnp.float32)
    spread = 10.0
    return noise_draw * ramp(D, spread)[:, None] * D ** (-0.5)


def draw_reduce_weight(key, part):
    key = jax.random.fold_in(key, 4)
    noise_draw = jax.random.normal(key, (FF, D), jnp.float32)
    spread = 10.0
    return noise_draw * ramp(D, spread)[None, :] * FF ** (-0.5)


def draw_norm_params(key, part):
    key = jax.random.fold_in(key, 5)
    noise_draw = jax.random.normal(key, (4, D), jnp.float32)
    return jnp.stack([1.0 + 0.2 * noise_draw[0], 0.5 * noise_draw[1], 1.0 + 0.2 * noise_draw[2], 0.5 * noise_draw[3]])


def draw_first_heads(key, part):
    key = jax.random.fold_in(key, 6)
    noise_draw = jax.random.normal(key, (3, D, D), jnp.float32)
    spread = 10.0
    return noise_draw * ramp(D, spread)[None, :, None] * 0.3


def draw_first_merge(key, part):
    key = jax.random.fold_in(key, 7)
    noise_draw = jax.random.normal(key, (D, D), jnp.float32)
    spread = 10.0
    return noise_draw * ramp(D, spread)[None, :] * 0.3


def draw_first_expand(key, part):
    key = jax.random.fold_in(key, 8)
    noise_draw = jax.random.normal(key, (D, FF), jnp.float32)
    spread = 10.0
    return noise_draw * ramp(D, spread)[:, None] * 0.3


def draw_first_reduce(key, part):
    key = jax.random.fold_in(key, 9)
    noise_draw = jax.random.normal(key, (FF, D), jnp.float32)
    spread = 10.0
    return noise_draw * ramp(D, spread)[None, :] * 0.3


def draw_segments(key, part):
    key = jax.random.fold_in(key, 11)
    cut_at = SEQ // 4 + jax.random.randint(key, (ROWS, 1), 0, SEQ // 4)
    return (jnp.arange(SEQ, dtype=jnp.int32)[None, :] >= cut_at).astype(jnp.int32)


def draw_token_marks(key, part):
    key = jax.random.fold_in(key, 12)
    sub_keys = jax.random.split(key, 5)
    groups = SEQ // 4
    firsts = SEQ // 8
    run_count = jax.random.randint(sub_keys[0], (ROWS, 1), 1, RUNS + 1)
    span_len = jax.random.randint(sub_keys[2], (ROWS, RUNS), 1, 4)
    wide_scores = jax.random.randint(sub_keys[1], (ROWS, groups), 0, 1 << 20) * groups + jnp.arange(groups, dtype=jnp.int32)[None, :]
    blocks = jnp.argsort(wide_scores, axis=1)[:, :RUNS].astype(jnp.int32)
    near_scores = jax.random.randint(sub_keys[3], (ROWS, firsts), 0, 1 << 20) * firsts + jnp.arange(firsts, dtype=jnp.int32)[None, :]
    near_blocks = jnp.argsort(near_scores, axis=1)[:, :RUNS].astype(jnp.int32)
    chosen = jax.random.randint(sub_keys[4], (), 0, ROWS)
    full_row = (jnp.arange(ROWS, dtype=jnp.int32) == chosen)[:, None]
    run_count = jnp.where(full_row, RUNS, run_count)
    span_len = jnp.where(full_row, 3, span_len)
    blocks = jnp.where(full_row, near_blocks, blocks)
    active = jnp.arange(RUNS, dtype=jnp.int32)[None, :] < run_count
    position = jnp.arange(SEQ, dtype=jnp.int32)
    covered = (position[None, None, :] // 4 == blocks[:, :, None]) & (position[None, None, :] % 4 < span_len[:, :, None]) & active[:, :, None]
    return jnp.any(covered, axis=1).astype(jnp.int32)


def with_spikes(values, own_key, source, target, blocks, factor):
    owner, partner = [(jnp.arange(values.shape[axis_at]) // (values.shape[axis_at] // blocks)).reshape([-1 if axis == axis_at else 1 for axis in range(values.ndim)]) for axis_at in (source, target)]
    chosen = jax.random.permutation(own_key, blocks)[partner]
    strong = (owner == chosen) | (owner == (partner + blocks // 2) % blocks)
    return jnp.where(strong, factor * values, values)


def block_levels(key, shape, cuts, least, top_value):
    factor_of = 1.0
    for dim, parts in cuts:
        steps = jax.random.uniform(jax.random.fold_in(jax.random.fold_in(key, 6), dim), (parts,), jnp.float32, least / len(cuts), top_value / len(cuts))
        factor_of = factor_of * jnp.repeat(jnp.exp(steps), shape[dim] // parts).reshape((-1,) + (1,) * (len(shape) - 1 - dim))
    return factor_of


def scatter_about(key, extent, deviation, most, pieces=(), kind=jnp.bfloat16):
    factor_of = block_levels(key, extent, pieces, -0.22, 0.18) if pieces else 1.0
    entries = jax.random.normal(key, extent, jnp.float32) * deviation * factor_of
    return jnp.minimum(jnp.maximum(entries, -most), most).astype(kind)


def noise_with(stream_key, shape, width, most, cuts, heavy, held_as=jnp.bfloat16):
    values = width * jax.random.normal(stream_key, shape, jnp.float32)
    if cuts:
        values = values * block_levels(stream_key, shape, cuts, -0.22, 0.18)
    return jnp.clip(with_spikes(values, jax.random.fold_in(stream_key, 3), *heavy), -most, most).astype(held_as)


def setup_inputs(seed: int = 0) -> dict:
    key_list = jax.random.split(jax.random.key(seed), 21)
    return {
        "inputs": scatter_about(key_list[0], (ROWS, SEQ, D), 1.0, 6.0, ((0, 16),)),
        "segments": draw_segments(jax.random.fold_in(key_list[20], 71), 0),
        "token_marks": draw_token_marks(jax.random.fold_in(key_list[20], 71), 0),
        "cotangent": noise_with(key_list[3], (ROWS, SEQ, D), 1.0, 6.0, ((0, 16), (1, 2)), (0, 2, 16, 2.0)),
        "heads_weight": draw_heads_weight(jax.random.fold_in(key_list[20], 71), 0),
        "merge_weight": draw_merge_weight(jax.random.fold_in(key_list[20], 71), 0),
        "expand_weight": draw_expand_weight(jax.random.fold_in(key_list[20], 71), 0),
        "reduce_weight": draw_reduce_weight(jax.random.fold_in(key_list[20], 71), 0),
        "norm_params": draw_norm_params(jax.random.fold_in(key_list[20], 71), 0),
        "first_heads": draw_first_heads(jax.random.fold_in(key_list[20], 71), 0),
        "first_merge": draw_first_merge(jax.random.fold_in(key_list[20], 71), 0),
        "first_expand": draw_first_expand(jax.random.fold_in(key_list[20], 71), 0),
        "first_reduce": draw_first_reduce(jax.random.fold_in(key_list[20], 71), 0),
        "first_norm": scatter_about(key_list[13], (4, D), 0.3, 4.0, ((1, 32),), jnp.float32),
        "second_heads": jnp.clip(jnp.exp(math.log(1.0) - 4.6051702 * jax.random.uniform(key_list[14], (3, D, D), jnp.float32) ** block_levels(key_list[14], (3, D, D), ((1, 16), (2, 2)), -0.2, 0.2)), 0.01, 1.0),
        "second_merge": jnp.clip(jnp.exp(math.log(1.0) - 4.6051702 * jax.random.uniform(key_list[15], (D, D), jnp.float32) ** block_levels(key_list[15], (D, D), ((0, 2), (1, 16)), -0.2, 0.2)), 0.01, 1.0),
        "second_expand": jnp.clip(jnp.exp(math.log(1.0) - 4.6051702 * jax.random.uniform(key_list[16], (D, FF), jnp.float32) ** block_levels(key_list[16], (D, FF), ((0, 16), (1, 2)), -0.2, 0.2)), 0.01, 1.0),
        "second_reduce": jnp.clip(jnp.exp(math.log(1.0) - 4.6051702 * jax.random.uniform(key_list[17], (FF, D), jnp.float32) ** block_levels(key_list[17], (FF, D), ((0, 2), (1, 16)), -0.2, 0.2)), 0.01, 1.0),
        "second_norm": jnp.clip(jnp.exp(math.log(1.0) - 4.6051702 * jax.random.uniform(key_list[18], (4, D), jnp.float32) ** block_levels(key_list[18], (4, D), ((1, 32),), -0.2, 0.2)), 0.01, 1.0),
        "step_count": jax.random.randint(key_list[19], (), 1, 100).astype(jnp.int32),
    }


@jax.custom_vjp
def low(v):
    return lax.optimization_barrier(v.astype(jnp.bfloat16)).astype(jnp.float32)

@jax.custom_vjp
def low_back(v):
    return v

def low_keep(v):
    return (low(v), None)

def low_pass(kept, grad):
    return (grad,)

def back_keep(v):
    return (v, None)

def back_low(kept, grad):
    return (low(grad),)
low.defvjp(low_keep, low_pass)
low_back.defvjp(back_keep, back_low)
NORM_EPS = 1e-12
BETA_ONE = 0.9
BETA_TWO = 0.999
ADAM_EPS = 1e-06
DECAY = 0.01
RATE = 0.25
MASKED = -1000000000.0

def matmul_high(left, right):
    return jnp.matmul(left, right, precision=lax.Precision.HIGHEST)

def layer_norm(values, norm_gain, norm_shift):
    average = lax.optimization_barrier(jnp.mean(values, axis=-1, keepdims=True))
    centered = values - average
    spread = lax.optimization_barrier(jnp.mean(centered * centered, axis=-1, keepdims=True))
    return centered * lax.rsqrt(spread + NORM_EPS) * norm_gain + norm_shift

def gelu_tanh(values):
    return 0.5 * values * (1.0 + jnp.tanh(0.7978845608028654 * (values + 0.044715 * values * values * values)))

def row_block(weights, norms, rows_in, seg_rows):
    w_query, w_key, w_value, w_merge, w_expand, w_reduce = weights
    flat_rows = rows_in.reshape(-1, D)
    queries = low(low_back(matmul_high(flat_rows, w_query))).reshape(-1, SEQ, HEADS, HEAD)
    keys_all = low(low_back(matmul_high(flat_rows, w_key))).reshape(-1, SEQ, HEADS, HEAD)
    values_all = low(low_back(matmul_high(flat_rows, w_value))).reshape(-1, SEQ, HEADS, HEAD)
    same_doc = seg_rows[:, :, None] == seg_rows[:, None, :]
    scores = jnp.einsum('gqhd,gkhd->ghqk', queries, keys_all, precision=lax.Precision.HIGHEST) * HEAD ** (-0.5)
    scores = low_back(scores)
    masked = jnp.where(same_doc[:, None], scores, MASKED)
    row_top = lax.optimization_barrier(jnp.max(masked, axis=-1, keepdims=True))
    exp_scores = jnp.exp(masked - row_top)
    probabilities = low(exp_scores / lax.optimization_barrier(jnp.sum(exp_scores, axis=-1, keepdims=True)))
    context = jnp.einsum('ghqk,gkhd->gqhd', probabilities, values_all, precision=lax.Precision.HIGHEST).reshape(-1, D)
    context = low(low_back(context))
    attended = flat_rows + low_back(matmul_high(context, w_merge))
    normed = layer_norm(attended, norms[0], norms[1])
    inner = low_back(matmul_high(low(normed), w_expand))
    hidden = low(gelu_tanh(inner))
    joined = normed + low_back(matmul_high(hidden, w_reduce))
    return layer_norm(joined, norms[2], norms[3]).reshape(rows_in.shape)

def forward(start_rows, heads, merge, expand, reduce_w, norms, segments):
    weights = (low(heads[0]), low(heads[1]), low(heads[2]), low(merge), low(expand), low(reduce_w))
    groups = start_rows.reshape(ROWS // 2, 2, SEQ, D)
    seg_groups = segments.reshape(ROWS // 2, 2, SEQ)
    block_fn = jax.checkpoint(partial(row_block, weights, norms))

    def one_group(packed):
        return block_fn(packed[0], packed[1])
    result = lax.map(one_group, (groups, seg_groups))
    return result.reshape(ROWS, SEQ, D)

def squares(heads_part, merge_part, expand_part, reduce_part, norm_part):
    return jnp.concatenate([lax.optimization_barrier(jnp.sum(heads_part * heads_part, axis=(1, 2))), jnp.sum(merge_part * merge_part)[None], jnp.sum(expand_part * expand_part)[None], jnp.sum(reduce_part * reduce_part)[None], lax.optimization_barrier(jnp.sum(norm_part * norm_part, axis=1))])

def moments(weight, gradient, first, second, decay, corr_one, corr_two):
    next_first = BETA_ONE * first + (1.0 - BETA_ONE) * gradient
    next_second = BETA_TWO * second + (1.0 - BETA_TWO) * gradient * gradient
    update = next_first / corr_one / (jnp.sqrt(next_second / corr_two) + ADAM_EPS) + decay * weight
    return (next_first, next_second, update)

def reference(inputs, segments, token_marks, cotangent, heads_weight, merge_weight, expand_weight, reduce_weight, norm_params, first_heads, first_merge, first_expand, first_reduce, first_norm, second_heads, second_merge, second_expand, second_reduce, second_norm, step_count):
    start_rows = inputs.astype(jnp.float32)

    def wrapped(rows_value, heads, merge, expand, reduce_w, norms):
        return forward(rows_value, heads, merge, expand, reduce_w, norms, segments)
    result, pullback = jax.vjp(wrapped, start_rows, heads_weight, merge_weight, expand_weight, reduce_weight, norm_params)
    seed_grad = cotangent.astype(jnp.float32) * token_marks.astype(jnp.float32)[..., None]
    input_grad, grad_heads, grad_merge, grad_expand, grad_reduce, grad_norm = pullback(seed_grad)
    steps_float = step_count.astype(jnp.float32)
    corr_one = 1.0 - BETA_ONE ** steps_float
    corr_two = 1.0 - BETA_TWO ** steps_float
    first_h, second_h, update_h = moments(heads_weight, grad_heads, first_heads, second_heads, DECAY, corr_one, corr_two)
    first_m, second_m, update_m = moments(merge_weight, grad_merge, first_merge, second_merge, DECAY, corr_one, corr_two)
    first_e, second_e, update_e = moments(expand_weight, grad_expand, first_expand, second_expand, DECAY, corr_one, corr_two)
    first_r, second_r, update_r = moments(reduce_weight, grad_reduce, first_reduce, second_reduce, DECAY, corr_one, corr_two)
    first_n, second_n, update_n = moments(norm_params, grad_norm, first_norm, second_norm, 0.0, corr_one, corr_two)
    weight_total = squares(heads_weight, merge_weight, expand_weight, reduce_weight, norm_params)
    update_total = squares(update_h, update_m, update_e, update_r, update_n)
    trust_ratios = jnp.sqrt(weight_total) / jnp.sqrt(update_total + 1e-12)
    next_heads = heads_weight - RATE * trust_ratios[0:3, None, None] * update_h
    next_merge = merge_weight - RATE * trust_ratios[3] * update_m
    next_expand = expand_weight - RATE * trust_ratios[4] * update_e
    next_reduce = reduce_weight - RATE * trust_ratios[5] * update_r
    next_norm = norm_params - RATE * trust_ratios[6:10, None] * update_n
    return (result.astype(jnp.bfloat16), input_grad, grad_heads, grad_merge, grad_expand, grad_reduce, grad_norm, first_h, first_m, first_e, first_r, first_n, second_h, second_m, second_e, second_r, second_n, next_heads, next_merge, next_expand, next_reduce, next_norm, trust_ratios)
```

```python
import functools

import jax
import jax.numpy as jnp
from jax import lax
from jax.experimental import pallas as pl
from jax.experimental.pallas import tpu as pltpu
from jax.sharding import PartitionSpec as P

D = 768
HEAD = 64
SEQ = 1024
FF = 3072
HALF = D // 2
FF_HALF = FF // 2
MARKED = 80
BLOCKS = 16
ROWS_OF = D // BLOCKS
NORM_COLS = 128
PAIRS = D // 128
MIB = 1 << 20

NORM_EPS = 1e-12
BETA_ONE = 0.9
BETA_TWO = 0.999
ADAM_EPS = 1e-06
DECAY = 0.01
RATE = 0.25
MASKED = -1000000000.0
SCALE = HEAD ** (-0.5)
GELU_A = 0.7978845608028654
GELU_B = 0.044715
ALL = ("dp", "tensor")
LOW = jnp.bfloat16
WIDE = jnp.float32


def dot(left, right):
    return jnp.dot(left, right, preferred_element_type=WIDE)


def dot_last(left, right):
    return lax.dot_general(left, right, (((1,), (1,)), ((), ())), preferred_element_type=WIDE)


def dot_first(left, right):
    return lax.dot_general(left, right, (((0,), (0,)), ((), ())), preferred_element_type=WIDE)


def layer_norm_parts(values):
    average = jnp.mean(values, axis=-1, keepdims=True)
    centered = values - average
    spread = jnp.mean(centered * centered, axis=-1, keepdims=True)
    inverse = lax.rsqrt(spread + NORM_EPS)
    return centered * inverse, inverse


def norm_back(normed, inverse, gain, grad_out):
    scaled = grad_out * gain
    return inverse * (
        scaled
        - jnp.mean(scaled, axis=-1, keepdims=True)
        - normed * jnp.mean(scaled * normed, axis=-1, keepdims=True)
    )


def gelu_tanh(values):
    return 0.5 * values * (1.0 + jnp.tanh(GELU_A * (values + GELU_B * values * values * values)))


def gelu_slope(values):
    square = values * values
    bent = jnp.tanh(GELU_A * (values + GELU_B * square * values))
    return 0.5 * (1.0 + bent) + 0.5 * values * (1.0 - bent * bent) * (
        GELU_A * (1.0 + 3.0 * GELU_B * square)
    )


def moments(weight, gradient, first, second, decay, corr_one, corr_two):
    next_first = BETA_ONE * first + (1.0 - BETA_ONE) * gradient
    next_second = BETA_TWO * second + (1.0 - BETA_TWO) * gradient * gradient
    update = next_first / corr_one / (jnp.sqrt(next_second / corr_two) + ADAM_EPS) + decay * weight
    return (next_first, next_second, update)


def squares(heads_part, merge_part, expand_part, reduce_part, norm_part):
    return jnp.concatenate(
        [
            jnp.sum(heads_part * heads_part, axis=(1, 2)),
            jnp.sum(merge_part * merge_part)[None],
            jnp.sum(expand_part * expand_part)[None],
            jnp.sum(reduce_part * reduce_part)[None],
            jnp.sum(norm_part * norm_part, axis=1),
        ]
    )


def weight_copies(info, pieces, columns, target, target_columns, sem, pick=None, both=True):
    member = info[0]
    width = columns[1] - columns[0]
    copies = []
    for half in range(2 if both else 1):
        if both:
            side = member if half == 0 else 1 - member
            start = pl.multiple_of(target_columns + side * width, 128)
        else:
            start = target_columns
        for place in range(BLOCKS):
            source = pieces[2 * half + place // 8]
            row = pl.multiple_of(info[1 + half * BLOCKS + place] * ROWS_OF, 16)
            if pick is None:
                from_ref = source.at[place % 8, :, pl.ds(columns[0], width)]
                to_ref = target.at[pl.ds(row, ROWS_OF), pl.ds(start, width)]
            else:
                from_ref = source.at[place % 8]
                to_ref = target.at[:, pl.ds(row, ROWS_OF), pl.ds(start, width)]
            copies.append(
                pltpu.make_async_copy(from_ref, to_ref, sem.at[half * BLOCKS + place])
            )
    return copies


def start_all(copies):
    for copy in copies:
        copy.start()


def wait_all(copies):
    for copy in copies:
        copy.wait()


def qkv_kernel(info, x_ref, a, b, c, d, out_ref, weight, sem):
    @pl.when(pl.program_id(0) == 0)
    def _():
        copies = weight_copies(info, (a, b, c, d), (0, HALF), weight, 0, sem, pick=True)
        start_all(copies)
        wait_all(copies)

    for kind in range(3):
        out_ref[:, kind * D : (kind + 1) * D] = dot(x_ref[...], weight[kind]).astype(LOW)


def lane_mask(rows, which):
    lanes = lax.broadcasted_iota(jnp.int32, (rows, 128), 1)
    return (lanes < HEAD) if which == 0 else (lanes >= HEAD)


def attend_kernel(q_ref, k_ref, v_ref, seg_row_ref, seg_col_ref, out_ref):
    seg_row = seg_row_ref[...]
    zero = jnp.float32(0)
    tiles = (
        (0, 0, 512, None),
        (256, 0, 1024, None),
        (512, 256, 1024, None),
        (768, 256, 1024, None),
    )
    for start, low, high, _unused in tiles:
        if start == 256:
            bias = jnp.where(seg_col_ref[256:512, :] == seg_row, zero, MASKED)
        else:
            bias = jnp.where(
                seg_row[:, low:high] == (0 if start == 0 else 1), zero, MASKED
            )
        queries = q_ref[start : start + 256, :] * jnp.asarray(SCALE, LOW)
        result = None
        for which in range(2):
            mask = lane_mask(256, which)
            own = jnp.where(mask, queries, jnp.zeros_like(queries))
            scores = dot_last(own, k_ref[low:high, :]) + bias
            top = jnp.max(scores, axis=-1, keepdims=True)
            exped = jnp.exp(scores - top)
            total = jnp.sum(exped, axis=-1, keepdims=True)
            weights = (exped * (1.0 / total)).astype(LOW)
            context = dot(weights, v_ref[low:high, :])
            result = context if which == 0 else jnp.where(mask, context, result)
        out_ref[start : start + 256, :] = result.astype(LOW)


def marked_one_kernel(
    info, sel_ref, x_ref, ctx_ref, norms, a, b, c, d,
    xm_ref, cm_ref, att_ref, y_ref, yb_ref, u_ref, h_ref,
    merge, expand, sem, sem_two,
):
    merge_copies = weight_copies(info, (a, b, c, d), (0, HALF), merge, 0, sem)
    expand_copies = weight_copies(info, (a, b, c, d), (HALF, HALF + FF_HALF), expand, 0, sem_two)
    start_all(merge_copies)
    start_all(expand_copies)
    chosen = sel_ref[...]
    x_marked = dot(chosen, x_ref[...])
    xm_ref[...] = x_marked.astype(LOW)
    c_marked = dot(chosen, ctx_ref[...]).astype(LOW)
    cm_ref[...] = c_marked
    wait_all(merge_copies)
    attended = x_marked + dot_last(c_marked, merge[...])
    att_ref[...] = attended
    normed, _unused = layer_norm_parts(attended)
    y = normed * norms[0:1, :] + norms[1:2, :]
    y_ref[...] = y
    low = y.astype(LOW)
    yb_ref[...] = low
    wait_all(expand_copies)

    @pl.loop(0, FF // 512)
    def _(step):
        columns = pl.ds(pl.multiple_of(step * 512, 512), 512)
        inner = dot(low, expand[:, columns])
        u_ref[:, columns] = inner
        h_ref[:, columns] = gelu_tanh(inner).astype(LOW)


def marked_two_kernel(
    info, sel_ref, cot_a, cot_b, norms, y_ref, h_ref, a, b, c, d,
    db_ref, dbb_ref, ng_ref, reduce_w, sem,
):
    copies = weight_copies(info, (a, b, c, d), (0, FF_HALF), reduce_w, 0, sem)
    start_all(copies)
    first = info[0] == 0
    half = SEQ // 2
    chosen = sel_ref[...]
    cot_low = jnp.where(first, cot_a[...], cot_b[...])
    cot_high = jnp.where(first, cot_b[...], cot_a[...])
    grad = dot(chosen[:, :half], cot_low) + dot(chosen[:, half:], cot_high)
    wait_all(copies)
    joined = y_ref[...] + dot_last(h_ref[...], reduce_w[...])
    normed, inverse = layer_norm_parts(joined)
    back = norm_back(normed, inverse, norms[2:3, :], grad)
    db_ref[...] = back
    dbb_ref[...] = back.astype(LOW)
    ng_ref[0:1, :] = jnp.sum(grad * normed, axis=0, keepdims=True)
    ng_ref[1:2, :] = jnp.sum(grad, axis=0, keepdims=True)


def marked_three_kernel(
    info, norms, db_ref, dbb_ref, u_ref, att_ref, a, b, c, d, e, f, g, h,
    da_ref, dab_ref, dc_ref, ng_ref, merge, expand, reduce_w, du, sem, sem_two, sem_three,
):
    reduce_copies = weight_copies(info, (e, f, g, h), (0, FF_HALF), reduce_w, 0, sem_three)
    expand_copies = weight_copies(info, (a, b, c, d), (HALF, HALF + FF_HALF), expand, 0, sem_two)
    merge_copies = weight_copies(info, (a, b, c, d), (0, HALF), merge, 0, sem)
    start_all(reduce_copies)
    start_all(expand_copies)
    start_all(merge_copies)
    low = dbb_ref[...]
    wait_all(reduce_copies)

    @pl.loop(0, FF // 512)
    def _(step):
        columns = pl.ds(pl.multiple_of(step * 512, 512), 512)
        du[:, columns] = (
            dot(low, reduce_w[:, columns]) * gelu_slope(u_ref[:, columns])
        ).astype(LOW)

    wait_all(expand_copies)
    grad_y = db_ref[...] + dot_last(du[...], expand[...])
    normed, inverse = layer_norm_parts(att_ref[...])
    grad_a = norm_back(normed, inverse, norms[0:1, :], grad_y)
    da_ref[...] = grad_a
    grad_low = grad_a.astype(LOW)
    dab_ref[...] = grad_low
    ng_ref[0:1, :] = jnp.sum(grad_y * normed, axis=0, keepdims=True)
    ng_ref[1:2, :] = jnp.sum(grad_y, axis=0, keepdims=True)
    wait_all(merge_copies)
    dc_ref[...] = dot(grad_low, merge[...]).astype(LOW)


def attend_back_kernel(
    sel_ref, q_ref, k_ref, v_ref, dc_ref, seg_row_ref, seg_mark_ref, dq_ref, dk_ref, dv_ref
):
    queries = dot(sel_ref[...], q_ref[...]).astype(LOW)
    keys, values, grads = k_ref[...], v_ref[...], dc_ref[...]
    same = seg_mark_ref[...] == seg_row_ref[...]
    none = jnp.zeros_like(queries)
    query_list, grad_list, weight_list, score_list, dq = [], [], [], [], None
    for which in range(2):
        mask = lane_mask(MARKED, which)
        own = jnp.where(mask, queries, none)
        own_grad = jnp.where(mask, grads, none)
        scores = dot_last(own * jnp.asarray(SCALE, LOW), keys)
        scores = jnp.where(same, scores, MASKED)
        top = jnp.max(scores, axis=-1, keepdims=True)
        exped = jnp.exp(scores - top)
        probs = exped * (1.0 / jnp.sum(exped, axis=-1, keepdims=True))
        grad_probs = dot_last(own_grad, values)
        delta = jnp.sum(probs * grad_probs, axis=-1, keepdims=True)
        grad_scores = (probs * (grad_probs - delta)).astype(LOW)
        part = dot(grad_scores, keys) * SCALE
        dq = part if which == 0 else jnp.where(mask, part, dq)
        query_list.append(own)
        grad_list.append(own_grad)
        weight_list.append(probs.astype(LOW))
        score_list.append(grad_scores)
    dq_ref[...] = dq.astype(LOW)
    dk_ref[...] = (
        dot_first(jnp.concatenate(score_list, 0), jnp.concatenate(query_list, 0)) * SCALE
    ).astype(LOW)
    dv_ref[...] = dot_first(
        jnp.concatenate(weight_list, 0), jnp.concatenate(grad_list, 0)
    ).astype(LOW)


def heads_grad_kernel(
    info, x_ref, dk_ref, dv_ref, xm_ref, dq_ref, cm_ref, dab_ref,
    keep_ref, send_ref, par_ref, total, sem,
):
    step = pl.program_id(0)
    half = lax.rem(step, 2)

    def put(kind, value):
        total[half, :, pl.ds(kind * HALF, HALF)] = value.astype(LOW)

    @pl.when(step < 2)
    def _():
        put(0, dot_first(xm_ref[...], dq_ref[...]))

    @pl.when((step >= 2) & (step < 4))
    def _():
        put(1, dot_first(x_ref[...], dk_ref[...]))

    @pl.when((step >= 4) & (step < 6))
    def _():
        put(2, dot_first(x_ref[...], dv_ref[...]))

    @pl.when(step >= 6)
    def _():
        put(3, dot_first(dab_ref[...], cm_ref[...]))

    @pl.when(step == 7)
    def _():
        member = info[0]
        copies = []
        for place in range(2 * BLOCKS):
            row = pl.multiple_of(info[1 + place] * ROWS_OF, 16)
            if place < BLOCKS:
                side, target = member, (keep_ref if place < 8 else send_ref).at[place % 8]
            else:
                side, target = 1 - member, par_ref.at[place - BLOCKS]
            copies.append(
                pltpu.make_async_copy(
                    total.at[side, pl.ds(row, ROWS_OF), :], target, sem.at[place]
                )
            )
        start_all(copies)
        wait_all(copies)


def ffn_grad_kernel(
    info, yb_ref, db_ref, ybc_ref, dbc_ref, a, b, c, d,
    out_ref, expand, reduce_w, hid, du, block, sem, sem_two,
):
    expand_copies = weight_copies(
        info, (a, b), (HALF, HALF + FF_HALF), expand, 0, sem, both=False
    )
    reduce_copies = weight_copies(info, (c, d), (0, FF_HALF), reduce_w, 0, sem_two, both=False)
    start_all(expand_copies)
    start_all(reduce_copies)
    wait_all(expand_copies)
    wait_all(reduce_copies)
    tokens = yb_ref.shape[0]

    @pl.loop(0, FF_HALF // 256)
    def _(step):
        columns = pl.ds(pl.multiple_of(step * 256, 256), 256)
        later = pl.ds(pl.multiple_of(FF_HALF + step * 256, 256), 256)
        inner = dot(yb_ref[...], expand[:, columns])
        hid[...] = gelu_tanh(inner).astype(LOW)
        du[...] = (dot(db_ref[...], reduce_w[:, columns]) * gelu_slope(inner)).astype(LOW)
        block[:, columns] = dot_first(ybc_ref[...], du[...]).astype(LOW)
        block[:, later] = dot_first(dbc_ref[...], hid[...]).astype(LOW)

    for place in range(4):
        row = pl.multiple_of(lax.rem(info[1 + 4 * place], 4) * ROWS_OF, 16)
        out_ref[place] = block[pl.ds(row, ROWS_OF), :]


def input_grad_kernel(
    info, dk_ref, dv_ref, sel_ref, da_ref, dq_ref, a, b, c, d, out_ref,
    weight, high, low, sem,
):
    @pl.when(pl.program_id(0) == 0)
    def _():
        copies = weight_copies(info, (a, b, c, d), (0, HALF), weight, 0, sem, pick=True)
        start_all(copies)
        wait_all(copies)
        extra = da_ref[...] + dot_last(dq_ref[...], weight[0])
        top = extra.astype(LOW)
        high[...] = top
        low[...] = (extra - top.astype(WIDE)).astype(LOW)

    chosen = sel_ref[...]
    out_ref[...] = (
        dot_last(dk_ref[...], weight[1])
        + dot_last(dv_ref[...], weight[2])
        + dot_first(chosen, high[...])
        + dot_first(chosen, low[...])
    )


def forward_kernel(
    info, x_ref, ctx_ref, norms, a, b, c, d, e, f, g, h, out_ref,
    merge, expand, reduce_w, sem, sem_two, sem_three,
):
    @pl.when(pl.program_id(0) == 0)
    def _():
        copies = (
            weight_copies(info, (a, b, c, d), (0, HALF), merge, 0, sem)
            + weight_copies(info, (a, b, c, d), (HALF, HALF + FF_HALF), expand, 0, sem_two)
            + weight_copies(info, (e, f, g, h), (0, FF_HALF), reduce_w, 0, sem_three)
        )
        start_all(copies)
        wait_all(copies)

    attended = x_ref[...].astype(WIDE) + dot_last(ctx_ref[...], merge[...])
    normed, _unused = layer_norm_parts(attended)
    y = normed * norms[0:1, :] + norms[1:2, :]
    low = y.astype(LOW)
    joined = y
    for step in range(FF // 768):
        columns = slice(step * 768, (step + 1) * 768)
        hidden = gelu_tanh(dot(low, expand[:, columns])).astype(LOW)
        joined = joined + dot_last(hidden, reduce_w[:, columns])
    normed_two, _unused_two = layer_norm_parts(joined)
    out_ref[...] = (normed_two * norms[2:3, :] + norms[3:4, :]).astype(LOW)


ANY = pl.BlockSpec(memory_space=pl.ANY)
SMEM = pl.BlockSpec(memory_space=pltpu.SMEM)
VMEM = pl.BlockSpec(memory_space=pltpu.VMEM)


def shape(dims, kind):
    return jax.ShapeDtypeStruct(dims, kind)


def params(mib):
    return pltpu.CompilerParams(vmem_limit_bytes=mib * MIB)


def cost(flops, moved, hard=0):
    return pl.CostEstimate(flops=int(flops), bytes_accessed=int(moved), transcendentals=int(hard))


def sems(count=2 * BLOCKS):
    return pltpu.SemaphoreType.DMA((count,))


def whole(dims):
    return pl.BlockSpec(dims, lambda *_: (0,) * len(dims))


def call_qkv(info, x, first):
    return pl.pallas_call(
        qkv_kernel,
        grid=(4,),
        in_specs=[SMEM, pl.BlockSpec((256, D), lambda i: (i, 0)), ANY, ANY, ANY, ANY],
        out_specs=pl.BlockSpec((256, 3 * D), lambda i: (i, 0)),
        out_shape=shape((SEQ, 3 * D), LOW),
        scratch_shapes=[pltpu.VMEM((3, D, D), LOW), sems()],
        compiler_params=params(32),
        cost_estimate=cost(2 * SEQ * D * 3 * D, 10e6),
        name="project",
    )(info, x, *first)


def call_attend(qkv, seg_row, seg_col):
    def at(base):
        return pl.BlockSpec((SEQ, 128), lambda i, base=base: (0, base + i))

    return pl.pallas_call(
        attend_kernel,
        grid=(PAIRS,),
        in_specs=[at(0), at(PAIRS), at(2 * PAIRS), whole((1, SEQ)), whole((SEQ, 1))],
        out_specs=at(0),
        out_shape=shape((SEQ, D), LOW),
        compiler_params=params(32),
        cost_estimate=cost(3 * SEQ * SEQ * 128 * 12, 6e6, 9e6),
        name="attend",
    )(qkv, qkv, qkv, seg_row, seg_col)


def call_marked_one(info, sel, x, context, norms, second):
    return pl.pallas_call(
        marked_one_kernel,
        in_specs=[SMEM, VMEM, VMEM, VMEM, VMEM, ANY, ANY, ANY, ANY],
        out_specs=[VMEM] * 7,
        out_shape=[
            shape((MARKED, D), LOW),
            shape((MARKED, D), LOW),
            shape((MARKED, D), WIDE),
            shape((MARKED, D), WIDE),
            shape((MARKED, D), LOW),
            shape((MARKED, FF), WIDE),
            shape((MARKED, FF), LOW),
        ],
        scratch_shapes=[pltpu.VMEM((D, D), LOW), pltpu.VMEM((D, FF), LOW), sems(), sems()],
        compiler_params=params(32),
        cost_estimate=cost(1.5e9, 12e6),
        name="marked_one",
    )(info, sel, x, context, norms, *second)


def call_marked_two(info, sel, cot_own, cot_other, norms, y, hidden, third):
    return pl.pallas_call(
        marked_two_kernel,
        in_specs=[SMEM, VMEM, VMEM, VMEM, VMEM, VMEM, VMEM, ANY, ANY, ANY, ANY],
        out_specs=[VMEM] * 3,
        out_shape=[
            shape((MARKED, D), WIDE),
            shape((MARKED, D), LOW),
            shape((2, D), WIDE),
        ],
        scratch_shapes=[pltpu.VMEM((D, FF), LOW), sems()],
        compiler_params=params(32),
        cost_estimate=cost(1e9, 8e6),
        name="marked_two",
    )(info, sel, cot_own, cot_other, norms, y, hidden, *third)


def call_marked_three(info, norms, grad_b, grad_b_low, inner, attended, second, third):
    return pl.pallas_call(
        marked_three_kernel,
        in_specs=[SMEM] + [VMEM] * 5 + [ANY] * 8,
        out_specs=[VMEM] * 4,
        out_shape=[
            shape((MARKED, D), WIDE),
            shape((MARKED, D), LOW),
            shape((MARKED, D), LOW),
            shape((2, D), WIDE),
        ],
        scratch_shapes=[
            pltpu.VMEM((D, D), LOW),
            pltpu.VMEM((D, FF), LOW),
            pltpu.VMEM((D, FF), LOW),
            pltpu.VMEM((MARKED, FF), LOW),
            sems(),
            sems(),
            sems(),
        ],
        compiler_params=params(32),
        cost_estimate=cost(1.5e9, 12e6),
        name="marked_three",
    )(info, norms, grad_b, grad_b_low, inner, attended, *second, *third)


def call_attend_back(sel, qkv, grad_context, seg_row, seg_mark):
    def at(base):
        return pl.BlockSpec((SEQ, 128), lambda i, base=base: (0, base + i))

    small = pl.BlockSpec((MARKED, 128), lambda i: (0, i))
    return pl.pallas_call(
        attend_back_kernel,
        grid=(PAIRS,),
        in_specs=[
            whole((MARKED, SEQ)),
            at(0),
            at(PAIRS),
            at(2 * PAIRS),
            small,
            whole((1, SEQ)),
            whole((MARKED, 1)),
        ],
        out_specs=[small, at(0), at(0)],
        out_shape=[shape((MARKED, D), LOW), shape((SEQ, D), LOW), shape((SEQ, D), LOW)],
        compiler_params=params(32),
        cost_estimate=cost(12 * 12 * MARKED * SEQ * 128, 8e6, 1e6),
        name="attend_back",
    )(sel, qkv, qkv, qkv, grad_context, seg_row, seg_mark)


def call_heads_grad(info, x, grad_k, grad_v, x_marked, grad_q, c_marked, grad_a_low):
    def part(rows):
        return pl.BlockSpec((rows, HALF), lambda i: (0, lax.rem(i, 2)))

    return pl.pallas_call(
        heads_grad_kernel,
        grid=(8,),
        in_specs=[
            SMEM,
            whole((SEQ, D)),
            part(SEQ),
            part(SEQ),
            whole((MARKED, D)),
            part(MARKED),
            part(MARKED),
            whole((MARKED, D)),
        ],
        out_specs=[ANY] * 3,
        out_shape=[
            shape((8, ROWS_OF, 4 * HALF), LOW),
            shape((8, ROWS_OF, 4 * HALF), LOW),
            shape((BLOCKS, ROWS_OF, 4 * HALF), LOW),
        ],
        scratch_shapes=[pltpu.VMEM((2, D, 4 * HALF), LOW), sems()],
        compiler_params=params(40),
        cost_estimate=cost(2 * SEQ * D * 2 * D, 12e6),
        name="heads_grad",
    )(info, x, grad_k, grad_v, x_marked, grad_q, c_marked, grad_a_low)


def call_ffn_grad(info, yb, db, yb_part, db_part, second, third):
    tokens = yb.shape[0]
    return pl.pallas_call(
        ffn_grad_kernel,
        in_specs=[SMEM] + [VMEM] * 4 + [ANY] * 4,
        out_specs=VMEM,
        out_shape=shape((4, ROWS_OF, FF), LOW),
        scratch_shapes=[
            pltpu.VMEM((D, FF_HALF), LOW),
            pltpu.VMEM((D, FF_HALF), LOW),
            pltpu.VMEM((tokens, 256), LOW),
            pltpu.VMEM((tokens, 256), LOW),
            pltpu.VMEM((4 * ROWS_OF, FF), LOW),
            sems(BLOCKS),
            sems(BLOCKS),
        ],
        compiler_params=params(32),
        cost_estimate=cost(5e9, 10e6),
        name="ffn_grad",
    )(info, yb, db, yb_part, db_part, second[0], second[1], third[0], third[1])


def call_input_grad(info, grad_k, grad_v, sel, grad_a, grad_q, first):
    tile = pl.BlockSpec((256, D), lambda i: (i, 0))
    return pl.pallas_call(
        input_grad_kernel,
        grid=(4,),
        in_specs=[
            SMEM,
            tile,
            tile,
            pl.BlockSpec((MARKED, 256), lambda i: (0, i)),
            whole((MARKED, D)),
            whole((MARKED, D)),
            ANY,
            ANY,
            ANY,
            ANY,
        ],
        out_specs=tile,
        out_shape=shape((SEQ, D), WIDE),
        scratch_shapes=[
            pltpu.VMEM((3, D, D), LOW),
            pltpu.VMEM((MARKED, D), LOW),
            pltpu.VMEM((MARKED, D), LOW),
            sems(),
        ],
        compiler_params=params(32),
        cost_estimate=cost(2 * SEQ * D * 2 * D, 10e6),
        name="input_grad",
    )(info, grad_k, grad_v, sel, grad_a, grad_q, *first)


def call_forward(info, x, context, norms, second, third):
    tile = pl.BlockSpec((256, D), lambda i: (i, 0))
    return pl.pallas_call(
        forward_kernel,
        grid=(4,),
        in_specs=[SMEM, tile, tile, whole((4, D))] + [ANY] * 8,
        out_specs=tile,
        out_shape=shape((SEQ, D), LOW),
        scratch_shapes=[
            pltpu.VMEM((D, D), LOW),
            pltpu.VMEM((D, FF), LOW),
            pltpu.VMEM((D, FF), LOW),
            sems(),
            sems(),
            sems(),
        ],
        compiler_params=params(48),
        cost_estimate=cost(2 * SEQ * D * (D + 2 * FF), 14e6),
        name="forward_rest",
    )(info, x, context, norms, *second, *third)


class Grid:
    def __init__(self, depth, rows, columns):
        self.depth, self.rows, self.columns = depth, rows, columns
        self.chips = depth * rows * columns

    def chip(self, z, y, x):
        return (z * self.rows + y) * self.columns + x

    def perm(self, where):
        pairs = []
        for z in range(self.depth):
            for y in range(self.rows):
                for x in range(self.columns):
                    for t in range(2):
                        z2, y2, x2, t2 = where(z, y, x, t)
                        pairs.append(
                            (self.chip(z, y, x) * 2 + t, self.chip(z2, y2, x2) * 2 + t2)
                        )
        return pairs

    def send(self, value, where):
        return lax.ppermute(value, ALL, self.perm(where))

    def along_z(self, value, step):
        return self.send(value, lambda z, y, x, t: (z ^ step, y, x, t))

    def inner(self, value):
        return self.send(value, lambda z, y, x, t: (z, y ^ (1 - t), x ^ t, t))

    def outer(self, value):
        return self.send(value, lambda z, y, x, t: (z, y ^ t, x ^ (1 - t), t))

    def gather_z(self, value):
        return jnp.concatenate([value] + [self.along_z(value, s) for s in range(1, self.depth)], 0)

    def gather(self, value):
        column = self.gather_z(value)
        eight = jnp.concatenate([column, self.inner(column)], 0)
        return eight, self.outer(eight)


def other_core(value):
    return lax.ppermute(value, "tensor", [(0, 1), (1, 0)])


def shards(
    fast,
    inputs,
    segments,
    token_marks,
    cotangent,
    heads_weight,
    merge_weight,
    expand_weight,
    reduce_weight,
    norm_params,
    first_heads,
    first_merge,
    first_expand,
    first_reduce,
    first_norm,
    second_heads,
    second_merge,
    second_expand,
    second_reduce,
    second_norm,
    step_count,
):
    member = lax.axis_index("tensor")
    here = lax.axis_index("dp")
    grid = Grid(4, 2, 2)
    half_seq = SEQ // 2
    shard_rows = heads_weight.shape[1]
    norm_width = norm_params.shape[1]

    if fast:
        z, y, x = here // 4, (here // 2) % 2, here % 2

        def places(core):
            place = jnp.arange(BLOCKS, dtype=jnp.int32)
            far, near, deep = place // 8, (place // 4) % 2, place % 4
            y_place = jnp.where(core == 0, near, far)
            x_place = jnp.where(core == 0, far, near)
            return (z ^ deep) * 4 + (y ^ y_place) * 2 + (x ^ x_place)

        info = jnp.concatenate([member[None], places(member), places(1 - member)])
    else:
        order = jnp.arange(BLOCKS, dtype=jnp.int32)
        info = jnp.concatenate([member[None], order, order])
    info = info.astype(jnp.int32)

    first_part = heads_weight.astype(LOW)
    merge_turned = merge_weight.astype(LOW).T
    second_list = [merge_turned, expand_weight.astype(LOW)]
    if fast:
        top = norm_params.astype(LOW)
        rest = norm_params - top.astype(WIDE)
        middle = rest.astype(LOW)
        last = (rest - middle.astype(WIDE)).astype(LOW)
        packed = jnp.concatenate([top, middle, last], 0)
        second_list.append(
            jnp.pad(packed, ((0, ROWS_OF - 12), (0, NORM_COLS - norm_width)))
        )
    second_part = jnp.concatenate(second_list, 1)
    third_part = reduce_weight.astype(LOW).T

    if fast:

        def pieces(part):
            eight, rest_eight = grid.gather(part[None])
            return eight, rest_eight, other_core(eight), other_core(rest_eight)

    else:

        def pieces(part):
            full = lax.all_gather(part, "dp", axis=part.ndim - 2, tiled=True)
            if part.ndim == 3:
                blocks = full.reshape(3, BLOCKS, ROWS_OF, HALF).transpose(1, 0, 2, 3)
            else:
                blocks = full.reshape(BLOCKS, ROWS_OF, part.shape[1])
            eight, rest_eight = blocks[:8], blocks[8:]
            return eight, rest_eight, other_core(eight), other_core(rest_eight)

    first_w = pieces(first_part)
    second_w = pieces(second_part)
    third_w = pieces(third_part)

    if fast:

        def norm_side(eight, rest_eight, table):
            both = jnp.concatenate(
                [v[:, :12, HALF + FF_HALF : HALF + FF_HALF + norm_width] for v in (eight, rest_eight)]
            ).astype(WIDE)
            summed = both[:, 0:4] + both[:, 4:8] + both[:, 8:12]
            place_of = jnp.sum(
                jnp.where(
                    table[None, :] == jnp.arange(BLOCKS)[:, None], jnp.arange(BLOCKS)[None, :], 0
                ),
                axis=1,
            )
            return summed[place_of]

        own_side = norm_side(second_w[0], second_w[1], info[1:17])
        other_side = norm_side(second_w[2], second_w[3], info[17:33])
        low_side = jnp.where(member == 0, own_side, other_side)
        high_side = jnp.where(member == 0, other_side, own_side)
        norms = jnp.stack([low_side, high_side], 1).transpose(2, 0, 1, 3).reshape(4, D)
    else:
        norms = lax.all_gather(norm_params, ALL, axis=1, tiled=True)

    x_row = lax.dynamic_index_in_dim(inputs, member, 0, keepdims=False)
    segment = lax.dynamic_index_in_dim(segments, member, 0, keepdims=False)
    marks = lax.dynamic_index_in_dim(token_marks, member, 0, keepdims=False)
    rank = jnp.cumsum(marks) - 1
    sel = (
        (rank[None, :] == jnp.arange(MARKED, dtype=jnp.int32)[:, None]) & (marks[None, :] == 1)
    ).astype(LOW)
    seg_row, seg_col = segment[None, :], segment[:, None]
    seg_mark = jnp.sum(
        jnp.where(sel > 0, segment[None, :], 0), axis=1, keepdims=True, dtype=jnp.int32
    )
    cot_own = lax.dynamic_index_in_dim(cotangent, member, 0, keepdims=False)
    cot_other = other_core(lax.dynamic_index_in_dim(cotangent, 1 - member, 0, keepdims=False))

    qkv = call_qkv(info, x_row, first_w)
    context = call_attend(qkv, seg_row, seg_col)
    x_marked, c_marked, attended, y_marked, yb, inner, hidden = call_marked_one(
        info, sel, x_row, context, norms, second_w
    )
    grad_b, dbb, norm_two = call_marked_two(
        info, sel, cot_own, cot_other, norms, y_marked, hidden, third_w
    )
    grad_a, dab, grad_context, norm_one = call_marked_three(
        info, norms, grad_b, dbb, inner, attended, second_w, third_w
    )
    grad_q, grad_k, grad_v = call_attend_back(sel, qkv, grad_context, seg_row, seg_mark)

    if fast:

        def shared(value):
            column = grid.gather_z(value)
            return jnp.concatenate([column, other_core(column)], 0)

        yb_all, db_all = shared(yb), shared(dbb)
        wide = D // 4
        yb_cols = lax.dynamic_slice_in_dim(yb_all, z * wide, wide, 1)
        db_cols = lax.dynamic_slice_in_dim(db_all, z * wide, wide, 1)
        four = call_ffn_grad(info, yb_all, db_all, yb_cols, db_cols, second_w, third_w)
        two = four[:2].astype(WIDE) + grid.outer(four[2:]).astype(WIDE)
        one = two[0] + grid.inner(two[1].astype(LOW)).astype(WIDE)
        part_expand, part_reduce = one[:, :FF_HALF], one[:, FF_HALF:].T
    else:
        yb_all = jnp.concatenate([yb, other_core(yb)], 0)
        db_all = jnp.concatenate([dbb, other_core(dbb)], 0)
        expand_half = jnp.concatenate(second_w[:2], 0).reshape(D, -1)[:, HALF : HALF + FF_HALF]
        reduce_half = jnp.concatenate(third_w[:2], 0).reshape(D, -1)
        inner_all = dot(yb_all, expand_half)
        back_all = (dot(db_all, reduce_half) * gelu_slope(inner_all)).astype(LOW)
        hidden_all = gelu_tanh(inner_all).astype(LOW)
        part_expand = lax.psum_scatter(
            dot_first(yb_all, back_all), "dp", scatter_dimension=0, tiled=True
        )
        part_reduce = lax.psum_scatter(
            dot_first(db_all, hidden_all), "dp", scatter_dimension=0, tiled=True
        ).T

    keep, give, other = call_heads_grad(
        info, x_row, grad_k, grad_v, x_marked, grad_q, c_marked, dab
    )
    came = other_core(other)
    if fast:
        eight = keep.astype(WIDE) + came[:8].astype(WIDE)
        eight_give = (give.astype(WIDE) + came[8:].astype(WIDE)).astype(LOW)
        eight = eight + grid.outer(eight_give).astype(WIDE)
        four_h = eight[:4] + grid.inner(eight[4:].astype(LOW)).astype(WIDE)
        low_four = four_h.astype(LOW)
        summed = four_h[0]
        for step in range(1, 4):
            summed = summed + grid.along_z(low_four[step], step).astype(WIDE)
    else:
        full = jnp.concatenate([keep, give], 0).astype(WIDE) + came.astype(WIDE)
        summed = lax.psum_scatter(
            full.reshape(D, 4 * HALF), "dp", scatter_dimension=0, tiled=True
        )
    part_heads = jnp.stack([summed[:, k * HALF : (k + 1) * HALF] for k in range(3)], 0)
    part_merge = summed[:, 3 * HALF :].T

    def halves(row):
        mine = lax.dynamic_slice_in_dim(row, member * half_seq, half_seq, 0)
        give_half = lax.dynamic_slice_in_dim(row, (1 - member) * half_seq, half_seq, 0)
        return mine, other_core(give_half.astype(LOW))

    def place_rows(mine, came_half):
        came_half = came_half.astype(mine.dtype)
        return jnp.where(
            member == 0, jnp.stack([mine, came_half]), jnp.stack([came_half, mine])
        )

    layer_output = place_rows(*halves(call_forward(info, x_row, context, norms, second_w, third_w)))
    input_grad = place_rows(
        *halves(call_input_grad(info, grad_k, grad_v, sel, grad_a, grad_q, first_w))
    )

    norm_terms = jnp.concatenate([norm_one, norm_two], 0)
    part_norm = lax.psum_scatter(norm_terms, ALL, scatter_dimension=1, tiled=True)

    steps_float = step_count.astype(WIDE)
    corr_one = 1.0 - BETA_ONE**steps_float
    corr_two = 1.0 - BETA_TWO**steps_float
    first_h, second_h, update_h = moments(
        heads_weight, part_heads, first_heads, second_heads, DECAY, corr_one, corr_two
    )
    first_m, second_m, update_m = moments(
        merge_weight, part_merge, first_merge, second_merge, DECAY, corr_one, corr_two
    )
    first_e, second_e, update_e = moments(
        expand_weight, part_expand, first_expand, second_expand, DECAY, corr_one, corr_two
    )
    first_r, second_r, update_r = moments(
        reduce_weight, part_reduce, first_reduce, second_reduce, DECAY, corr_one, corr_two
    )
    first_n, second_n, update_n = moments(
        norm_params, part_norm, first_norm, second_norm, 0.0, corr_one, corr_two
    )
    both = jnp.stack(
        [
            squares(heads_weight, merge_weight, expand_weight, reduce_weight, norm_params),
            squares(update_h, update_m, update_e, update_r, update_n),
        ]
    )
    if fast:
        both = both + other_core(both)
        both = (
            both
            + grid.send(both, lambda z, y, x, t: (z, y ^ 1, x, t))
            + grid.send(both, lambda z, y, x, t: (z, y, x ^ 1, t))
            + grid.send(both, lambda z, y, x, t: (z, y ^ 1, x ^ 1, t))
        )
        both = (both + grid.along_z(both, 1)) + (grid.along_z(both, 2) + grid.along_z(both, 3))
    else:
        both = lax.psum(both, ALL)
    trust_ratios = jnp.sqrt(both[0]) / jnp.sqrt(both[1] + 1e-12)
    next_heads = heads_weight - RATE * trust_ratios[0:3, None, None] * update_h
    next_merge = merge_weight - RATE * trust_ratios[3] * update_m
    next_expand = expand_weight - RATE * trust_ratios[4] * update_e
    next_reduce = reduce_weight - RATE * trust_ratios[5] * update_r
    next_norm = norm_params - RATE * trust_ratios[6:10, None] * update_n
    return (
        layer_output,
        input_grad,
        part_heads,
        part_merge,
        part_expand,
        part_reduce,
        part_norm,
        first_h,
        first_m,
        first_e,
        first_r,
        first_n,
        second_h,
        second_m,
        second_e,
        second_r,
        second_n,
        next_heads,
        next_merge,
        next_expand,
        next_reduce,
        next_norm,
        trust_ratios,
    )


def solution(mesh):
    fast = mesh.shape["dp"] == BLOCKS and mesh.shape["tensor"] == 2
    return jax.shard_map(
        functools.partial(shards, fast),
        mesh=mesh,
        in_specs=(
            P("dp", None, None),
            P("dp", None),
            P("dp", None),
            P("dp", "tensor", None),
            P(None, "dp", "tensor"),
            P("tensor", "dp"),
            P("dp", "tensor"),
            P("tensor", "dp"),
            P(None, ("dp", "tensor")),
            P(None, "dp", "tensor"),
            P("tensor", "dp"),
            P("dp", "tensor"),
            P("tensor", "dp"),
            P(None, ("dp", "tensor")),
            P(None, "dp", "tensor"),
            P("tensor", "dp"),
            P("dp", "tensor"),
            P("tensor", "dp"),
            P(None, ("dp", "tensor")),
            P(),
        ),
        out_specs=(
            P("dp", "tensor", None),
            P("dp", "tensor", None),
            P(None, "dp", "tensor"),
            P("tensor", "dp"),
            P("dp", "tensor"),
            P("tensor", "dp"),
            P(None, ("dp", "tensor")),
            P(None, "dp", "tensor"),
            P("tensor", "dp"),
            P("dp", "tensor"),
            P("tensor", "dp"),
            P(None, ("dp", "tensor")),
            P(None, "dp", "tensor"),
            P("tensor", "dp"),
            P("dp", "tensor"),
            P("tensor", "dp"),
            P(None, ("dp", "tensor")),
            P(None, "dp", "tensor"),
            P("tensor", "dp"),
            P("dp", "tensor"),
            P("tensor", "dp"),
            P(None, ("dp", "tensor")),
            P(),
        ),
        check_vma=False,
    )
```

```python
import functools

import jax
import jax.numpy as jnp
from jax import lax
from jax.experimental import pallas as pl
from jax.experimental.pallas import tpu as pltpu
from jax.sharding import PartitionSpec as P

D = 768
HEAD = 64
SEQ = 1024
FF = 3072
HALF = D // 2
FF_HALF = FF // 2
MARKED = 80
BLOCKS = 16
ROWS_OF = D // BLOCKS
NORM_COLS = 128
PAIRS = D // 128
MIB = 1 << 20
SCOPED = 12

NORM_EPS = 1e-12
BETA_ONE = 0.9
BETA_TWO = 0.999
ADAM_EPS = 1e-06
DECAY = 0.01
RATE = 0.25
MASKED = -1000000000.0
SCALE = HEAD ** (-0.5)
GELU_A = 0.7978845608028654
GELU_B = 0.044715
ALL = ("dp", "tensor")
LOW = jnp.bfloat16
WIDE = jnp.float32


def dot(left, right):
    return jnp.dot(left, right, preferred_element_type=WIDE)


def dot_last(left, right):
    return lax.dot_general(left, right, (((1,), (1,)), ((), ())), preferred_element_type=WIDE)


def dot_first(left, right):
    return lax.dot_general(left, right, (((0,), (0,)), ((), ())), preferred_element_type=WIDE)


def layer_norm_parts(values):
    average = jnp.mean(values, axis=-1, keepdims=True)
    centered = values - average
    spread = jnp.mean(centered * centered, axis=-1, keepdims=True)
    inverse = lax.rsqrt(spread + NORM_EPS)
    return centered * inverse, inverse


def norm_back(normed, inverse, gain, grad_out):
    scaled = grad_out * gain
    return inverse * (
        scaled
        - jnp.mean(scaled, axis=-1, keepdims=True)
        - normed * jnp.mean(scaled * normed, axis=-1, keepdims=True)
    )


def gelu_tanh(values):
    return 0.5 * values * (1.0 + jnp.tanh(GELU_A * (values + GELU_B * values * values * values)))


def gelu_slope(values):
    square = values * values
    bent = jnp.tanh(GELU_A * (values + GELU_B * square * values))
    return 0.5 * (1.0 + bent) + 0.5 * values * (1.0 - bent * bent) * (
        GELU_A * (1.0 + 3.0 * GELU_B * square)
    )


def moments(weight, gradient, first, second, decay, corr_one, corr_two):
    next_first = BETA_ONE * first + (1.0 - BETA_ONE) * gradient
    next_second = BETA_TWO * second + (1.0 - BETA_TWO) * gradient * gradient
    update = next_first / corr_one / (jnp.sqrt(next_second / corr_two) + ADAM_EPS) + decay * weight
    return (next_first, next_second, update)


def squares(heads_part, merge_part, expand_part, reduce_part, norm_part):
    return jnp.concatenate(
        [
            jnp.sum(heads_part * heads_part, axis=(1, 2)),
            jnp.sum(merge_part * merge_part)[None],
            jnp.sum(expand_part * expand_part)[None],
            jnp.sum(reduce_part * reduce_part)[None],
            jnp.sum(norm_part * norm_part, axis=1),
        ]
    )


def weight_copies(info, pieces, columns, target, sem):
    member = info[0]
    width = columns[1] - columns[0]
    copies = []
    for place in range(len(pieces) * 8):
        source = pieces[place // 8].at[place % 8, :, pl.ds(columns[0], width)]
        row = pl.multiple_of(info[1 + place] * ROWS_OF, 16)
        start = 0
        if len(pieces) == 4:
            start = pl.multiple_of((member if place < BLOCKS else 1 - member) * width, 128)
        copies.append(
            pltpu.make_async_copy(
                source, target.at[pl.ds(row, ROWS_OF), pl.ds(start, width)], sem
            )
        )
    return copies


def wait_whole(target, sem):
    pltpu.make_async_copy(target, target, sem).wait()


def start_all(copies):
    for copy in copies:
        copy.start()


def wait_all(copies):
    for copy in copies:
        copy.wait()


def qkv_kernel(info, x_ref, a, b, c, d, out_ref, weight, sem):
    member = info[0]
    for which in range(3):
        for place in range(2 * BLOCKS):
            side = member if place < BLOCKS else 1 - member
            row = pl.multiple_of(info[1 + place] * ROWS_OF, 16)
            column = pl.multiple_of(side * HALF, 128)
            pltpu.make_async_copy(
                (a, b, c, d)[place // 8].at[place % 8, which],
                weight.at[which, pl.ds(row, ROWS_OF), pl.ds(column, HALF)],
                sem.at[which],
            ).start()
    for which in range(3):
        wait_whole(weight.at[which], sem.at[which])
        out_ref[:, which * D : (which + 1) * D] = dot(x_ref[...], weight[which]).astype(LOW)


def lane_mask(rows, which):
    lanes = lax.broadcasted_iota(jnp.int32, (rows, 128), 1)
    return (lanes < HEAD) if which == 0 else (lanes >= HEAD)


def attend_kernel(start, count, qkv_ref, seg_row_ref, out_ref):
    seg_row = seg_row_ref[...]
    zero = jnp.float32(0)
    one = jnp.asarray(1, LOW)
    edge = seg_row[:, 256:512]
    diagonal = lax.broadcasted_iota(jnp.int32, (256, 256), 0) == lax.broadcasted_iota(
        jnp.int32, (256, 256), 1
    )
    edge_column = jnp.sum(jnp.where(diagonal, edge, 0), axis=1, keepdims=True)
    tiles = ((0, 256, 0, 512), (256, 256, 0, 1024), (512, 512, 256, 1024))

    @pl.loop(0, count)
    def _(pair):
        def lanes(base):
            return pl.ds(pl.multiple_of((base + start + pair) * 128, 128), 128)

        q_lanes, k_lanes, v_lanes = lanes(0), lanes(PAIRS), lanes(2 * PAIRS)
        values = qkv_ref[:, v_lanes]
        with_sum = [jnp.where(lane_mask(SEQ, which), values, one) for which in range(2)]
        for first, rows, low, high in tiles:
            if first == 256:
                bias = jnp.where(edge_column == seg_row, zero, MASKED)
            else:
                bias = jnp.where(edge == (0 if first == 0 else 1), zero, MASKED)
            queries = qkv_ref[first : first + rows, q_lanes] * jnp.asarray(SCALE, LOW)
            result = None
            for which in range(2):
                mask = lane_mask(rows, which)
                own = jnp.where(mask, queries, jnp.zeros_like(queries))
                scores = dot_last(own, qkv_ref[low:high, k_lanes])
                if first == 0:
                    scores = jnp.concatenate([scores[:, :256], scores[:, 256:] + bias], 1)
                elif first == 256:
                    scores = scores + bias
                else:
                    scores = jnp.concatenate([scores[:, :256] + bias, scores[:, 256:]], 1)
                top = jnp.max(scores, axis=-1, keepdims=True)
                weights = jnp.exp(scores - top).astype(LOW)
                context = dot(weights, with_sum[which][low:high, :])
                context = context / pltpu.roll(context, HEAD, 1)
                result = context if which == 0 else jnp.where(mask, context, result)
            out_ref[first : first + rows, pl.ds(pl.multiple_of(pair * 128, 128), 128)] = (
                result.astype(LOW)
            )


def middle_kernel(
    info, sel_ref, x_ref, ctx_a, ctx_b, ctx_c, norms_in, a, b, c, d,
    cm_ref, att_ref, ym_ref, yb_ref, u_ref, hm_ref, y_ref, h_ref, norms, merge, expand,
    packed, sem,
):
    contexts = (ctx_a, ctx_b, ctx_c)
    third = D // 3

    def first_norm(x, parts):
        attended = x
        for index, part in enumerate(parts):
            attended = attended + dot_last(part, merge[:, index * third : (index + 1) * third])
        normed, _unused = layer_norm_parts(attended)
        return attended, normed * norms[0:1, :] + norms[1:2, :]

    start_all(weight_copies(info, (a, b, c, d), (0, HALF), merge, sem.at[0]))
    if norms_in is None:
        member = info[0]
        for place in range(2 * BLOCKS):
            side = member if place < BLOCKS else 1 - member
            source = (a, b, c, d)[place // 8]
            pltpu.make_async_copy(
                source.at[place % 8, pl.ds(0, 16), pl.ds(HALF + FF_HALF, NORM_COLS)],
                packed.at[side, info[1 + place]],
                sem.at[2],
            ).start()
    start_all(weight_copies(info, (a, b, c, d), (HALF, HALF + FF_HALF), expand, sem.at[1]))
    chosen = sel_ref[...]
    x_marked = dot(chosen, x_ref[...])
    c_marked = [dot(chosen, part[...]).astype(LOW) for part in contexts]
    for index, part in enumerate(c_marked):
        cm_ref[:, index * third : (index + 1) * third] = part
    if norms_in is None:
        wait_whole(packed, sem.at[2])
        pieces = []
        for block in range(BLOCKS):
            for side in range(2):
                part = packed[side, block].astype(WIDE)
                pieces.append((part[0:4] + part[4:8] + part[8:12])[:, :24])
        norms[...] = jnp.concatenate(pieces, 1)
    else:
        norms[...] = norms_in[...]
    wait_whole(merge, sem.at[0])
    attended, y = first_norm(x_marked, c_marked)
    att_ref[...] = attended
    ym_ref[...] = y
    low = y.astype(LOW)
    yb_ref[...] = low
    wait_whole(expand, sem.at[1])

    @pl.loop(0, FF // 512)
    def _(part):
        columns = pl.ds(pl.multiple_of(part * 512, 512), 512)
        inner = dot(low, expand[:, columns])
        u_ref[:, columns] = inner
        hm_ref[:, columns] = gelu_tanh(inner).astype(LOW)

    @pl.loop(0, SEQ // 256)
    def _(tile):
        rows = pl.ds(pl.multiple_of(tile * 256, 256), 256)
        _unused, y_tile = first_norm(
            x_ref[rows, :].astype(WIDE), [part[rows, :] for part in contexts]
        )
        y_ref[rows, :] = y_tile
        low_tile = y_tile.astype(LOW)
        for part in range(FF // 768):
            columns = slice(part * 768, (part + 1) * 768)
            h_ref[rows, columns] = gelu_tanh(dot(low_tile, expand[:, columns])).astype(LOW)


def turn_kernel(info, x_ref, sel_ref, own_ref, par_ref, own_m_ref, par_m_ref):
    picks = pick_rows(info, 0, BLOCKS)
    for which, full_ref, marked_ref in (
        (info[0], own_ref, own_m_ref),
        (1 - info[0], par_ref, par_m_ref),
    ):
        full = dot_last(picks, x_ref[which]).astype(LOW)
        full_ref[...] = full
        marked_ref[...] = dot_last(full, sel_ref[which]).astype(LOW)


def pick_rows(info, first, count):
    within = lax.broadcasted_iota(jnp.int32, (ROWS_OF, D), 0)
    lanes = lax.broadcasted_iota(jnp.int32, (ROWS_OF, D), 1)
    return jnp.concatenate(
        [
            jnp.where(lanes == within + info[1 + place] * ROWS_OF, 1.0, 0.0)
            for place in range(first, first + count)
        ],
        0,
    ).astype(LOW)


def marked_back_kernel(
    info, sel_ref, cot_ref, cot_b, norms, y_ref, yb_ref, h_ref, u_ref, att_ref, merge, expand,
    e, f, g, h,
    yd_ref, da_ref, dab_ref, dc_ref, ng_ref, reduce_w, du, sem,
):
    start_all(weight_copies(info, (e, f, g, h), (0, FF_HALF), reduce_w, sem.at[0]))
    first = info[0] == 0
    half = SEQ // 2
    chosen = sel_ref[...]
    cot_own = cot_ref[info[0]]
    cot_low = jnp.where(first, cot_own, cot_b[...])
    cot_high = jnp.where(first, cot_b[...], cot_own)
    grad = dot(chosen[:, :half], cot_low) + dot(chosen[:, half:], cot_high)
    wait_whole(reduce_w, sem.at[0])
    joined = y_ref[...] + dot_last(h_ref[...], reduce_w[...])
    normed, inverse = layer_norm_parts(joined)
    back = norm_back(normed, inverse, norms[2:3, :], grad)
    low = back.astype(LOW)
    yd_ref[:MARKED] = yb_ref[...]
    yd_ref[MARKED:] = low
    ng_ref[2:3, :] = jnp.sum(grad * normed, axis=0, keepdims=True)
    ng_ref[3:4, :] = jnp.sum(grad, axis=0, keepdims=True)
    for step in range(FF // 512):
        columns = slice(step * 512, (step + 1) * 512)
        du[:, columns] = (
            dot(low, reduce_w[:, columns]) * gelu_slope(u_ref[:, columns])
        ).astype(LOW)
    grad_y = back + dot_last(du[...], expand[...])
    normed_one, inverse_one = layer_norm_parts(att_ref[...])
    grad_a = norm_back(normed_one, inverse_one, norms[0:1, :], grad_y)
    da_ref[...] = grad_a
    grad_low = grad_a.astype(LOW)
    dab_ref[...] = grad_low
    ng_ref[0:1, :] = jnp.sum(grad_y * normed_one, axis=0, keepdims=True)
    ng_ref[1:2, :] = jnp.sum(grad_y, axis=0, keepdims=True)
    dc_ref[...] = dot(grad_low, merge[...]).astype(LOW)


def half_back_kernel(
    other, info, sel_ref, qkv_ref, dc_ref, seg_row_ref, dq_ref, dk_ref, dv_ref
):
    half = 1 - info[0] if other else info[0]
    mask = lane_mask(MARKED, 0)
    seg_row = seg_row_ref[...].astype(WIDE)
    mark_segs = jnp.sum(sel_ref[...].astype(WIDE) * seg_row, axis=1, keepdims=True)
    same = jnp.concatenate([mark_segs, mark_segs], 0) == seg_row
    for pair in range(PAIRS // 2):
        first = half * (PAIRS // 2) + pair

        def lanes(base):
            return pl.ds(pl.multiple_of((base + first) * 128, 128), 128)

        out = slice(pair * 128, (pair + 1) * 128)
        queries = dot(sel_ref[...], qkv_ref[:, lanes(0)]).astype(LOW)
        keys, values = qkv_ref[:, lanes(PAIRS)], qkv_ref[:, lanes(2 * PAIRS)]
        grads = dc_ref[:, lanes(0)]
        none = jnp.zeros_like(queries)
        query_both = jnp.concatenate(
            [jnp.where(mask, queries, none), jnp.where(mask, none, queries)], 0
        )
        grad_both = jnp.concatenate(
            [jnp.where(mask, grads, none), jnp.where(mask, none, grads)], 0
        )
        scores = dot_last(query_both * jnp.asarray(SCALE, LOW), keys)
        scores = jnp.where(same, scores, MASKED)
        top = jnp.max(scores, axis=-1, keepdims=True)
        exped = jnp.exp(scores - top)
        probs = exped * (1.0 / jnp.sum(exped, axis=-1, keepdims=True))
        grad_probs = dot_last(grad_both, values)
        delta = jnp.sum(probs * grad_probs, axis=-1, keepdims=True)
        grad_scores = (probs * (grad_probs - delta)).astype(LOW)
        dq_both = dot(grad_scores, keys) * SCALE
        dq_ref[:, out] = jnp.where(mask, dq_both[:MARKED], dq_both[MARKED:]).astype(LOW)
        dk_ref[:, out] = (dot_first(grad_scores, query_both) * SCALE).astype(LOW)
        dv_ref[:, out] = dot_first(probs.astype(LOW), grad_both).astype(LOW)


def heads_grad_kernel(
    info, xt_a, xt_b, dk_a, dk_b, dv_a, dv_b, xm_a, xm_b, dq_a, dq_b,
    dab_a, dab_b, cm_a, cm_b, ng_a, ng_b, keep_ref, give_ref, small,
):
    norm_grads = ng_a[...] + ng_b[...]
    for block in range(BLOCKS):
        sides = [
            norm_grads[:, (2 * block + side) * 24 : (2 * block + side + 1) * 24]
            for side in range(2)
        ]
        part = jnp.where(info[0] == 0, sides[0], sides[1])
        part = jnp.concatenate([part, jnp.zeros((4, NORM_COLS - 24), WIDE)], 1)
        part = jnp.concatenate([part, jnp.zeros((ROWS_OF - 4, NORM_COLS), WIDE)], 0)
        small[block] = part.astype(LOW)
    tall = 8 * ROWS_OF
    own = pl.ds(pl.multiple_of(info[0] * HALF, 128), HALF)
    for half, out_ref in ((1, give_ref), (0, keep_ref)):
        rows = slice(half * tall, (half + 1) * tall)

        def put(kind, value):
            out_ref[:, :, kind * HALF : (kind + 1) * HALF] = value.astype(LOW).reshape(
                8, ROWS_OF, HALF
            )

        put(1, dot(xt_a[rows, :], dk_a[...]) + dot(xt_b[rows, :], dk_b[...]))
        put(2, dot(xt_a[rows, :], dv_a[...]) + dot(xt_b[rows, :], dv_b[...]))
        put(0, dot(xm_a[rows, :], dq_a[...]) + dot(xm_b[rows, :], dq_b[...]))
        picks = pick_rows(info, 8 * half, 8)
        put(
            3,
            dot(dot_last(picks, dab_a[...]).astype(LOW), cm_a[:, own])
            + dot(dot_last(picks, dab_b[...]).astype(LOW), cm_b[:, own]),
        )
        for place in range(8):
            out_ref[place, :, 4 * HALF :] = small[info[1 + 8 * half + place]]


def ffn_grad_kernel(
    info, p0, p1, p2, p3, p4, p5, p6, p7, expand, reduce_w,
    keep_ref, give_ref, block, yb, db, yb_turned, db_turned, sem,
):
    loads = []
    for index, source in enumerate((p0, p1, p2, p3, p4, p5, p6, p7)):
        for which, target in enumerate((yb, db)):
            loads.append(
                pltpu.make_async_copy(
                    source.at[0, pl.ds(which * MARKED, MARKED)],
                    target.at[pl.ds(index * MARKED, MARKED)],
                    sem.at[which],
                )
            )
    start_all(loads)
    wide = 4 * ROWS_OF
    start = info[2 * BLOCKS + 1] * wide
    picks = jnp.where(
        lax.broadcasted_iota(jnp.int32, (wide, D), 1)
        == lax.broadcasted_iota(jnp.int32, (wide, D), 0) + start,
        1.0,
        0.0,
    ).astype(LOW)
    wait_whole(yb, sem.at[0])
    wait_whole(db, sem.at[1])
    yb_turned[...] = dot_last(picks, yb[...]).astype(LOW)
    db_turned[...] = dot_last(picks, db[...]).astype(LOW)

    @pl.loop(0, FF_HALF // 256)
    def _(step):
        columns = pl.ds(pl.multiple_of(step * 256, 256), 256)
        later = pl.ds(pl.multiple_of(FF_HALF + step * 256, 256), 256)
        own = pl.ds(pl.multiple_of(info[0] * FF_HALF + step * 256, 256), 256)
        inner = dot(yb[...], expand[:, own])
        hidden = gelu_tanh(inner).astype(LOW)
        back = (dot(db[...], reduce_w[:, own]) * gelu_slope(inner)).astype(LOW)
        block[:, columns] = dot(yb_turned[...], back).astype(LOW)
        block[:, later] = dot(db_turned[...], hidden).astype(LOW)

    for place in range(4):
        row = pl.multiple_of(lax.rem(info[1 + 4 * place], 4) * ROWS_OF, 16)
        (keep_ref, give_ref)[place // 2][place % 2] = block[pl.ds(row, ROWS_OF), :]


def input_grad_kernel(
    info, dk_own, dk_par, dv_own, dv_par, sel_ref, da_ref, dq_own, dq_par, weight,
    give_ref, keep_ref,
):
    member = info[0]

    def ordered(own, par):
        first = member == 0
        return jnp.concatenate([jnp.where(first, own, par), jnp.where(first, par, own)], 1)

    extra = da_ref[...] + dot_last(ordered(dq_own[...], dq_par[...]), weight[0])
    high = extra.astype(LOW)
    low = (extra - high.astype(WIDE)).astype(LOW)
    for tile in range(4):
        rows = token_rows(member, tile)
        chosen = sel_ref[:, rows]
        hand_out(
            dot_last(ordered(dk_own[rows, :], dk_par[rows, :]), weight[1])
            + dot_last(ordered(dv_own[rows, :], dv_par[rows, :]), weight[2])
            + dot_first(chosen, high)
            + dot_first(chosen, low),
            tile,
            give_ref,
            keep_ref,
        )


def token_rows(member, tile):
    half = 1 - member if tile < 2 else member
    return pl.ds(pl.multiple_of(half * 512 + (tile % 2) * 256, 256), 256)


def forward_two_kernel(info, y_ref, h_ref, norms, reduce_w, give_ref, keep_ref):
    for tile in range(4):
        rows = token_rows(info[0], tile)
        joined = y_ref[rows, :] + dot_last(h_ref[rows, :], reduce_w[...])
        normed, _unused = layer_norm_parts(joined)
        hand_out(normed * norms[2:3, :] + norms[3:4, :], tile, give_ref, keep_ref)


def hand_out(result, tile, give_ref, keep_ref):
    rows = slice((tile % 2) * 256, (tile % 2 + 1) * 256)
    out_ref = give_ref if tile < 2 else keep_ref
    out_ref[rows, :] = result.astype(out_ref.dtype)


def place_kernel(info, keep_ref, came_ref, out_ref):
    out_ref[info[0]] = keep_ref[...]
    out_ref[1 - info[0]] = came_ref[...].astype(out_ref.dtype)


def join_kernel(count, *refs):
    parts, out_ref, sem = refs[:count], refs[-2], refs[-1]
    copies, start = [], 0
    for index, part in enumerate(parts):
        size = part.shape[0]
        copies.append(
            pltpu.make_async_copy(part, out_ref.at[pl.ds(start, size)], sem.at[index])
        )
        start += size
    start_all(copies)
    wait_all(copies)


def fold_kernel(keep, a_ref, b_ref, *outs):
    outs[0][...] = (a_ref[:keep].astype(WIDE) + b_ref[:keep].astype(WIDE)).astype(outs[0].dtype)
    sent = outs[1:]
    size = (a_ref.shape[0] - keep) // len(sent)
    for index, out in enumerate(sent):
        rows = slice(keep + index * size, keep + (index + 1) * size)
        out[...] = (a_ref[rows].astype(WIDE) + b_ref[rows].astype(WIDE)).astype(LOW)


def lamb_step(corr, refs, gradient, decay):
    weight_ref, first_ref, second_ref, grad_ref, next_first_ref, next_second_ref, u_ref = refs
    weight = weight_ref[...]
    grad_ref[...] = gradient
    first, second, update = moments(
        weight, gradient, first_ref[...], second_ref[...], decay, corr[0], corr[1]
    )
    next_first_ref[...] = first
    next_second_ref[...] = second
    u_ref[...] = update
    return weight * weight, update * update


def put_sums(sums_ref, entries):
    lanes = lax.broadcasted_iota(jnp.int32, (8, 128), 1)
    rows = lax.broadcasted_iota(jnp.int32, (8, 128), 0)
    total = jnp.zeros((8, 128), WIDE)
    for lane, (weight_square, update_square) in entries:
        for row, value in enumerate((weight_square, update_square)):
            total = total + jnp.where((lanes == lane) & (rows == row), jnp.sum(value), 0.0)
    sums_ref[...] = total


def lamb_ffn_kernel(corr, keep_ref, came_ref, *refs):
    expand, reduce_refs, sums_ref = refs[0:3] + refs[6:10], refs[3:6] + refs[10:14], refs[14]
    summed = keep_ref[0].astype(WIDE) + came_ref[0].astype(WIDE)
    put_sums(
        sums_ref,
        [
            (4, lamb_step(corr, expand, summed[:, :FF_HALF], DECAY)),
            (5, lamb_step(corr, reduce_refs, summed[:, FF_HALF:], DECAY)),
        ],
    )


def lamb_rest_kernel(corr, keep_ref, came_a, came_b, came_c, other_sums, *refs):
    heads, merge, norm = refs[0:3] + refs[9:13], refs[3:6] + refs[13:17], refs[6:9] + refs[17:21]
    sums_ref = refs[21]
    summed = (
        keep_ref[0].astype(WIDE)
        + came_a[0].astype(WIDE)
        + came_b[0].astype(WIDE)
        + came_c[0].astype(WIDE)
    )
    norm_width = norm[0].shape[1]
    heads_grad = jnp.stack([summed[:, k * HALF : (k + 1) * HALF] for k in range(3)], 0)
    squares_w, squares_u = lamb_step(corr, heads, heads_grad, DECAY)
    entries = [(k, (squares_w[k], squares_u[k])) for k in range(3)]
    merge_grad = summed[:, 3 * HALF : 4 * HALF]
    entries.append((3, lamb_step(corr, merge, merge_grad, DECAY)))
    norm_grad = summed[:4, 4 * HALF : 4 * HALF + norm_width]
    squares_w, squares_u = lamb_step(corr, norm, norm_grad, 0.0)
    entries += [(6 + k, (squares_w[k : k + 1], squares_u[k : k + 1])) for k in range(4)]
    put_sums(sums_ref, entries)
    sums_ref[...] += other_sums[...]


def lamb_end_kernel(sums_ref, *refs):
    sums = sums_ref[...]
    ratios = jnp.sqrt(sums[0:1, :]) / jnp.sqrt(sums[1:2, :] + 1e-12)
    refs[15][...] = ratios
    weights, updates, outs = refs[0:5], refs[5:10], refs[10:15]

    def moved(index, part, ratio):
        return weights[index][part] - RATE * ratio * updates[index][part]

    for k in range(3):
        outs[0][k] = moved(0, k, ratios[:, k : k + 1])
    for index in range(1, 4):
        outs[index][...] = moved(index, Ellipsis, ratios[:, 2 + index : 3 + index])
    for k in range(4):
        outs[4][k : k + 1] = moved(4, slice(k, k + 1), ratios[:, 6 + k : 7 + k])


ANY = pl.BlockSpec(memory_space=pl.ANY)
SMEM = pl.BlockSpec(memory_space=pltpu.SMEM)
VMEM = pl.BlockSpec(memory_space=pltpu.VMEM)


def shape(dims, kind):
    return jax.ShapeDtypeStruct(dims, kind)


def params(mib):
    return pltpu.CompilerParams(vmem_limit_bytes=mib * MIB)


def cost(flops, moved, hard=0):
    return pl.CostEstimate(
        flops=int(flops) // 50, bytes_accessed=int(moved) // 50, transcendentals=int(hard) // 50
    )


def sems(count=2 * BLOCKS):
    return pltpu.SemaphoreType.DMA((count,))


def whole(dims):
    return pl.BlockSpec(dims, lambda *_: (0,) * len(dims))


def near(dims, kind):
    return pltpu.VMEM(dims, kind)


def held(*arrays):
    return [pltpu.with_memory_space_constraint(array, pltpu.VMEM) for array in arrays]


def call(kernel, name, ins, specs, out_shape, out_specs, deps=(), **options):
    count, extra = len(ins), len(deps)

    def body(*refs):
        kernel(*refs[:count], *refs[count + extra :])

    return pl.pallas_call(
        body,
        in_specs=list(specs) + [ANY] * extra,
        out_specs=out_specs,
        out_shape=out_shape,
        name=name,
        **options,
    )(*ins, *deps)


def call_join(parts, deps=()):
    count = len(parts)
    rows = sum(part.shape[0] for part in parts)
    size = rows * parts[0][0].size * 2
    return call(
        functools.partial(join_kernel, count),
        "join",
        parts,
        [ANY] * count,
        shape((rows,) + parts[0].shape[1:], parts[0].dtype),
        VMEM,
        deps,
        scratch_shapes=[sems(count)],
        compiler_params=params(SCOPED),
        cost_estimate=cost(0, 2 * size),
    )


def call_fold(keep, left, right, sends=1, deps=()):
    block = left.shape[1:]
    size = (left.shape[0] - keep) // sends
    return call(
        functools.partial(fold_kernel, keep),
        "fold",
        [left, right],
        [VMEM] * 2,
        [shape((keep,) + block, LOW)] + [shape((size,) + block, LOW)] * sends,
        [VMEM] * (1 + sends),
        deps,
        compiler_params=params(SCOPED),
        cost_estimate=cost(left.size, 4 * left.size),
    )


def call_qkv(info, x, first, deps=()):
    return call(
        qkv_kernel,
        "project",
        [info, x, *first],
        [SMEM, VMEM, ANY, ANY, ANY, ANY],
        [near((SEQ, 3 * D), LOW), near((3, D, D), LOW)],
        [VMEM] * 2,
        deps,
        scratch_shapes=[sems(3)],
        compiler_params=params(SCOPED),
        cost_estimate=cost(2 * SEQ * D * 3 * D, 10e6),
    )


def call_attend(qkv, seg_row, start, count, deps=()):
    return call(
        functools.partial(attend_kernel, start, count),
        "attend",
        [*held(qkv), seg_row],
        [VMEM] * 2,
        near((SEQ, 128 * count), LOW),
        VMEM,
        deps,
        compiler_params=params(SCOPED),
        cost_estimate=cost(3 * SEQ * SEQ * 128 * 2 * count, 1e6 * count, 1.5e6 * count),
    )


def call_middle(info, sel, x, contexts, norms, second, deps=()):
    ins = [info, sel, x, *held(*contexts)]
    specs = [SMEM] + [VMEM] * 5
    if norms is None:

        def kernel(*refs):
            middle_kernel(*refs[:6], None, *refs[6:])

    else:
        kernel = middle_kernel
        ins.append(norms)
        specs.append(VMEM)
    return call(
        kernel,
        "middle",
        ins + list(second),
        specs + [ANY] * 4,
        [
            near((MARKED, D), LOW),
            near((MARKED, D), WIDE),
            near((MARKED, D), WIDE),
            near((MARKED, D), LOW),
            near((MARKED, FF), WIDE),
            near((MARKED, FF), LOW),
            near((SEQ, D), WIDE),
            near((SEQ, FF), LOW),
            near((4, D), WIDE),
            near((D, D), LOW),
            near((D, FF), LOW),
        ],
        [VMEM] * 11,
        deps,
        scratch_shapes=[pltpu.VMEM((2, BLOCKS, 16, NORM_COLS), LOW), sems(3)],
        compiler_params=params(SCOPED),
        cost_estimate=cost(2 * SEQ * D * (D + FF), 22e6, SEQ * FF),
    )


def call_turn(info, x_both, sel_both, deps=()):
    return call(
        turn_kernel,
        "turn",
        [info, x_both, sel_both],
        [SMEM] + [VMEM] * 2,
        [near((D, SEQ), LOW)] * 2 + [near((D, MARKED), LOW)] * 2,
        [VMEM] * 4,
        deps,
        compiler_params=params(SCOPED),
        cost_estimate=cost(4 * SEQ * D * D, 6e6),
    )


def call_marked_back(info, sel, cotangent, cot_other, resident, third, deps=()):
    return call(
        marked_back_kernel,
        "marked_back",
        [info, sel, cotangent, cot_other, *held(*resident), *third],
        [SMEM] + [VMEM] * 11 + [ANY] * 4,
        [
            near((2 * MARKED, D), LOW),
            near((MARKED, D), WIDE),
            near((MARKED, D), LOW),
            near((MARKED, D), LOW),
            near((4, D), WIDE),
            near((D, FF), LOW),
        ],
        [VMEM] * 6,
        deps,
        scratch_shapes=[pltpu.VMEM((MARKED, FF), LOW), sems(1)],
        compiler_params=params(SCOPED),
        cost_estimate=cost(2.5e9, 15e6),
    )


def call_half_back(other, info, sel, qkv, grad_context, seg_row, deps=()):
    return call(
        functools.partial(half_back_kernel, other),
        "half_back",
        [info, sel, *held(qkv, grad_context), seg_row],
        [SMEM] + [VMEM] * 4,
        [near((MARKED, HALF), LOW), near((SEQ, HALF), LOW), near((SEQ, HALF), LOW)],
        [VMEM] * 3,
        deps,
        compiler_params=params(SCOPED),
        cost_estimate=cost(3e9, 6e6, 0.5e6),
    )


def call_heads_grad(info, x_turned, grad_k, grad_v, xm_turned, grad_q, dab, cm, ng, deps=()):
    width = 4 * HALF + NORM_COLS
    ins = [*held(*x_turned), *grad_k, *grad_v, *held(*xm_turned), *grad_q, *dab, *cm, *ng]
    return call(
        heads_grad_kernel,
        "heads_grad",
        [info, *ins],
        [SMEM] + [VMEM] * len(ins),
        [near((8, ROWS_OF, width), LOW)] * 2,
        [VMEM] * 2,
        deps,
        scratch_shapes=[pltpu.VMEM((BLOCKS, ROWS_OF, NORM_COLS), LOW)],
        compiler_params=params(SCOPED),
        cost_estimate=cost(4 * SEQ * D * D, 10e6),
    )


def call_ffn_grad(info, shared, expand, reduce_w, deps=()):
    tokens = MARKED * len(shared)
    wide = 4 * ROWS_OF
    return call(
        ffn_grad_kernel,
        "ffn_grad",
        [info, *shared, *held(expand, reduce_w)],
        [SMEM] + [ANY] * 8 + [VMEM] * 2,
        [near((2, ROWS_OF, FF), LOW)] * 2,
        [VMEM] * 2,
        deps,
        scratch_shapes=[
            pltpu.VMEM((wide, FF), LOW),
            pltpu.VMEM((tokens, D), LOW),
            pltpu.VMEM((tokens, D), LOW),
            pltpu.VMEM((wide, tokens), LOW),
            pltpu.VMEM((wide, tokens), LOW),
            sems(2),
        ],
        compiler_params=params(SCOPED),
        cost_estimate=cost(5e9, 10e6),
    )


def call_place(info, keep, came):
    return call(
        place_kernel,
        "place",
        [info, keep, came],
        [SMEM] + [VMEM] * 2,
        shape((2,) + keep.shape, keep.dtype),
        VMEM,
        compiler_params=params(SCOPED),
        cost_estimate=cost(1e6, 3e6),
    )


def call_input_grad(info, grad_k, grad_v, sel, grad_a, grad_q, weight, deps=()):
    return call(
        input_grad_kernel,
        "input_grad",
        [info, *held(*grad_k, *grad_v), sel, *held(grad_a, *grad_q, weight)],
        [SMEM] + [VMEM] * 9,
        [shape((SEQ // 2, D), LOW), shape((SEQ // 2, D), WIDE)],
        [VMEM] * 2,
        deps,
        compiler_params=params(SCOPED),
        cost_estimate=cost(2 * SEQ * D * 2 * D, 10e6),
    )


def call_forward_two(info, y, hidden, norms, reduce_w, deps=()):
    return call(
        forward_two_kernel,
        "forward_two",
        [info, *held(y, hidden, norms, reduce_w)],
        [SMEM] + [VMEM] * 4,
        [shape((SEQ // 2, D), LOW)] * 2,
        [VMEM] * 2,
        deps,
        compiler_params=params(SCOPED),
        cost_estimate=cost(2 * SEQ * D * FF, 16e6),
    )


def like(arrays):
    return [shape(array.shape, WIDE) for array in arrays]


def call_lamb_ffn(corr, keep, came, expand, reduce_w, deps=()):
    ins = [corr, keep, came, *expand, *reduce_w]
    return call(
        lamb_ffn_kernel,
        "lamb_ffn",
        ins,
        [SMEM] + [VMEM] * (len(ins) - 1),
        like([expand[0]] * 4 + [reduce_w[0]] * 4) + [shape((8, 128), WIDE)],
        [VMEM] * 9,
        deps,
        compiler_params=params(SCOPED),
        cost_estimate=cost(3e6, 8e6),
    )


def call_lamb_rest(corr, keep, came, sums, heads, merge, norm):
    ins = [corr, keep, *came, sums, *heads, *merge, *norm]
    return call(
        lamb_rest_kernel,
        "lamb_rest",
        ins,
        [SMEM] + [VMEM] * (len(ins) - 1),
        like([heads[0]] * 4 + [merge[0]] * 4 + [norm[0]] * 4) + [shape((8, 128), WIDE)],
        [VMEM] * 13,
        compiler_params=params(SCOPED),
        cost_estimate=cost(3e6, 8e6),
    )


def call_lamb_end(sums, weights, updates):
    return call(
        lamb_end_kernel,
        "lamb_end",
        [sums, *weights, *updates],
        [VMEM] * 11,
        like(weights) + [shape((1, 128), WIDE)],
        [VMEM] * 6,
        compiler_params=params(SCOPED),
        cost_estimate=cost(1e6, 4e6),
    )


class Grid:
    def __init__(self, depth, rows, columns):
        self.depth, self.rows, self.columns = depth, rows, columns
        self.chips = depth * rows * columns

    def chip(self, z, y, x):
        return (z * self.rows + y) * self.columns + x

    def perm(self, where):
        pairs = []
        for z in range(self.depth):
            for y in range(self.rows):
                for x in range(self.columns):
                    for t in range(2):
                        z2, y2, x2, t2 = where(z, y, x, t)
                        pairs.append(
                            (self.chip(z, y, x) * 2 + t, self.chip(z2, y2, x2) * 2 + t2)
                        )
        return pairs

    def send(self, value, where):
        return lax.ppermute(value, ALL, self.perm(where))

    def along_z(self, value, step):
        return self.send(value, lambda z, y, x, t: (z ^ step, y, x, t))

    def inner(self, value):
        return self.send(value, lambda z, y, x, t: (z, y ^ (1 - t), x ^ t, t))

    def outer(self, value):
        return self.send(value, lambda z, y, x, t: (z, y ^ t, x ^ (1 - t), t))

    def column(self, value):
        return [value] + [self.along_z(value, step) for step in range(1, self.depth)]


def after(value, *deps):
    return lax.optimization_barrier((value, *deps))[0]


def other_core(value):
    return lax.ppermute(value, "tensor", [(0, 1), (1, 0)])


def shards(
    fast,
    inputs,
    segments,
    token_marks,
    cotangent,
    heads_weight,
    merge_weight,
    expand_weight,
    reduce_weight,
    norm_params,
    first_heads,
    first_merge,
    first_expand,
    first_reduce,
    first_norm,
    second_heads,
    second_merge,
    second_expand,
    second_reduce,
    second_norm,
    step_count,
):
    member = lax.axis_index("tensor")
    here = lax.axis_index("dp")
    grid = Grid(4, 2, 2)
    norm_width = norm_params.shape[1]

    if fast:
        z, y, x = here // 4, (here // 2) % 2, here % 2

        def places(core):
            place = jnp.arange(BLOCKS, dtype=jnp.int32)
            far, near, deep = place // 8, (place // 4) % 2, place % 4
            y_place = jnp.where(core == 0, near, far)
            x_place = jnp.where(core == 0, far, near)
            return (z ^ deep) * 4 + (y ^ y_place) * 2 + (x ^ x_place)

        info = jnp.concatenate([member[None], places(member), places(1 - member), z[None]])
    else:
        order = jnp.arange(BLOCKS, dtype=jnp.int32)
        info = jnp.concatenate([member[None], order, order])
    info = info.astype(jnp.int32)

    first_part = heads_weight.astype(LOW)
    merge_turned = merge_weight.astype(LOW).T
    second_list = [merge_turned, expand_weight.astype(LOW)]
    if fast:
        top = norm_params.astype(LOW)
        rest = norm_params - top.astype(WIDE)
        middle = rest.astype(LOW)
        last = (rest - middle.astype(WIDE)).astype(LOW)
        packed = jnp.concatenate([top, middle, last], 0)
        second_list.append(
            jnp.pad(packed, ((0, ROWS_OF - 12), (0, NORM_COLS - norm_width)))
        )
    second_part = jnp.concatenate(second_list, 1)
    third_part = reduce_weight.astype(LOW).T

    def row_of(array, which):
        return lax.dynamic_index_in_dim(array, which, 0, keepdims=False)

    x_row = row_of(inputs, member)
    segment = row_of(segments, member)
    rank = jnp.cumsum(token_marks, axis=1) - 1
    sel_both = (
        (rank[:, None, :] == jnp.arange(MARKED, dtype=jnp.int32)[None, :, None])
        & (token_marks[:, None, :] == 1)
    ).astype(LOW)
    sel = row_of(sel_both, member)
    seg_row = segment[None, :]
    cot_other = other_core(row_of(cotangent, 1 - member))
    steps_float = step_count.astype(WIDE)
    corr_one = 1.0 - BETA_ONE**steps_float
    corr_two = 1.0 - BETA_TWO**steps_float
    corr = jnp.stack([corr_one, corr_two])

    if fast:
        second_part, third_part = second_part[None], third_part[None]
        four_a = call_join(
            grid.column(first_part[None]),
            [second_part, sel_both, corr, cot_other, info],
        )
        near_a = grid.inner(four_a)
        second_b = grid.along_z(after(second_part, four_a), 2)
        turned = call_turn(info, inputs, sel_both, [four_a])
        eight_a = call_join([four_a, near_a], [second_b, *turned])
        far_a = grid.outer(eight_a)
        cross_a = other_core(eight_a)
        late = after(second_part, eight_a, third_part, x_row, seg_row)
        four_b = call_join(
            [second_part, grid.along_z(late, 1), second_b, grid.along_z(late, 3)], [cross_a]
        )
        far_a, four_b = lax.optimization_barrier((far_a, four_b))
        first_w = (eight_a, far_a, cross_a, other_core(far_a))
        near_b = grid.inner(four_b)
        second_c = grid.along_z(after(third_part, four_b), 2)
        qkv, heads_full = call_qkv(info, x_row, first_w, [four_b])
        eight_b = call_join([four_b, near_b], [qkv, second_c])
        far_b = grid.outer(eight_b)
        cross_b = other_core(eight_b)
        late = after(third_part, eight_b)
        column_c = [third_part, grid.along_z(late, 1), second_c, grid.along_z(late, 3)]
        context_a = call_attend(qkv, seg_row, 0, 2, [eight_b])
        context_b = call_attend(qkv, seg_row, 2, 2, [context_a])
        four_c = call_join(column_c, [context_b, cross_b])
        far_b, four_c = lax.optimization_barrier((far_b, four_c))
        second_w = (eight_b, far_b, cross_b, other_core(far_b))
        near_c = grid.inner(four_c)
        context_c = call_attend(qkv, seg_row, 4, 2, [four_c])
        eight_c = call_join([four_c, near_c], [context_c])
        far_c = grid.outer(eight_c)
        cross_c = other_core(eight_c)
    else:

        def pieces(part):
            full = lax.all_gather(part, "dp", axis=part.ndim - 2, tiled=True)
            if part.ndim == 3:
                blocks = full.reshape(3, BLOCKS, ROWS_OF, HALF).transpose(1, 0, 2, 3)
            else:
                blocks = full.reshape(BLOCKS, ROWS_OF, part.shape[1])
            eight, rest_eight = blocks[:8], blocks[8:]
            return eight, rest_eight, other_core(eight), other_core(rest_eight)

        first_w, second_w, third_w = pieces(first_part), pieces(second_part), pieces(third_part)
        turned = call_turn(info, inputs, sel_both)
        qkv, heads_full = call_qkv(info, x_row, first_w)
        context_a, context_b, context_c = [
            call_attend(qkv, seg_row, start, 2) for start in (0, 2, 4)
        ]

    norms = None if fast else lax.all_gather(norm_params, ALL, axis=1, tiled=True)

    (
        c_marked, attended, y_marked, yb, inner, hidden, y_row, hidden_row, norms,
        merge_full, expand_full,
    ) = call_middle(
        info, sel, x_row, (context_a, context_b, context_c), norms, second_w,
        [eight_c] if fast else [],
    )
    if fast:
        third_w = (eight_c, far_c, cross_c, other_core(after(far_c, y_row)))
    cm_own, cm_par = c_marked, other_core(c_marked)
    shared, grad_a, dab, grad_context, norm_terms, reduce_full = call_marked_back(
        info, sel, cotangent, cot_other,
        (norms, y_marked, yb, hidden, inner, attended, merge_full, expand_full),
        third_w, [y_row],
    )
    if fast:
        column_d = grid.column(shared[None])
    from_other = [other_core(dab), other_core(norm_terms)]
    par_parts = call_half_back(
        True, info, sel, qkv, grad_context, seg_row
    )
    came_parts = [other_core(part) for part in par_parts]
    own_parts = call_half_back(
        False, info, sel, qkv, grad_context, seg_row, par_parts[:1]
    )
    keep, give = call_heads_grad(
        info,
        turned[:2],
        (own_parts[1], came_parts[1]),
        (own_parts[2], came_parts[2]),
        turned[2:],
        (own_parts[0], came_parts[0]),
        (dab, from_other[0]),
        (cm_own, cm_par),
        (norm_terms, from_other[1]),
    )
    grad_q, grad_k, grad_v = zip(own_parts, par_parts)

    weights = (heads_weight, merge_weight, expand_weight, reduce_weight, norm_params)
    firsts = (first_heads, first_merge, first_expand, first_reduce, first_norm)
    seconds = (second_heads, second_merge, second_expand, second_reduce, second_norm)
    if fast:
        weights, firsts, seconds = [
            tuple(v.T if index in (1, 3) else v for index, v in enumerate(values))
            for values in (weights, firsts, seconds)
        ]
        tensors = list(zip(weights, firsts, seconds))
        far = grid.outer(give)
        column_d = list(lax.optimization_barrier((*column_d, give))[:4])
        across_d = [other_core(part) for part in column_d]
        keep_ffn, give_ffn = call_ffn_grad(
            info, column_d + across_d, expand_full, reduce_full, [give]
        )
        keep, give = call_fold(4, keep, far, deps=[give_ffn])
        near = grid.inner(give)
        far_ffn = grid.outer(after(give_ffn, give))
        input_give, input_keep = call_input_grad(
            info, grad_k, grad_v, sel, grad_a, grad_q, heads_full, [give]
        )
        input_came = other_core(input_give)
        keep, *gives = call_fold(1, keep, near, 3, deps=[input_give])
        came = [grid.along_z(gives[step], step + 1) for step in range(3)]
        keep_ffn, give_ffn = call_fold(1, keep_ffn, far_ffn, deps=gives)
        came_ffn = grid.inner(give_ffn)
        output_give, output_keep = call_forward_two(
            info, y_row, hidden_row, norms, reduce_full, [give_ffn]
        )
        output_came = other_core(output_give)
        lamb_ffn = call_lamb_ffn(
            corr, keep_ffn, came_ffn, tensors[2], tensors[3], [output_give]
        )
        lamb_rest = call_lamb_rest(
            corr, keep, came, lamb_ffn[8], tensors[0], tensors[1], tensors[4]
        )
        both = lamb_rest[12]
    else:
        both_cores = (shared, other_core(shared))
        yb_all = jnp.concatenate([part[:MARKED] for part in both_cores], 0)
        db_all = jnp.concatenate([part[MARKED:] for part in both_cores], 0)
        expand_half = jnp.concatenate(second_w[:2], 0).reshape(D, -1)[:, HALF : HALF + FF_HALF]
        reduce_half = jnp.concatenate(third_w[:2], 0).reshape(D, -1)
        inner_all = dot(yb_all, expand_half)
        back_all = (dot(db_all, reduce_half) * gelu_slope(inner_all)).astype(LOW)
        hidden_all = gelu_tanh(inner_all).astype(LOW)
        part_expand = lax.psum_scatter(
            dot_first(yb_all, back_all), "dp", scatter_dimension=0, tiled=True
        )
        part_reduce = lax.psum_scatter(
            dot_first(db_all, hidden_all), "dp", scatter_dimension=0, tiled=True
        ).T
        full = jnp.concatenate([keep, give], 0).astype(WIDE).reshape(D, -1)
        summed = lax.psum_scatter(full, "dp", scatter_dimension=0, tiled=True)
        part_norm = lax.psum_scatter(norm_terms, ALL, scatter_dimension=1, tiled=True)
        input_give, input_keep = call_input_grad(
            info, grad_k, grad_v, sel, grad_a, grad_q, heads_full
        )
        output_give, output_keep = call_forward_two(info, y_row, hidden_row, norms, reduce_full)
        input_came, output_came = other_core(input_give), other_core(output_give)
        part_heads = jnp.stack([summed[:, k * HALF : (k + 1) * HALF] for k in range(3)], 0)
        part_merge = summed[:, 3 * HALF : 4 * HALF].T

    layer_output = call_place(info, output_keep, output_came)
    input_grad = call_place(info, input_keep, input_came)

    if fast:
        both = both + other_core(both)
        both = (
            both
            + grid.send(both, lambda z, y, x, t: (z, y ^ 1, x, t))
            + grid.send(both, lambda z, y, x, t: (z, y, x ^ 1, t))
            + grid.send(both, lambda z, y, x, t: (z, y ^ 1, x ^ 1, t))
        )
        both = (both + grid.along_z(both, 1)) + (grid.along_z(both, 2) + grid.along_z(both, 3))
        sets = [lamb_rest[0:4], lamb_rest[4:8], lamb_ffn[0:4], lamb_ffn[4:8], lamb_rest[8:12]]
        *nexts, ratios = call_lamb_end(both, weights, [values[3] for values in sets])
        parts, next_firsts, next_seconds = [
            [values[index] for values in sets] for index in range(3)
        ]
        parts, next_firsts, next_seconds, nexts = [
            [v.T if index in (1, 3) else v for index, v in enumerate(values)]
            for values in (parts, next_firsts, next_seconds, nexts)
        ]
        trust_ratios = ratios[0, :10]
    else:
        parts = (part_heads, part_merge, part_expand, part_reduce, part_norm)
        results = [
            moments(*values, decay, corr_one, corr_two)
            for *values, decay in zip(
                weights, parts, firsts, seconds, (DECAY, DECAY, DECAY, DECAY, 0.0)
            )
        ]
        next_firsts, next_seconds, updates = zip(*results)
        weight_total, update_total = lax.psum((squares(*weights), squares(*updates)), ALL)
        trust_ratios = jnp.sqrt(weight_total) / jnp.sqrt(update_total + 1e-12)
        ratios = (
            trust_ratios[0:3, None, None],
            trust_ratios[3],
            trust_ratios[4],
            trust_ratios[5],
            trust_ratios[6:10, None],
        )
        nexts = [
            weight - RATE * ratio * update
            for weight, ratio, update in zip(weights, ratios, updates)
        ]
    return (
        layer_output,
        input_grad,
        *parts,
        *next_firsts,
        *next_seconds,
        *nexts,
        trust_ratios,
    )


def solution(mesh):
    fast = mesh.shape["dp"] == BLOCKS and mesh.shape["tensor"] == 2
    return jax.shard_map(
        functools.partial(shards, fast),
        mesh=mesh,
        in_specs=(
            P("dp", None, None),
            P("dp", None),
            P("dp", None),
            P("dp", "tensor", None),
            P(None, "dp", "tensor"),
            P("tensor", "dp"),
            P("dp", "tensor"),
            P("tensor", "dp"),
            P(None, ("dp", "tensor")),
            P(None, "dp", "tensor"),
            P("tensor", "dp"),
            P("dp", "tensor"),
            P("tensor", "dp"),
            P(None, ("dp", "tensor")),
            P(None, "dp", "tensor"),
            P("tensor", "dp"),
            P("dp", "tensor"),
            P("tensor", "dp"),
            P(None, ("dp", "tensor")),
            P(),
        ),
        out_specs=(
            P("dp", "tensor", None),
            P("dp", "tensor", None),
            P(None, "dp", "tensor"),
            P("tensor", "dp"),
            P("dp", "tensor"),
            P("tensor", "dp"),
            P(None, ("dp", "tensor")),
            P(None, "dp", "tensor"),
            P("tensor", "dp"),
            P("dp", "tensor"),
            P("tensor", "dp"),
            P(None, ("dp", "tensor")),
            P(None, "dp", "tensor"),
            P("tensor", "dp"),
            P("dp", "tensor"),
            P("tensor", "dp"),
            P(None, ("dp", "tensor")),
            P(None, "dp", "tensor"),
            P("tensor", "dp"),
            P("dp", "tensor"),
            P("tensor", "dp"),
            P(None, ("dp", "tensor")),
            P(),
        ),
        check_vma=False,
    )
```

```python
import functools

import jax
import jax.numpy as jnp
from jax import lax
from jax.experimental import pallas as pl
from jax.experimental.pallas import tpu as pltpu
from jax.sharding import PartitionSpec as P

D = 768
HEAD = 64
SEQ = 1024
FF = 3072
HALF = D // 2
FF_HALF = FF // 2
MARKED = 80
BLOCKS = 16
ROWS_OF = D // BLOCKS
NORM_COLS = 128
PAIRS = D // 128
MIB = 1 << 20
SCOPED = 12
LONG = 3e12

NORM_EPS = 1e-12
BETA_ONE = 0.9
BETA_TWO = 0.999
ADAM_EPS = 1e-06
DECAY = 0.01
RATE = 0.25
MASKED = -1000000000.0
SCALE = HEAD ** (-0.5)
GELU_A = 0.7978845608028654
GELU_B = 0.044715
ALL = ("dp", "tensor")
LOW = jnp.bfloat16
WIDE = jnp.float32


def dot(left, right):
    return jnp.dot(left, right, preferred_element_type=WIDE)


def dot_last(left, right):
    return lax.dot_general(left, right, (((1,), (1,)), ((), ())), preferred_element_type=WIDE)


def dot_first(left, right):
    return lax.dot_general(left, right, (((0,), (0,)), ((), ())), preferred_element_type=WIDE)


def layer_norm_parts(values):
    average = jnp.mean(values, axis=-1, keepdims=True)
    centered = values - average
    spread = jnp.mean(centered * centered, axis=-1, keepdims=True)
    inverse = lax.rsqrt(spread + NORM_EPS)
    return centered * inverse, inverse


def norm_back(normed, inverse, gain, grad_out):
    scaled = grad_out * gain
    return inverse * (
        scaled
        - jnp.mean(scaled, axis=-1, keepdims=True)
        - normed * jnp.mean(scaled * normed, axis=-1, keepdims=True)
    )


def gelu_tanh(values):
    half = 0.5 * values
    return half + half * jnp.tanh(values * (GELU_A + (GELU_A * GELU_B) * (values * values)))


def gelu_slope(values):
    square = values * values
    bent = jnp.tanh(values * (GELU_A + (GELU_A * GELU_B) * square))
    return 0.5 * (1.0 + bent) + (0.5 * values) * (1.0 - bent * bent) * (
        GELU_A + (3.0 * GELU_A * GELU_B) * square
    )


def moments(weight, gradient, first, second, decay, corr_one, corr_two):
    next_first = BETA_ONE * first + (1.0 - BETA_ONE) * gradient
    next_second = BETA_TWO * second + (1.0 - BETA_TWO) * gradient * gradient
    update = next_first / corr_one / (jnp.sqrt(next_second / corr_two) + ADAM_EPS) + decay * weight
    return (next_first, next_second, update)


def squares(heads_part, merge_part, expand_part, reduce_part, norm_part):
    return jnp.concatenate(
        [
            jnp.sum(heads_part * heads_part, axis=(1, 2)),
            jnp.sum(merge_part * merge_part)[None],
            jnp.sum(expand_part * expand_part)[None],
            jnp.sum(reduce_part * reduce_part)[None],
            jnp.sum(norm_part * norm_part, axis=1),
        ]
    )


def place_weights(info, pieces, columns, target):
    member = info[0]
    width = columns[1] - columns[0]
    for place in range(2 * BLOCKS):
        row = pl.multiple_of(info[1 + place] * ROWS_OF, 16)
        start = pl.multiple_of((member if place < BLOCKS else 1 - member) * width, 128)
        target[pl.ds(row, ROWS_OF), pl.ds(start, width)] = pieces[place // 8][
            place % 8, :, columns[0] : columns[1]
        ]


def qkv_kernel(info, x_ref, a, b, c, d, out_ref, weight):
    member = info[0]
    for which in range(3):
        for place in range(2 * BLOCKS):
            side = member if place < BLOCKS else 1 - member
            row = pl.multiple_of(info[1 + place] * ROWS_OF, 16)
            column = pl.multiple_of(side * HALF, 128)
            weight[which, pl.ds(row, ROWS_OF), pl.ds(column, HALF)] = (a, b, c, d)[place // 8][
                place % 8, which
            ]
        out_ref[:, which * D : (which + 1) * D] = dot(x_ref[...], weight[which]).astype(LOW)


def lane_mask(rows, which):
    lanes = lax.broadcasted_iota(jnp.int32, (rows, 128), 1)
    return (lanes < HEAD) if which == 0 else (lanes >= HEAD)


def attend_kernel(start, count, qkv_ref, seg_row_ref, out_ref):
    seg_row = seg_row_ref[...]
    zero = jnp.float32(0)
    one = jnp.asarray(1, LOW)
    edge = seg_row[:, 256:512]
    diagonal = lax.broadcasted_iota(jnp.int32, (256, 256), 0) == lax.broadcasted_iota(
        jnp.int32, (256, 256), 1
    )
    edge_column = jnp.sum(jnp.where(diagonal, edge, 0), axis=1, keepdims=True)
    tiles = ((0, 256, 0, 512), (256, 256, 0, 1024), (512, 512, 256, 1024))

    @pl.loop(0, count)
    def _(pair):
        def lanes(base):
            return pl.ds(pl.multiple_of((base + start + pair) * 128, 128), 128)

        q_lanes, k_lanes, v_lanes = lanes(0), lanes(PAIRS), lanes(2 * PAIRS)
        values = qkv_ref[:, v_lanes]
        with_sum = [jnp.where(lane_mask(SEQ, which), values, one) for which in range(2)]
        for first, rows, low, high in tiles:
            if first == 256:
                bias = jnp.where(edge_column == seg_row, zero, MASKED)
            else:
                bias = jnp.where(edge == (0 if first == 0 else 1), zero, MASKED)
            queries = qkv_ref[first : first + rows, q_lanes] * jnp.asarray(SCALE, LOW)
            result = None
            for which in range(2):
                mask = lane_mask(rows, which)
                own = jnp.where(mask, queries, jnp.zeros_like(queries))
                scores = dot_last(own, qkv_ref[low:high, k_lanes])
                if first == 0:
                    scores = jnp.concatenate([scores[:, :256], scores[:, 256:] + bias], 1)
                elif first == 256:
                    scores = scores + bias
                else:
                    scores = jnp.concatenate([scores[:, :256] + bias, scores[:, 256:]], 1)
                top = jnp.max(scores, axis=-1, keepdims=True)
                weights = jnp.exp(scores - top).astype(LOW)
                context = dot(weights, with_sum[which][low:high, :])
                context = context / pltpu.roll(context, HEAD, 1)
                result = context if which == 0 else jnp.where(mask, context, result)
            out_ref[first : first + rows, pl.ds(pl.multiple_of(pair * 128, 128), 128)] = (
                result.astype(LOW)
            )


def middle_kernel(
    info, sel_ref, x_ref, ctx_a, ctx_b, ctx_c, norms_in, a, b, c, d,
    cm_ref, att_ref, ym_ref, yb_ref, u_ref, hm_ref, norms, merge, expand,
):
    contexts = (ctx_a, ctx_b, ctx_c)
    third = D // 3
    place_weights(info, (a, b, c, d), (0, HALF), merge)
    place_weights(info, (a, b, c, d), (HALF, HALF + FF_HALF), expand)
    chosen = sel_ref[...]
    x_marked = dot(chosen, x_ref[...])
    c_marked = [dot(chosen, part[...]).astype(LOW) for part in contexts]
    for index, part in enumerate(c_marked):
        cm_ref[:, index * third : (index + 1) * third] = part
    if norms_in is None:
        first = info[0] == 0
        sides = [
            [
                pieces[place // 8][place % 8, 0:16, HALF + FF_HALF :].astype(WIDE)
                for place in range(BLOCKS)
            ]
            for pieces in ((a, b), (c, d))
        ]
        summed = [[p[0:4] + p[4:8] + p[8:12] for p in side] for side in sides]
        lanes = lax.broadcasted_iota(jnp.int32, (4, D), 1)
        total = jnp.zeros((4, D), WIDE)
        for half in range(2):
            side = info[0] if half == 0 else 1 - info[0]
            for place in range(BLOCKS):
                start = (2 * info[1 + half * BLOCKS + place] + side) * 24
                wide = jnp.concatenate([summed[half][place]] * (D // NORM_COLS), 1)
                moved = pltpu.roll(wide, start, 1)
                total = jnp.where((lanes >= start) & (lanes < start + 24), moved, total)
        norms[...] = total
    else:
        norms[...] = norms_in[...]
    attended, y = first_norm(x_marked, c_marked, merge, norms)
    att_ref[...] = attended
    ym_ref[...] = y
    low = y.astype(LOW)
    yb_ref[...] = low

    @pl.loop(0, FF // 512)
    def _(part):
        columns = pl.ds(pl.multiple_of(part * 512, 512), 512)
        inner = dot(low, expand[:, columns])
        u_ref[:, columns] = inner
        hm_ref[:, columns] = gelu_tanh(inner).astype(LOW)


def first_norm(x, contexts, merge, norms):
    third = D // 3
    attended = x
    for index, part in enumerate(contexts):
        attended = attended + dot_last(part, merge[:, index * third : (index + 1) * third])
    normed, _unused = layer_norm_parts(attended)
    return attended, normed * norms[0:1, :] + norms[1:2, :]


def forward_one_kernel(
    x_ref, ctx_a, ctx_b, ctx_c, norms, merge, expand, y_ref, h_ref, low
):
    for tile in range(SEQ // 256):
        rows = slice(tile * 256, (tile + 1) * 256)
        _unused, y = first_norm(
            x_ref[rows, :].astype(WIDE),
            [part[rows, :] for part in (ctx_a, ctx_b, ctx_c)],
            merge,
            norms,
        )
        y_ref[rows, :] = y
        low[rows, :] = y.astype(LOW)

    @pl.loop(0, FF // 256)
    def _(part):
        columns = pl.ds(pl.multiple_of(part * 256, 256), 256)
        h_ref[:, columns] = gelu_tanh(dot(low[...], expand[:, columns])).astype(LOW)


def turn_kernel(info, x_ref, sel_ref, own_ref, par_ref, own_m_ref, par_m_ref):
    picks = pick_rows(info, 0, BLOCKS)
    for which, full_ref, marked_ref in (
        (info[0], own_ref, own_m_ref),
        (1 - info[0], par_ref, par_m_ref),
    ):
        full = dot_last(picks, x_ref[which]).astype(LOW)
        full_ref[...] = full
        marked_ref[...] = dot_last(full, sel_ref[which]).astype(LOW)


def pick_rows(info, first, count):
    within = lax.broadcasted_iota(jnp.int32, (ROWS_OF, D), 0)
    lanes = lax.broadcasted_iota(jnp.int32, (ROWS_OF, D), 1)
    return jnp.concatenate(
        [
            jnp.where(lanes == within + info[1 + place] * ROWS_OF, 1.0, 0.0)
            for place in range(first, first + count)
        ],
        0,
    ).astype(LOW)


def marked_back_kernel(
    info, sel_ref, cot_ref, cot_b, norms, y_ref, yb_ref, h_ref, u_ref, att_ref, merge, expand,
    e, f, g, h,
    yd_ref, da_ref, dab_ref, dc_ref, ng_ref, reduce_w, du,
):
    place_weights(info, (e, f, g, h), (0, FF_HALF), reduce_w)
    first = info[0] == 0
    half = SEQ // 2
    chosen = sel_ref[...]
    cot_own = cot_ref[info[0]]
    cot_low = jnp.where(first, cot_own, cot_b[...])
    cot_high = jnp.where(first, cot_b[...], cot_own)
    grad = dot(chosen[:, :half], cot_low) + dot(chosen[:, half:], cot_high)
    joined = y_ref[...] + dot_last(h_ref[...], reduce_w[...])
    normed, inverse = layer_norm_parts(joined)
    back = norm_back(normed, inverse, norms[2:3, :], grad)
    low = back.astype(LOW)
    yd_ref[:MARKED] = yb_ref[...]
    yd_ref[MARKED:] = low
    ng_ref[2:3, :] = jnp.sum(grad * normed, axis=0, keepdims=True)
    ng_ref[3:4, :] = jnp.sum(grad, axis=0, keepdims=True)
    for step in range(FF // 512):
        columns = slice(step * 512, (step + 1) * 512)
        du[:, columns] = (
            dot(low, reduce_w[:, columns]) * gelu_slope(u_ref[:, columns])
        ).astype(LOW)
    grad_y = back + dot_last(du[...], expand[...])
    normed_one, inverse_one = layer_norm_parts(att_ref[...])
    grad_a = norm_back(normed_one, inverse_one, norms[0:1, :], grad_y)
    da_ref[...] = grad_a
    grad_low = grad_a.astype(LOW)
    dab_ref[...] = grad_low
    ng_ref[0:1, :] = jnp.sum(grad_y * normed_one, axis=0, keepdims=True)
    ng_ref[1:2, :] = jnp.sum(grad_y, axis=0, keepdims=True)
    dc_ref[...] = dot(grad_low, merge[...]).astype(LOW)


def half_back_kernel(
    other, info, sel_ref, qkv_ref, dc_ref, seg_row_ref, dq_ref, dk_ref, dv_ref
):
    half = 1 - info[0] if other else info[0]
    mask = lane_mask(MARKED, 0)
    seg_row = seg_row_ref[...].astype(WIDE)
    mark_segs = jnp.sum(sel_ref[...].astype(WIDE) * seg_row, axis=1, keepdims=True)
    same = jnp.concatenate([mark_segs, mark_segs], 0) == seg_row
    for pair in range(PAIRS // 2):
        first = half * (PAIRS // 2) + pair

        def lanes(base):
            return pl.ds(pl.multiple_of((base + first) * 128, 128), 128)

        out = slice(pair * 128, (pair + 1) * 128)
        queries = dot(sel_ref[...], qkv_ref[:, lanes(0)]).astype(LOW)
        keys, values = qkv_ref[:, lanes(PAIRS)], qkv_ref[:, lanes(2 * PAIRS)]
        grads = dc_ref[:, lanes(0)]
        none = jnp.zeros_like(queries)
        query_both = jnp.concatenate(
            [jnp.where(mask, queries, none), jnp.where(mask, none, queries)], 0
        )
        grad_both = jnp.concatenate(
            [jnp.where(mask, grads, none), jnp.where(mask, none, grads)], 0
        )
        scores = dot_last(query_both * jnp.asarray(SCALE, LOW), keys)
        scores = jnp.where(same, scores, MASKED)
        top = jnp.max(scores, axis=-1, keepdims=True)
        exped = jnp.exp(scores - top)
        probs = exped * (1.0 / jnp.sum(exped, axis=-1, keepdims=True))
        grad_probs = dot_last(grad_both, values)
        delta = jnp.sum(probs * grad_probs, axis=-1, keepdims=True)
        grad_scores = (probs * (grad_probs - delta)).astype(LOW)
        dq_both = dot(grad_scores, keys) * SCALE
        dq_ref[:, out] = jnp.where(mask, dq_both[:MARKED], dq_both[MARKED:]).astype(LOW)
        dk_ref[:, out] = (dot_first(grad_scores, query_both) * SCALE).astype(LOW)
        dv_ref[:, out] = dot_first(probs.astype(LOW), grad_both).astype(LOW)


def heads_grad_kernel(
    info, xt_a, xt_b, dk_a, dk_b, dv_a, dv_b, xm_a, xm_b, dq_a, dq_b,
    dab_a, dab_b, cm_a, cm_b, ng_a, ng_b, keep_ref, give_ref, small,
):
    norm_grads = ng_a[...] + ng_b[...]
    for block in range(BLOCKS):
        sides = [
            norm_grads[:, (2 * block + side) * 24 : (2 * block + side + 1) * 24]
            for side in range(2)
        ]
        part = jnp.where(info[0] == 0, sides[0], sides[1])
        part = jnp.concatenate([part, jnp.zeros((4, NORM_COLS - 24), WIDE)], 1)
        part = jnp.concatenate([part, jnp.zeros((ROWS_OF - 4, NORM_COLS), WIDE)], 0)
        small[block] = part.astype(LOW)
    tall = 8 * ROWS_OF
    own = pl.ds(pl.multiple_of(info[0] * HALF, 128), HALF)
    for half, out_ref in ((1, give_ref), (0, keep_ref)):
        rows = slice(half * tall, (half + 1) * tall)

        def put(kind, value):
            out_ref[:, :, kind * HALF : (kind + 1) * HALF] = value.astype(LOW).reshape(
                8, ROWS_OF, HALF
            )

        put(1, dot(xt_a[rows, :], dk_a[...]) + dot(xt_b[rows, :], dk_b[...]))
        put(2, dot(xt_a[rows, :], dv_a[...]) + dot(xt_b[rows, :], dv_b[...]))
        put(0, dot(xm_a[rows, :], dq_a[...]) + dot(xm_b[rows, :], dq_b[...]))
        picks = pick_rows(info, 8 * half, 8)
        put(
            3,
            dot(dot_last(picks, dab_a[...]).astype(LOW), cm_a[:, own])
            + dot(dot_last(picks, dab_b[...]).astype(LOW), cm_b[:, own]),
        )
        for place in range(8):
            out_ref[place, :, 4 * HALF :] = small[info[1 + 8 * half + place]]


def ffn_grad_kernel(
    info, part_a, part_b, expand, reduce_w,
    keep_ref, give_ref, block, yb, db, yb_turned, db_turned,
):
    for side, part in enumerate((part_a, part_b)):
        for index in range(4):
            rows = slice((4 * side + index) * MARKED, (4 * side + index + 1) * MARKED)
            yb[rows, :] = part[index, :MARKED, :]
            db[rows, :] = part[index, MARKED:, :]
    wide = 4 * ROWS_OF
    start = info[2 * BLOCKS + 1] * wide
    picks = jnp.where(
        lax.broadcasted_iota(jnp.int32, (wide, D), 1)
        == lax.broadcasted_iota(jnp.int32, (wide, D), 0) + start,
        1.0,
        0.0,
    ).astype(LOW)
    yb_turned[...] = dot_last(picks, yb[...]).astype(LOW)
    db_turned[...] = dot_last(picks, db[...]).astype(LOW)

    @pl.loop(0, FF_HALF // 256)
    def _(step):
        columns = pl.ds(pl.multiple_of(step * 256, 256), 256)
        later = pl.ds(pl.multiple_of(FF_HALF + step * 256, 256), 256)
        own = pl.ds(pl.multiple_of(info[0] * FF_HALF + step * 256, 256), 256)
        inner = dot(yb[...], expand[:, own])
        hidden = gelu_tanh(inner).astype(LOW)
        back = (dot(db[...], reduce_w[:, own]) * gelu_slope(inner)).astype(LOW)
        block[:, columns] = dot(yb_turned[...], back).astype(LOW)
        block[:, later] = dot(db_turned[...], hidden).astype(LOW)

    for place in range(4):
        row = pl.multiple_of(lax.rem(info[1 + 4 * place], 4) * ROWS_OF, 16)
        (keep_ref, give_ref)[place // 2][place % 2] = block[pl.ds(row, ROWS_OF), :]


def input_grad_kernel(
    info, dk_own, dk_par, dv_own, dv_par, sel_ref, da_ref, dq_own, dq_par, weight,
    give_ref, keep_ref,
):
    member = info[0]

    def ordered(own, par):
        first = member == 0
        return jnp.concatenate([jnp.where(first, own, par), jnp.where(first, par, own)], 1)

    extra = da_ref[...] + dot_last(ordered(dq_own[...], dq_par[...]), weight[0])
    high = extra.astype(LOW)
    low = (extra - high.astype(WIDE)).astype(LOW)
    for tile in range(4):
        rows = token_rows(member, tile)
        chosen = sel_ref[:, rows]
        hand_out(
            dot_last(ordered(dk_own[rows, :], dk_par[rows, :]), weight[1])
            + dot_last(ordered(dv_own[rows, :], dv_par[rows, :]), weight[2])
            + dot_first(chosen, high)
            + dot_first(chosen, low),
            tile,
            give_ref,
            keep_ref,
        )


def token_rows(member, tile):
    half = 1 - member if tile < 2 else member
    return pl.ds(pl.multiple_of(half * 512 + (tile % 2) * 256, 256), 256)


def forward_two_kernel(info, y_ref, h_ref, norms, reduce_w, give_ref, keep_ref):
    for tile in range(4):
        rows = token_rows(info[0], tile)
        joined = y_ref[rows, :] + dot_last(h_ref[rows, :], reduce_w[...])
        normed, _unused = layer_norm_parts(joined)
        hand_out(normed * norms[2:3, :] + norms[3:4, :], tile, give_ref, keep_ref)


def hand_out(result, tile, give_ref, keep_ref):
    rows = slice((tile % 2) * 256, (tile % 2 + 1) * 256)
    out_ref = give_ref if tile < 2 else keep_ref
    out_ref[rows, :] = result.astype(out_ref.dtype)


def place_kernel(info, keep_ref, came_ref, out_ref):
    out_ref[info[0]] = keep_ref[...]
    out_ref[1 - info[0]] = came_ref[...].astype(out_ref.dtype)


def join_kernel(count, *refs):
    parts, out_ref = refs[:count], refs[-1]
    start = 0
    for part in parts:
        size = part.shape[0]
        out_ref[start : start + size] = part[...]
        start += size


def fold_kernel(keep, a_ref, b_ref, *outs):
    outs[0][...] = (a_ref[:keep].astype(WIDE) + b_ref[:keep].astype(WIDE)).astype(outs[0].dtype)
    sent = outs[1:]
    size = (a_ref.shape[0] - keep) // len(sent)
    for index, out in enumerate(sent):
        rows = slice(keep + index * size, keep + (index + 1) * size)
        out[...] = (a_ref[rows].astype(WIDE) + b_ref[rows].astype(WIDE)).astype(LOW)


def lamb_step(corr, refs, gradient, decay):
    weight_ref, first_ref, second_ref, grad_ref, next_first_ref, next_second_ref, u_ref = refs
    weight = weight_ref[...]
    grad_ref[...] = gradient
    first, second, update = moments(
        weight, gradient, first_ref[...], second_ref[...], decay, corr[0], corr[1]
    )
    next_first_ref[...] = first
    next_second_ref[...] = second
    u_ref[...] = update
    return weight * weight, update * update


def put_sums(sums_ref, entries):
    lanes = lax.broadcasted_iota(jnp.int32, (8, 128), 1)
    rows = lax.broadcasted_iota(jnp.int32, (8, 128), 0)
    total = jnp.zeros((8, 128), WIDE)
    for lane, (weight_square, update_square) in entries:
        for row, value in enumerate((weight_square, update_square)):
            total = total + jnp.where((lanes == lane) & (rows == row), jnp.sum(value), 0.0)
    sums_ref[...] = total


def lamb_ffn_kernel(corr, keep_ref, came_ref, other_sums, *refs):
    expand, reduce_refs, sums_ref = refs[0:3] + refs[6:10], refs[3:6] + refs[10:14], refs[14]
    summed = keep_ref[0].astype(WIDE) + came_ref[0].astype(WIDE)
    put_sums(
        sums_ref,
        [
            (4, lamb_step(corr, expand, summed[:, :FF_HALF], DECAY)),
            (5, lamb_step(corr, reduce_refs, summed[:, FF_HALF:], DECAY)),
        ],
    )
    sums_ref[...] += other_sums[...]


def lamb_rest_kernel(corr, keep_ref, came_a, came_b, came_c, *refs):
    heads, merge, norm = refs[0:3] + refs[9:13], refs[3:6] + refs[13:17], refs[6:9] + refs[17:21]
    sums_ref = refs[21]
    summed = (
        keep_ref[0].astype(WIDE)
        + came_a[0].astype(WIDE)
        + came_b[0].astype(WIDE)
        + came_c[0].astype(WIDE)
    )
    norm_width = norm[0].shape[1]
    heads_grad = jnp.stack([summed[:, k * HALF : (k + 1) * HALF] for k in range(3)], 0)
    squares_w, squares_u = lamb_step(corr, heads, heads_grad, DECAY)
    entries = [(k, (squares_w[k], squares_u[k])) for k in range(3)]
    merge_grad = summed[:, 3 * HALF : 4 * HALF]
    entries.append((3, lamb_step(corr, merge, merge_grad, DECAY)))
    norm_grad = summed[:4, 4 * HALF : 4 * HALF + norm_width]
    squares_w, squares_u = lamb_step(corr, norm, norm_grad, 0.0)
    entries += [(6 + k, (squares_w[k : k + 1], squares_u[k : k + 1])) for k in range(4)]
    put_sums(sums_ref, entries)


def lamb_end_kernel(sums_ref, *refs):
    sums = sums_ref[...]
    ratios = jnp.sqrt(sums[0:1, :]) / jnp.sqrt(sums[1:2, :] + 1e-12)
    refs[15][...] = ratios
    weights, updates, outs = refs[0:5], refs[5:10], refs[10:15]

    def moved(index, part, ratio):
        return weights[index][part] - RATE * ratio * updates[index][part]

    for k in range(3):
        outs[0][k] = moved(0, k, ratios[:, k : k + 1])
    for index in range(1, 4):
        outs[index][...] = moved(index, Ellipsis, ratios[:, 2 + index : 3 + index])
    for k in range(4):
        outs[4][k : k + 1] = moved(4, slice(k, k + 1), ratios[:, 6 + k : 7 + k])


ANY = pl.BlockSpec(memory_space=pl.ANY)
SMEM = pl.BlockSpec(memory_space=pltpu.SMEM)
VMEM = pl.BlockSpec(memory_space=pltpu.VMEM)


def shape(dims, kind):
    return jax.ShapeDtypeStruct(dims, kind)


def params(mib):
    return pltpu.CompilerParams(vmem_limit_bytes=mib * MIB)


def cost(flops, moved, hard=0):
    return pl.CostEstimate(
        flops=int(flops) // 50, bytes_accessed=int(moved) // 50, transcendentals=int(hard) // 50
    )


def whole(dims):
    return pl.BlockSpec(dims, lambda *_: (0,) * len(dims))


def near(dims, kind):
    return pltpu.VMEM(dims, kind)


def held(*arrays):
    return [pltpu.with_memory_space_constraint(array, pltpu.VMEM) for array in arrays]


def call(kernel, name, ins, specs, out_shape, out_specs, deps=(), **options):
    count, extra = len(ins), len(deps)

    def body(*refs):
        kernel(*refs[:count], *refs[count + extra :])

    return pl.pallas_call(
        body,
        in_specs=list(specs) + [ANY] * extra,
        out_specs=out_specs,
        out_shape=out_shape,
        name=name,
        **options,
    )(*ins, *deps)


def call_join(parts, deps=(), work=0):
    count = len(parts)
    rows = sum(part.shape[0] for part in parts)
    return call(
        functools.partial(join_kernel, count),
        "join",
        held(*parts),
        [VMEM] * count,
        near((rows,) + parts[0].shape[1:], parts[0].dtype),
        VMEM,
        deps,
        compiler_params=params(SCOPED),
        cost_estimate=cost(work, 4 * rows * parts[0][0].size),
    )


def call_fold(keep, left, right, sends=1, deps=()):
    block = left.shape[1:]
    size = (left.shape[0] - keep) // sends
    return call(
        functools.partial(fold_kernel, keep),
        "fold",
        [left, right],
        [VMEM] * 2,
        [shape((keep,) + block, LOW)] + [shape((size,) + block, LOW)] * sends,
        [VMEM] * (1 + sends),
        deps,
        compiler_params=params(SCOPED),
        cost_estimate=cost(left.size, 4 * left.size),
    )


def call_qkv(info, x, first, deps=()):
    return call(
        qkv_kernel,
        "project",
        [info, x, *held(*first)],
        [SMEM] + [VMEM] * 5,
        [near((SEQ, 3 * D), LOW), near((3, D, D), LOW)],
        [VMEM] * 2,
        deps,
        compiler_params=params(SCOPED),
        cost_estimate=cost(2 * SEQ * D * 3 * D, 10e6),
    )


def call_attend(qkv, seg_row, start, count, deps=()):
    return call(
        functools.partial(attend_kernel, start, count),
        "attend",
        [*held(qkv), seg_row],
        [VMEM] * 2,
        near((SEQ, 128 * count), LOW),
        VMEM,
        deps,
        compiler_params=params(SCOPED),
        cost_estimate=cost(3 * SEQ * SEQ * 128 * 2 * count, 1e6 * count, 1.5e6 * count),
    )


def call_middle(info, sel, x, contexts, norms, second, deps=()):
    ins = [info, sel, x, *held(*contexts)]
    specs = [SMEM] + [VMEM] * 5
    if norms is None:

        def kernel(*refs):
            middle_kernel(*refs[:6], None, *refs[6:])

    else:
        kernel = middle_kernel
        ins.append(norms)
        specs.append(VMEM)
    return call(
        kernel,
        "middle",
        ins + held(*second),
        specs + [VMEM] * 4,
        [
            near((MARKED, D), LOW),
            near((MARKED, D), WIDE),
            near((MARKED, D), WIDE),
            near((MARKED, D), LOW),
            near((MARKED, FF), WIDE),
            near((MARKED, FF), LOW),
            near((4, D), WIDE),
            near((D, D), LOW),
            near((D, FF), LOW),
        ],
        [VMEM] * 9,
        deps,
        compiler_params=params(SCOPED),
        cost_estimate=cost(1.5e9, 10e6, MARKED * FF),
    )


def call_forward_one(x, contexts, norms, merge, expand, deps=()):
    return call(
        forward_one_kernel,
        "forward_one",
        [x, *held(*contexts, norms, merge, expand)],
        [VMEM] * 7,
        [near((SEQ, D), WIDE), near((SEQ, FF), LOW)],
        [VMEM] * 2,
        deps,
        scratch_shapes=[pltpu.VMEM((SEQ, D), LOW)],
        compiler_params=params(SCOPED),
        cost_estimate=cost(2 * SEQ * D * (D + FF), 22e6, SEQ * FF),
    )


def call_turn(info, x_both, sel_both, deps=()):
    return call(
        turn_kernel,
        "turn",
        [info, x_both, sel_both],
        [SMEM] + [VMEM] * 2,
        [near((D, SEQ), LOW)] * 2 + [near((D, MARKED), LOW)] * 2,
        [VMEM] * 4,
        deps,
        compiler_params=params(SCOPED),
        cost_estimate=cost(4 * SEQ * D * D, 6e6),
    )


def call_marked_back(info, sel, cotangent, cot_other, resident, third, deps=()):
    return call(
        marked_back_kernel,
        "marked_back",
        [info, sel, cotangent, cot_other, *held(*resident), *held(*third)],
        [SMEM] + [VMEM] * 15,
        [
            near((2 * MARKED, D), LOW),
            near((MARKED, D), WIDE),
            near((MARKED, D), LOW),
            near((MARKED, D), LOW),
            near((4, D), WIDE),
            near((D, FF), LOW),
        ],
        [VMEM] * 6,
        deps,
        scratch_shapes=[pltpu.VMEM((MARKED, FF), LOW)],
        compiler_params=params(SCOPED),
        cost_estimate=cost(2.5e9, 15e6),
    )


def call_half_back(other, info, sel, qkv, grad_context, seg_row, deps=(), work=3e9):
    return call(
        functools.partial(half_back_kernel, other),
        "half_back",
        [info, sel, *held(qkv, grad_context), seg_row],
        [SMEM] + [VMEM] * 4,
        [near((MARKED, HALF), LOW), near((SEQ, HALF), LOW), near((SEQ, HALF), LOW)],
        [VMEM] * 3,
        deps,
        compiler_params=params(SCOPED),
        cost_estimate=cost(work, 6e6, 0.5e6),
    )


def call_heads_grad(info, x_turned, grad_k, grad_v, xm_turned, grad_q, dab, cm, ng, deps=()):
    width = 4 * HALF + NORM_COLS
    ins = [*held(*x_turned), *grad_k, *grad_v, *held(*xm_turned), *grad_q, *dab, *cm, *ng]
    return call(
        heads_grad_kernel,
        "heads_grad",
        [info, *ins],
        [SMEM] + [VMEM] * len(ins),
        [near((8, ROWS_OF, width), LOW)] * 2,
        [VMEM] * 2,
        deps,
        scratch_shapes=[pltpu.VMEM((BLOCKS, ROWS_OF, NORM_COLS), LOW)],
        compiler_params=params(SCOPED),
        cost_estimate=cost(4 * SEQ * D * D, 10e6),
    )


def call_ffn_grad(info, shared, expand, reduce_w, deps=()):
    tokens = 8 * MARKED
    wide = 4 * ROWS_OF
    return call(
        ffn_grad_kernel,
        "ffn_grad",
        [info, *held(*shared, expand, reduce_w)],
        [SMEM] + [VMEM] * 4,
        [near((2, ROWS_OF, FF), LOW)] * 2,
        [VMEM] * 2,
        deps,
        scratch_shapes=[
            pltpu.VMEM((wide, FF), LOW),
            pltpu.VMEM((tokens, D), LOW),
            pltpu.VMEM((tokens, D), LOW),
            pltpu.VMEM((wide, tokens), LOW),
            pltpu.VMEM((wide, tokens), LOW),
        ],
        compiler_params=params(SCOPED),
        cost_estimate=cost(5e9, 10e6),
    )


def call_place(info, keep, came, deps=()):
    return call(
        place_kernel,
        "place",
        [info, keep, came],
        [SMEM] + [VMEM] * 2,
        pltpu.HBM((2,) + keep.shape, keep.dtype),
        VMEM,
        deps,
        compiler_params=params(SCOPED),
        cost_estimate=cost(1e6, 3e6),
    )


def call_input_grad(info, grad_k, grad_v, sel, grad_a, grad_q, weight, deps=()):
    return call(
        input_grad_kernel,
        "input_grad",
        [info, *held(*grad_k, *grad_v), sel, *held(grad_a, *grad_q, weight)],
        [SMEM] + [VMEM] * 9,
        [shape((SEQ // 2, D), LOW), shape((SEQ // 2, D), WIDE)],
        [VMEM] * 2,
        deps,
        compiler_params=params(SCOPED),
        cost_estimate=cost(2 * SEQ * D * 2 * D, 10e6),
    )


def call_forward_two(info, y, hidden, norms, reduce_w, deps=()):
    return call(
        forward_two_kernel,
        "forward_two",
        [info, *held(y, hidden, norms, reduce_w)],
        [SMEM] + [VMEM] * 4,
        [shape((SEQ // 2, D), LOW)] * 2,
        [VMEM] * 2,
        deps,
        compiler_params=params(SCOPED),
        cost_estimate=cost(2 * SEQ * D * FF, 16e6),
    )


def like(arrays):
    return [shape(array.shape, WIDE) for array in arrays]


def call_lamb_ffn(corr, keep, came, sums, expand, reduce_w, deps=()):
    ins = [corr, keep, came, sums, *expand, *reduce_w]
    return call(
        lamb_ffn_kernel,
        "lamb_ffn",
        ins,
        [SMEM] + [VMEM] * (len(ins) - 1),
        like([expand[0]] * 4 + [reduce_w[0]] * 4) + [shape((8, 128), WIDE)],
        [VMEM] * 9,
        deps,
        compiler_params=params(SCOPED),
        cost_estimate=cost(3e6, 8e6),
    )


def call_lamb_rest(corr, keep, came, heads, merge, norm, deps):
    ins = [corr, keep, *came, *heads, *merge, *norm]
    return call(
        lamb_rest_kernel,
        "lamb_rest",
        ins,
        [SMEM] + [VMEM] * (len(ins) - 1),
        like([heads[0]] * 4 + [merge[0]] * 4 + [norm[0]] * 4) + [shape((8, 128), WIDE)],
        [VMEM] * 13,
        deps,
        compiler_params=params(SCOPED),
        cost_estimate=cost(LONG, 8e6),
    )


def call_lamb_end(sums, weights, updates, deps):
    return call(
        lamb_end_kernel,
        "lamb_end",
        [sums, *weights, *updates],
        [VMEM] * 11,
        like(weights) + [shape((1, 128), WIDE)],
        [VMEM] * 6,
        deps,
        compiler_params=params(SCOPED),
        cost_estimate=cost(1e6, 4e6),
    )


class Grid:
    def __init__(self, depth, rows, columns):
        self.depth, self.rows, self.columns = depth, rows, columns
        self.chips = depth * rows * columns

    def chip(self, z, y, x):
        return (z * self.rows + y) * self.columns + x

    def perm(self, where):
        pairs = []
        for z in range(self.depth):
            for y in range(self.rows):
                for x in range(self.columns):
                    for t in range(2):
                        z2, y2, x2, t2 = where(z, y, x, t)
                        pairs.append(
                            (self.chip(z, y, x) * 2 + t, self.chip(z2, y2, x2) * 2 + t2)
                        )
        return pairs

    def send(self, value, where):
        return lax.ppermute(value, ALL, self.perm(where))

    def along_z(self, value, step):
        return self.send(value, lambda z, y, x, t: (z ^ step, y, x, t))

    def inner(self, value):
        return self.send(value, lambda z, y, x, t: (z, y ^ (1 - t), x ^ t, t))

    def outer(self, value):
        return self.send(value, lambda z, y, x, t: (z, y ^ t, x ^ (1 - t), t))

    def column(self, value):
        return [value] + [self.along_z(value, step) for step in range(1, self.depth)]


def after(value, *deps):
    return lax.optimization_barrier((value, *deps))[0]


def other_core(value):
    return lax.ppermute(value, "tensor", [(0, 1), (1, 0)])


def shards(
    fast,
    inputs,
    segments,
    token_marks,
    cotangent,
    heads_weight,
    merge_weight,
    expand_weight,
    reduce_weight,
    norm_params,
    first_heads,
    first_merge,
    first_expand,
    first_reduce,
    first_norm,
    second_heads,
    second_merge,
    second_expand,
    second_reduce,
    second_norm,
    step_count,
):
    member = lax.axis_index("tensor")
    here = lax.axis_index("dp")
    grid = Grid(4, 2, 2)
    norm_width = norm_params.shape[1]

    if fast:
        z, y, x = here // 4, (here // 2) % 2, here % 2

        def places(core):
            place = jnp.arange(BLOCKS, dtype=jnp.int32)
            far, near, deep = place // 8, (place // 4) % 2, place % 4
            y_place = jnp.where(core == 0, near, far)
            x_place = jnp.where(core == 0, far, near)
            return (z ^ deep) * 4 + (y ^ y_place) * 2 + (x ^ x_place)

        info = jnp.concatenate([member[None], places(member), places(1 - member), z[None]])
    else:
        order = jnp.arange(BLOCKS, dtype=jnp.int32)
        info = jnp.concatenate([member[None], order, order])
    info = info.astype(jnp.int32)

    first_part = heads_weight.astype(LOW)
    merge_turned = merge_weight.astype(LOW).T
    second_list = [merge_turned, expand_weight.astype(LOW)]
    if fast:
        top = norm_params.astype(LOW)
        rest = norm_params - top.astype(WIDE)
        middle = rest.astype(LOW)
        last = (rest - middle.astype(WIDE)).astype(LOW)
        packed = jnp.concatenate([top, middle, last], 0)
        second_list.append(
            jnp.pad(packed, ((0, ROWS_OF - 12), (0, NORM_COLS - norm_width)))
        )
    second_part = jnp.concatenate(second_list, 1)
    third_part = reduce_weight.astype(LOW).T

    def row_of(array, which):
        return lax.dynamic_index_in_dim(array, which, 0, keepdims=False)

    x_row = row_of(inputs, member)
    segment = row_of(segments, member)
    rank = jnp.cumsum(token_marks, axis=1) - 1
    sel_both = (
        (rank[:, None, :] == jnp.arange(MARKED, dtype=jnp.int32)[None, :, None])
        & (token_marks[:, None, :] == 1)
    ).astype(LOW)
    sel = row_of(sel_both, member)
    seg_row = segment[None, :]
    cot_other = other_core(row_of(cotangent, 1 - member))
    steps_float = step_count.astype(WIDE)
    corr_one = 1.0 - BETA_ONE**steps_float
    corr_two = 1.0 - BETA_TWO**steps_float
    corr = jnp.stack([corr_one, corr_two])

    if fast:
        second_part, third_part = second_part[None], third_part[None]
        four_a = call_join(
            grid.column(first_part[None]),
            [second_part, sel_both, corr, cot_other, info],
        )
        near_a = grid.inner(four_a)
        second_b = grid.along_z(after(second_part, four_a), 2)
        turned = call_turn(info, inputs, sel_both, [four_a])
        eight_a = call_join([four_a, near_a], [second_b, *turned])
        far_a = grid.outer(eight_a)
        cross_a = other_core(eight_a)
        late = after(second_part, eight_a, third_part, x_row, seg_row)
        four_b = call_join(
            [second_part, grid.along_z(late, 1), second_b, grid.along_z(late, 3)], [cross_a]
        )
        far_a, four_b = lax.optimization_barrier((far_a, four_b))
        first_w = (eight_a, far_a, cross_a, other_core(far_a))
        near_b = grid.inner(four_b)
        second_c = grid.along_z(after(third_part, four_b), 2)
        qkv, heads_full = call_qkv(info, x_row, first_w, [four_b])
        eight_b = call_join([four_b, near_b], [qkv, second_c])
        far_b = grid.outer(eight_b)
        cross_b = other_core(eight_b)
        late = after(third_part, eight_b)
        column_c = [third_part, grid.along_z(late, 1), second_c, grid.along_z(late, 3)]
        context_a = call_attend(qkv, seg_row, 0, 2, [eight_b])
        context_b = call_attend(qkv, seg_row, 2, 2, [context_a])
        four_c = call_join(column_c, [context_b, cross_b])
        far_b, four_c = lax.optimization_barrier((far_b, four_c))
        second_w = (eight_b, far_b, cross_b, other_core(far_b))
        near_c = grid.inner(four_c)
        context_c = call_attend(qkv, seg_row, 4, 2, [four_c])
        eight_c = call_join([four_c, near_c], [context_c])
        far_c = grid.outer(eight_c)
        cross_c = other_core(eight_c)
    else:

        def pieces(part):
            full = lax.all_gather(part, "dp", axis=part.ndim - 2, tiled=True)
            if part.ndim == 3:
                blocks = full.reshape(3, BLOCKS, ROWS_OF, HALF).transpose(1, 0, 2, 3)
            else:
                blocks = full.reshape(BLOCKS, ROWS_OF, part.shape[1])
            eight, rest_eight = blocks[:8], blocks[8:]
            return eight, rest_eight, other_core(eight), other_core(rest_eight)

        first_w, second_w, third_w = pieces(first_part), pieces(second_part), pieces(third_part)
        turned = call_turn(info, inputs, sel_both)
        qkv, heads_full = call_qkv(info, x_row, first_w)
        context_a, context_b, context_c = [
            call_attend(qkv, seg_row, start, 2) for start in (0, 2, 4)
        ]

    norms = None if fast else lax.all_gather(norm_params, ALL, axis=1, tiled=True)

    contexts = (context_a, context_b, context_c)
    c_marked, attended, y_marked, yb, inner, hidden, norms, merge_full, expand_full = call_middle(
        info, sel, x_row, contexts, norms, second_w, [eight_c] if fast else []
    )
    cm_own, cm_par = c_marked, other_core(c_marked)
    y_row, hidden_row = call_forward_one(
        x_row, contexts, norms, merge_full, expand_full, [yb]
    )
    if fast:
        third_w = (eight_c, far_c, cross_c, other_core(after(far_c, y_row)))
    shared, grad_a, dab, grad_context, norm_terms, reduce_full = call_marked_back(
        info, sel, cotangent, cot_other,
        (norms, y_marked, yb, hidden, inner, attended, merge_full, expand_full),
        third_w, [y_row],
    )
    shared = shared[None]
    early_d = [grid.along_z(shared, step) for step in (1, 2)] if fast else [shared]
    from_other = [other_core(dab), other_core(norm_terms)]
    par_parts = call_half_back(
        True, info, sel, qkv, grad_context, seg_row
    )
    came_parts = [other_core(part) for part in par_parts]
    own_parts = call_half_back(
        False, info, sel, qkv, grad_context, seg_row, par_parts[:1]
    )
    own_q = call_join(own_parts[:1], early_d, LONG)
    keep, give = call_heads_grad(
        info,
        turned[:2],
        (own_parts[1], came_parts[1]),
        (own_parts[2], came_parts[2]),
        turned[2:],
        (own_q, came_parts[0]),
        (dab, from_other[0]),
        (cm_own, cm_par),
        (norm_terms, from_other[1]),
    )
    grad_q, grad_k, grad_v = zip(own_parts, par_parts)

    weights = (heads_weight, merge_weight, expand_weight, reduce_weight, norm_params)
    firsts = (first_heads, first_merge, first_expand, first_reduce, first_norm)
    seconds = (second_heads, second_merge, second_expand, second_reduce, second_norm)
    if fast:
        weights, firsts, seconds = [
            tuple(v.T if index in (1, 3) else v for index, v in enumerate(values))
            for values in (weights, firsts, seconds)
        ]
        tensors = list(zip(weights, firsts, seconds))
        far = grid.outer(give)
        late = after(shared, give)
        column_d = [shared, *early_d, grid.along_z(late, 3)]
        input_give, input_keep = call_input_grad(
            info, grad_k, grad_v, sel, grad_a, grad_q, heads_full, [give]
        )
        input_came = other_core(input_give)
        output_give, output_keep = call_forward_two(
            info, y_row, hidden_row, norms, reduce_full, [input_give]
        )
        output_came = other_core(output_give)
        keep, give = call_fold(4, keep, far, deps=[output_give])
        near_heads = grid.inner(give)
        shared_four = call_join(column_d, [give])
        keep_ffn, give_ffn = call_ffn_grad(
            info, (shared_four, other_core(shared_four)), expand_full, reduce_full, [give]
        )
        keep, *gives = call_fold(1, keep, near_heads, 3, deps=[give_ffn])
        came = [grid.along_z(gives[step], step + 1) for step in range(3)]
        far_ffn = grid.outer(after(give_ffn, keep))
        layer_output = call_place(info, output_keep, output_came, gives)
        keep_ffn, give_ffn = call_fold(1, keep_ffn, far_ffn, deps=[layer_output])
        came_ffn = grid.inner(give_ffn)
        input_grad = call_place(info, input_keep, input_came, [give_ffn])
        lamb_rest = call_lamb_rest(
            corr, keep, came, tensors[0], tensors[1], tensors[4], [input_grad]
        )
        lamb_ffn = call_lamb_ffn(
            corr, keep_ffn, came_ffn, lamb_rest[12], tensors[2], tensors[3]
        )
        both = lamb_ffn[8]
    else:
        both_cores = (shared[0], other_core(shared[0]))
        yb_all = jnp.concatenate([part[:MARKED] for part in both_cores], 0)
        db_all = jnp.concatenate([part[MARKED:] for part in both_cores], 0)
        expand_half = jnp.concatenate(second_w[:2], 0).reshape(D, -1)[:, HALF : HALF + FF_HALF]
        reduce_half = jnp.concatenate(third_w[:2], 0).reshape(D, -1)
        inner_all = dot(yb_all, expand_half)
        back_all = (dot(db_all, reduce_half) * gelu_slope(inner_all)).astype(LOW)
        hidden_all = gelu_tanh(inner_all).astype(LOW)
        part_expand = lax.psum_scatter(
            dot_first(yb_all, back_all), "dp", scatter_dimension=0, tiled=True
        )
        part_reduce = lax.psum_scatter(
            dot_first(db_all, hidden_all), "dp", scatter_dimension=0, tiled=True
        ).T
        full = jnp.concatenate([keep, give], 0).astype(WIDE).reshape(D, -1)
        summed = lax.psum_scatter(full, "dp", scatter_dimension=0, tiled=True)
        part_norm = lax.psum_scatter(norm_terms, ALL, scatter_dimension=1, tiled=True)
        input_give, input_keep = call_input_grad(
            info, grad_k, grad_v, sel, grad_a, grad_q, heads_full
        )
        output_give, output_keep = call_forward_two(info, y_row, hidden_row, norms, reduce_full)
        input_came, output_came = other_core(input_give), other_core(output_give)
        part_heads = jnp.stack([summed[:, k * HALF : (k + 1) * HALF] for k in range(3)], 0)
        part_merge = summed[:, 3 * HALF : 4 * HALF].T

    if not fast:
        layer_output = call_place(info, output_keep, output_came)
        input_grad = call_place(info, input_keep, input_came)

    if fast:
        both = both + other_core(both)
        both = (
            both
            + grid.send(both, lambda z, y, x, t: (z, y ^ 1, x, t))
            + grid.send(both, lambda z, y, x, t: (z, y, x ^ 1, t))
            + grid.send(both, lambda z, y, x, t: (z, y ^ 1, x ^ 1, t))
        )
        both = (both + grid.along_z(both, 1)) + (grid.along_z(both, 2) + grid.along_z(both, 3))
        sets = [lamb_rest[0:4], lamb_rest[4:8], lamb_ffn[0:4], lamb_ffn[4:8], lamb_rest[8:12]]
        *nexts, ratios = call_lamb_end(
            both, weights, [values[3] for values in sets], [input_grad]
        )
        parts, next_firsts, next_seconds = [
            [values[index] for values in sets] for index in range(3)
        ]
        parts, next_firsts, next_seconds, nexts = [
            [v.T if index in (1, 3) else v for index, v in enumerate(values)]
            for values in (parts, next_firsts, next_seconds, nexts)
        ]
        trust_ratios = ratios[0, :10]
    else:
        parts = (part_heads, part_merge, part_expand, part_reduce, part_norm)
        results = [
            moments(*values, decay, corr_one, corr_two)
            for *values, decay in zip(
                weights, parts, firsts, seconds, (DECAY, DECAY, DECAY, DECAY, 0.0)
            )
        ]
        next_firsts, next_seconds, updates = zip(*results)
        weight_total, update_total = lax.psum((squares(*weights), squares(*updates)), ALL)
        trust_ratios = jnp.sqrt(weight_total) / jnp.sqrt(update_total + 1e-12)
        ratios = (
            trust_ratios[0:3, None, None],
            trust_ratios[3],
            trust_ratios[4],
            trust_ratios[5],
            trust_ratios[6:10, None],
        )
        nexts = [
            weight - RATE * ratio * update
            for weight, ratio, update in zip(weights, ratios, updates)
        ]
    return (
        layer_output,
        input_grad,
        *parts,
        *next_firsts,
        *next_seconds,
        *nexts,
        trust_ratios,
    )


def solution(mesh):
    fast = mesh.shape["dp"] == BLOCKS and mesh.shape["tensor"] == 2
    return jax.shard_map(
        functools.partial(shards, fast),
        mesh=mesh,
        in_specs=(
            P("dp", None, None),
            P("dp", None),
            P("dp", None),
            P("dp", "tensor", None),
            P(None, "dp", "tensor"),
            P("tensor", "dp"),
            P("dp", "tensor"),
            P("tensor", "dp"),
            P(None, ("dp", "tensor")),
            P(None, "dp", "tensor"),
            P("tensor", "dp"),
            P("dp", "tensor"),
            P("tensor", "dp"),
            P(None, ("dp", "tensor")),
            P(None, "dp", "tensor"),
            P("tensor", "dp"),
            P("dp", "tensor"),
            P("tensor", "dp"),
            P(None, ("dp", "tensor")),
            P(),
        ),
        out_specs=(
            P("dp", "tensor", None),
            P("dp", "tensor", None),
            P(None, "dp", "tensor"),
            P("tensor", "dp"),
            P("dp", "tensor"),
            P("tensor", "dp"),
            P(None, ("dp", "tensor")),
            P(None, "dp", "tensor"),
            P("tensor", "dp"),
            P("dp", "tensor"),
            P("tensor", "dp"),
            P(None, ("dp", "tensor")),
            P(None, "dp", "tensor"),
            P("tensor", "dp"),
            P("dp", "tensor"),
            P("tensor", "dp"),
            P(None, ("dp", "tensor")),
            P(None, "dp", "tensor"),
            P("tensor", "dp"),
            P("dp", "tensor"),
            P("tensor", "dp"),
            P(None, ("dp", "tensor")),
            P(),
        ),
        check_vma=False,
    )
```

```python
import functools

import jax
import jax.numpy as jnp
from jax import lax
from jax.experimental import pallas as pl
from jax.experimental.pallas import tpu as pltpu
from jax.sharding import PartitionSpec as P

D = 768
HEAD = 64
SEQ = 1024
FF = 3072
HALF = D // 2
FF_HALF = FF // 2
MARKED = 80
BLOCKS = 16
ROWS_OF = D // BLOCKS
NORM_COLS = 128
PAIRS = D // 128
MIB = 1 << 20
SCOPED = 12
LONG = 3e12
WIDTH_C = 1024

NORM_EPS = 1e-12
BETA_ONE = 0.9
BETA_TWO = 0.999
ADAM_EPS = 1e-06
DECAY = 0.01
RATE = 0.25
MASKED = -1000000000.0
SCALE = HEAD ** (-0.5)
GELU_A = 0.7978845608028654
GELU_B = 0.044715
ALL = ("dp", "tensor")
LOW = jnp.bfloat16
WIDE = jnp.float32


def dot(left, right):
    return jnp.dot(left, right, preferred_element_type=WIDE)


def dot_last(left, right):
    return lax.dot_general(left, right, (((1,), (1,)), ((), ())), preferred_element_type=WIDE)


def dot_first(left, right):
    return lax.dot_general(left, right, (((0,), (0,)), ((), ())), preferred_element_type=WIDE)


def layer_norm_parts(values):
    average = jnp.mean(values, axis=-1, keepdims=True)
    centered = values - average
    spread = jnp.mean(centered * centered, axis=-1, keepdims=True)
    inverse = lax.rsqrt(spread + NORM_EPS)
    return centered * inverse, inverse


def norm_back(normed, inverse, gain, grad_out):
    scaled = grad_out * gain
    return inverse * (
        scaled
        - jnp.mean(scaled, axis=-1, keepdims=True)
        - normed * jnp.mean(scaled * normed, axis=-1, keepdims=True)
    )


def gelu_tanh(values):
    half = 0.5 * values
    return half + half * jnp.tanh(values * (GELU_A + (GELU_A * GELU_B) * (values * values)))


def gelu_slope(values):
    square = values * values
    bent = jnp.tanh(values * (GELU_A + (GELU_A * GELU_B) * square))
    return 0.5 * (1.0 + bent) + (0.5 * values) * (1.0 - bent * bent) * (
        GELU_A + (3.0 * GELU_A * GELU_B) * square
    )


def moments(weight, gradient, first, second, decay, corr_one, corr_two):
    next_first = BETA_ONE * first + (1.0 - BETA_ONE) * gradient
    next_second = BETA_TWO * second + (1.0 - BETA_TWO) * gradient * gradient
    update = next_first / corr_one / (jnp.sqrt(next_second / corr_two) + ADAM_EPS) + decay * weight
    return (next_first, next_second, update)


def squares(heads_part, merge_part, expand_part, reduce_part, norm_part):
    return jnp.concatenate(
        [
            jnp.sum(heads_part * heads_part, axis=(1, 2)),
            jnp.sum(merge_part * merge_part)[None],
            jnp.sum(expand_part * expand_part)[None],
            jnp.sum(reduce_part * reduce_part)[None],
            jnp.sum(norm_part * norm_part, axis=1),
        ]
    )


def place_weights(info, pieces, columns, target, span=None):
    member = info[0]
    width = columns[1] - columns[0]
    for place in range(2 * BLOCKS):
        row = pl.multiple_of(info[1 + place] * ROWS_OF, 16)
        side = member if place < BLOCKS else 1 - member
        start = pl.multiple_of(side * (span or width), 128)
        target[pl.ds(row, ROWS_OF), pl.ds(start, width)] = pieces[place // 8][
            place % 8, :, columns[0] : columns[1]
        ]


def place_last(info, halves, target, span, offset):
    width = span - offset
    for half, blocks in enumerate(halves):
        side = info[0] if half == 0 else 1 - info[0]
        start = pl.multiple_of(side * span + offset, 128)
        for index in range(BLOCKS):
            place = (index % 4) * 4 + index // 4
            row = pl.multiple_of(info[1 + half * BLOCKS + place] * ROWS_OF, 16)
            target[pl.ds(row, ROWS_OF), pl.ds(start, width)] = blocks[index]


def qkv_kernel(info, x_ref, a, b, c, d, out_ref, weight):
    member = info[0]
    for which in range(3):
        for place in range(2 * BLOCKS):
            side = member if place < BLOCKS else 1 - member
            row = pl.multiple_of(info[1 + place] * ROWS_OF, 16)
            column = pl.multiple_of(side * HALF, 128)
            weight[which, pl.ds(row, ROWS_OF), pl.ds(column, HALF)] = (a, b, c, d)[place // 8][
                place % 8, which
            ]
        out_ref[:, which * D : (which + 1) * D] = dot(x_ref[...], weight[which]).astype(LOW)


def lane_mask(rows, which):
    lanes = lax.broadcasted_iota(jnp.int32, (rows, 128), 1)
    return (lanes < HEAD) if which == 0 else (lanes >= HEAD)


def attend_kernel(start, count, qkv_ref, seg_row_ref, out_ref):
    seg_row = seg_row_ref[...]
    zero = jnp.float32(0)
    one = jnp.asarray(1, LOW)
    edge = seg_row[:, 256:512]
    diagonal = lax.broadcasted_iota(jnp.int32, (256, 256), 0) == lax.broadcasted_iota(
        jnp.int32, (256, 256), 1
    )
    edge_column = jnp.sum(jnp.where(diagonal, edge, 0), axis=1, keepdims=True)
    tiles = ((0, 256, 0, 512), (256, 256, 0, 1024), (512, 512, 256, 1024))

    @pl.loop(0, count)
    def _(pair):
        def lanes(base):
            return pl.ds(pl.multiple_of((base + start + pair) * 128, 128), 128)

        q_lanes, k_lanes, v_lanes = lanes(0), lanes(PAIRS), lanes(2 * PAIRS)
        values = qkv_ref[:, v_lanes]
        with_sum = [jnp.where(lane_mask(SEQ, which), values, one) for which in range(2)]
        for first, rows, low, high in tiles:
            if first == 256:
                bias = jnp.where(edge_column == seg_row, zero, MASKED)
            else:
                bias = jnp.where(edge == (0 if first == 0 else 1), zero, MASKED)
            queries = qkv_ref[first : first + rows, q_lanes] * jnp.asarray(SCALE, LOW)
            result = None
            for which in range(2):
                mask = lane_mask(rows, which)
                own = jnp.where(mask, queries, jnp.zeros_like(queries))
                scores = dot_last(own, qkv_ref[low:high, k_lanes])
                if first == 0:
                    scores = jnp.concatenate([scores[:, :256], scores[:, 256:] + bias], 1)
                elif first == 256:
                    scores = scores + bias
                else:
                    scores = jnp.concatenate([scores[:, :256] + bias, scores[:, 256:]], 1)
                top = jnp.max(scores, axis=-1, keepdims=True)
                weights = jnp.exp(scores - top).astype(LOW)
                context = dot(weights, with_sum[which][low:high, :])
                context = context / pltpu.roll(context, HEAD, 1)
                result = context if which == 0 else jnp.where(mask, context, result)
            out_ref[first : first + rows, pl.ds(pl.multiple_of(pair * 128, 128), 128)] = (
                result.astype(LOW)
            )


def middle_kernel(
    info, sel_ref, x_ref, ctx_a, ctx_b, ctx_c, norms_in, a, b, c, d,
    cm_ref, att_ref, ym_ref, yb_ref, u_ref, hm_ref, norms, merge, expand,
):
    contexts = (ctx_a, ctx_b, ctx_c)
    third = D // 3
    place_weights(info, (a, b, c, d), (0, HALF), merge)
    place_weights(info, (a, b, c, d), (HALF, HALF + FF_HALF), expand)
    chosen = sel_ref[...]
    x_marked = dot(chosen, x_ref[...])
    c_marked = [dot(chosen, part[...]).astype(LOW) for part in contexts]
    for index, part in enumerate(c_marked):
        cm_ref[:, index * third : (index + 1) * third] = part
    if norms_in is None:
        first = info[0] == 0
        sides = [
            [
                pieces[place // 8][place % 8, 0:16, HALF + FF_HALF :].astype(WIDE)
                for place in range(BLOCKS)
            ]
            for pieces in ((a, b), (c, d))
        ]
        summed = [[p[0:4] + p[4:8] + p[8:12] for p in side] for side in sides]
        lanes = lax.broadcasted_iota(jnp.int32, (4, D), 1)
        total = jnp.zeros((4, D), WIDE)
        for half in range(2):
            side = info[0] if half == 0 else 1 - info[0]
            for place in range(BLOCKS):
                start = (2 * info[1 + half * BLOCKS + place] + side) * 24
                wide = jnp.concatenate([summed[half][place]] * (D // NORM_COLS), 1)
                moved = pltpu.roll(wide, start, 1)
                total = jnp.where((lanes >= start) & (lanes < start + 24), moved, total)
        norms[...] = total
    else:
        norms[...] = norms_in[...]
    attended, y = first_norm(x_marked, c_marked, merge, norms)
    att_ref[...] = attended
    ym_ref[...] = y
    low = y.astype(LOW)
    yb_ref[...] = low

    @pl.loop(0, FF // 512)
    def _(part):
        columns = pl.ds(pl.multiple_of(part * 512, 512), 512)
        inner = dot(low, expand[:, columns])
        u_ref[:, columns] = inner
        hm_ref[:, columns] = gelu_tanh(inner).astype(LOW)


def first_norm(x, contexts, merge, norms):
    third = D // 3
    attended = x
    for index, part in enumerate(contexts):
        attended = attended + dot_last(part, merge[:, index * third : (index + 1) * third])
    normed, _unused = layer_norm_parts(attended)
    return attended, normed * norms[0:1, :] + norms[1:2, :]


def forward_one_kernel(
    x_ref, ctx_a, ctx_b, ctx_c, norms, merge, expand, y_ref, h_ref, low
):
    for tile in range(SEQ // 256):
        rows = slice(tile * 256, (tile + 1) * 256)
        _unused, y = first_norm(
            x_ref[rows, :].astype(WIDE),
            [part[rows, :] for part in (ctx_a, ctx_b, ctx_c)],
            merge,
            norms,
        )
        y_ref[rows, :] = y
        low[rows, :] = y.astype(LOW)

    @pl.loop(0, FF // 256)
    def _(part):
        columns = pl.ds(pl.multiple_of(part * 256, 256), 256)
        h_ref[:, columns] = gelu_tanh(dot(low[...], expand[:, columns])).astype(LOW)


def turn_kernel(info, x_ref, sel_ref, own_ref, par_ref, own_m_ref, par_m_ref):
    picks = pick_rows(info, 0, BLOCKS)
    for which, full_ref, marked_ref in (
        (info[0], own_ref, own_m_ref),
        (1 - info[0], par_ref, par_m_ref),
    ):
        full = dot_last(picks, x_ref[which]).astype(LOW)
        full_ref[...] = full
        marked_ref[...] = dot_last(full, sel_ref[which]).astype(LOW)


def pick_rows(info, first, count):
    within = lax.broadcasted_iota(jnp.int32, (ROWS_OF, D), 0)
    lanes = lax.broadcasted_iota(jnp.int32, (ROWS_OF, D), 1)
    return jnp.concatenate(
        [
            jnp.where(lanes == within + info[1 + place] * ROWS_OF, 1.0, 0.0)
            for place in range(first, first + count)
        ],
        0,
    ).astype(LOW)


def marked_back_kernel(
    info, sel_ref, cot_ref, cot_b, norms, y_ref, yb_ref, h_ref, u_ref, att_ref, merge, expand,
    e, f, g, h, last_a, last_b,
    yd_ref, da_ref, dab_ref, dc_ref, ng_ref, reduce_w, du,
):
    width = e.shape[2]
    place_weights(info, (e, f, g, h), (0, width), reduce_w, FF_HALF)
    if last_a is not None:
        place_last(info, (last_a, last_b), reduce_w, FF_HALF, width)
    first = info[0] == 0
    half = SEQ // 2
    chosen = sel_ref[...]
    cot_own = cot_ref[info[0]]
    cot_low = jnp.where(first, cot_own, cot_b[...])
    cot_high = jnp.where(first, cot_b[...], cot_own)
    grad = dot(chosen[:, :half], cot_low) + dot(chosen[:, half:], cot_high)
    joined = y_ref[...] + dot_last(h_ref[...], reduce_w[...])
    normed, inverse = layer_norm_parts(joined)
    back = norm_back(normed, inverse, norms[2:3, :], grad)
    low = back.astype(LOW)
    yd_ref[:MARKED] = yb_ref[...]
    yd_ref[MARKED:] = low
    ng_ref[2:3, :] = jnp.sum(grad * normed, axis=0, keepdims=True)
    ng_ref[3:4, :] = jnp.sum(grad, axis=0, keepdims=True)
    for step in range(FF // 512):
        columns = slice(step * 512, (step + 1) * 512)
        du[:, columns] = (
            dot(low, reduce_w[:, columns]) * gelu_slope(u_ref[:, columns])
        ).astype(LOW)
    grad_y = back + dot_last(du[...], expand[...])
    normed_one, inverse_one = layer_norm_parts(att_ref[...])
    grad_a = norm_back(normed_one, inverse_one, norms[0:1, :], grad_y)
    da_ref[...] = grad_a
    grad_low = grad_a.astype(LOW)
    dab_ref[...] = grad_low
    ng_ref[0:1, :] = jnp.sum(grad_y * normed_one, axis=0, keepdims=True)
    ng_ref[1:2, :] = jnp.sum(grad_y, axis=0, keepdims=True)
    dc_ref[...] = dot(grad_low, merge[...]).astype(LOW)


def half_back_kernel(
    other, info, sel_ref, qkv_ref, dc_ref, seg_row_ref, dq_ref, dkv_ref
):
    half = 1 - info[0] if other else info[0]
    mask = lane_mask(MARKED, 0)
    seg_row = seg_row_ref[...].astype(WIDE)
    mark_segs = jnp.sum(sel_ref[...].astype(WIDE) * seg_row, axis=1, keepdims=True)
    same = jnp.concatenate([mark_segs, mark_segs], 0) == seg_row
    for pair in range(PAIRS // 2):
        first = half * (PAIRS // 2) + pair

        def lanes(base):
            return pl.ds(pl.multiple_of((base + first) * 128, 128), 128)

        out = slice(pair * 128, (pair + 1) * 128)
        queries = dot(sel_ref[...], qkv_ref[:, lanes(0)]).astype(LOW)
        keys, values = qkv_ref[:, lanes(PAIRS)], qkv_ref[:, lanes(2 * PAIRS)]
        grads = dc_ref[:, lanes(0)]
        none = jnp.zeros_like(queries)
        query_both = jnp.concatenate(
            [jnp.where(mask, queries, none), jnp.where(mask, none, queries)], 0
        )
        grad_both = jnp.concatenate(
            [jnp.where(mask, grads, none), jnp.where(mask, none, grads)], 0
        )
        scores = dot_last(query_both * jnp.asarray(SCALE, LOW), keys)
        scores = jnp.where(same, scores, MASKED)
        top = jnp.max(scores, axis=-1, keepdims=True)
        exped = jnp.exp(scores - top)
        probs = exped * (1.0 / jnp.sum(exped, axis=-1, keepdims=True))
        grad_probs = dot_last(grad_both, values)
        delta = jnp.sum(probs * grad_probs, axis=-1, keepdims=True)
        grad_scores = (probs * (grad_probs - delta)).astype(LOW)
        dq_both = dot(grad_scores, keys) * SCALE
        dq_ref[:, out] = jnp.where(mask, dq_both[:MARKED], dq_both[MARKED:]).astype(LOW)
        dkv_ref[:, out] = (dot_first(grad_scores, query_both) * SCALE).astype(LOW)
        dkv_ref[:, HALF + pair * 128 : HALF + (pair + 1) * 128] = dot_first(
            probs.astype(LOW), grad_both
        ).astype(LOW)


def heads_grad_kernel(
    info, xt_a, xt_b, dkv_a, dkv_b, xm_a, xm_b, dq_a, dq_b,
    dab_a, dab_b, cm_a, cm_b, ng_a, ng_b, keep_ref, give_ref, small,
):
    norm_grads = ng_a[...] + ng_b[...]
    for block in range(BLOCKS):
        sides = [
            norm_grads[:, (2 * block + side) * 24 : (2 * block + side + 1) * 24]
            for side in range(2)
        ]
        part = jnp.where(info[0] == 0, sides[0], sides[1])
        part = jnp.concatenate([part, jnp.zeros((4, NORM_COLS - 24), WIDE)], 1)
        part = jnp.concatenate([part, jnp.zeros((ROWS_OF - 4, NORM_COLS), WIDE)], 0)
        small[block] = part.astype(LOW)
    tall = 8 * ROWS_OF
    own = pl.ds(pl.multiple_of(info[0] * HALF, 128), HALF)
    for half, out_ref in ((1, give_ref), (0, keep_ref)):
        rows = slice(half * tall, (half + 1) * tall)

        def put(kind, value):
            out_ref[:, :, kind * HALF : (kind + 1) * HALF] = value.astype(LOW).reshape(
                8, ROWS_OF, HALF
            )

        both = dot(xt_a[rows, :], dkv_a[...]) + dot(xt_b[rows, :], dkv_b[...])
        put(1, both[:, :HALF])
        put(2, both[:, HALF:])
        put(0, dot(xm_a[rows, :], dq_a[...]) + dot(xm_b[rows, :], dq_b[...]))
        picks = pick_rows(info, 8 * half, 8)
        put(
            3,
            dot(dot_last(picks, dab_a[...]).astype(LOW), cm_a[:, own])
            + dot(dot_last(picks, dab_b[...]).astype(LOW), cm_b[:, own]),
        )
        for place in range(8):
            out_ref[place, :, 4 * HALF :] = small[info[1 + 8 * half + place]]


def ffn_grad_kernel(
    info, part_a, part_b, expand, reduce_w,
    keep_ref, give_ref, block, yb, db, yb_turned, db_turned,
):
    for side, part in enumerate((part_a, part_b)):
        for index in range(4):
            rows = slice((4 * side + index) * MARKED, (4 * side + index + 1) * MARKED)
            yb[rows, :] = part[index, :MARKED, :]
            db[rows, :] = part[index, MARKED:, :]
    wide = 4 * ROWS_OF
    start = info[2 * BLOCKS + 1] * wide
    picks = jnp.where(
        lax.broadcasted_iota(jnp.int32, (wide, D), 1)
        == lax.broadcasted_iota(jnp.int32, (wide, D), 0) + start,
        1.0,
        0.0,
    ).astype(LOW)
    yb_turned[...] = dot_last(picks, yb[...]).astype(LOW)
    db_turned[...] = dot_last(picks, db[...]).astype(LOW)

    @pl.loop(0, FF_HALF // 256)
    def _(step):
        columns = pl.ds(pl.multiple_of(step * 256, 256), 256)
        later = pl.ds(pl.multiple_of(FF_HALF + step * 256, 256), 256)
        own = pl.ds(pl.multiple_of(info[0] * FF_HALF + step * 256, 256), 256)
        inner = dot(yb[...], expand[:, own])
        hidden = gelu_tanh(inner).astype(LOW)
        back = (dot(db[...], reduce_w[:, own]) * gelu_slope(inner)).astype(LOW)
        block[:, columns] = dot(yb_turned[...], back).astype(LOW)
        block[:, later] = dot(db_turned[...], hidden).astype(LOW)

    for place in range(4):
        row = pl.multiple_of(lax.rem(info[1 + 4 * place], 4) * ROWS_OF, 16)
        (keep_ref, give_ref)[place // 2][place % 2] = block[pl.ds(row, ROWS_OF), :]


def input_grad_kernel(
    info, own_ref, par_ref, sel_ref, da_ref, dq_own, dq_par, weight,
    give_ref, keep_ref,
):
    member = info[0]

    def ordered(own, par):
        first = member == 0
        return jnp.concatenate([jnp.where(first, own, par), jnp.where(first, par, own)], 1)

    extra = da_ref[...] + dot_last(ordered(dq_own[...], dq_par[...]), weight[0])
    high = extra.astype(LOW)
    low = (extra - high.astype(WIDE)).astype(LOW)
    for tile in range(4):
        rows = token_rows(member, tile)
        chosen = sel_ref[:, rows]
        hand_out(
            dot_last(ordered(own_ref[rows, :HALF], par_ref[rows, :HALF]), weight[1])
            + dot_last(ordered(own_ref[rows, HALF:], par_ref[rows, HALF:]), weight[2])
            + dot_first(chosen, high)
            + dot_first(chosen, low),
            tile,
            give_ref,
            keep_ref,
        )


def token_rows(member, tile):
    half = 1 - member if tile < 2 else member
    return pl.ds(pl.multiple_of(half * 512 + (tile % 2) * 256, 256), 256)


def forward_two_kernel(info, y_ref, h_ref, norms, reduce_w, give_ref, keep_ref):
    for tile in range(4):
        rows = token_rows(info[0], tile)
        joined = y_ref[rows, :] + dot_last(h_ref[rows, :], reduce_w[...])
        normed, _unused = layer_norm_parts(joined)
        hand_out(normed * norms[2:3, :] + norms[3:4, :], tile, give_ref, keep_ref)


def hand_out(result, tile, give_ref, keep_ref):
    rows = slice((tile % 2) * 256, (tile % 2 + 1) * 256)
    out_ref = give_ref if tile < 2 else keep_ref
    out_ref[rows, :] = result.astype(out_ref.dtype)


def place_kernel(info, keep_ref, came_ref, out_ref, token_ref):
    token_ref[...] = jnp.zeros((8, 128), WIDE)
    out_ref[info[0]] = keep_ref[...]
    out_ref[1 - info[0]] = came_ref[...].astype(out_ref.dtype)


def join_kernel(count, *refs):
    parts, out_ref = refs[:count], refs[-1]
    start = 0
    for part in parts:
        size = part.shape[0]
        out_ref[start : start + size] = part[...]
        start += size


def fold_kernel(keep, a_ref, b_ref, *outs):
    outs[0][...] = (a_ref[:keep].astype(WIDE) + b_ref[:keep].astype(WIDE)).astype(outs[0].dtype)
    sent = outs[1:]
    size = (a_ref.shape[0] - keep) // len(sent)
    for index, out in enumerate(sent):
        rows = slice(keep + index * size, keep + (index + 1) * size)
        out[...] = (a_ref[rows].astype(WIDE) + b_ref[rows].astype(WIDE)).astype(LOW)


def lamb_step(corr, refs, gradient, decay):
    weight_ref, first_ref, second_ref, grad_ref, next_first_ref, next_second_ref, u_ref = refs
    weight = weight_ref[...]
    grad_ref[...] = gradient
    first, second, update = moments(
        weight, gradient, first_ref[...], second_ref[...], decay, corr[0], corr[1]
    )
    next_first_ref[...] = first
    next_second_ref[...] = second
    u_ref[...] = update
    return weight * weight, update * update


def put_sums(sums_ref, entries):
    lanes = lax.broadcasted_iota(jnp.int32, (8, 128), 1)
    rows = lax.broadcasted_iota(jnp.int32, (8, 128), 0)
    total = jnp.zeros((8, 128), WIDE)
    for lane, (weight_square, update_square) in entries:
        for row, value in enumerate((weight_square, update_square)):
            total = total + jnp.where((lanes == lane) & (rows == row), jnp.sum(value), 0.0)
    sums_ref[...] = total


def lamb_ffn_kernel(corr, keep_ref, came_ref, other_sums, *refs):
    expand, reduce_refs, sums_ref = refs[0:3] + refs[6:10], refs[3:6] + refs[10:14], refs[14]
    summed = keep_ref[0].astype(WIDE) + came_ref[0].astype(WIDE)
    put_sums(
        sums_ref,
        [
            (4, lamb_step(corr, expand, summed[:, :FF_HALF], DECAY)),
            (5, lamb_step(corr, reduce_refs, summed[:, FF_HALF:], DECAY)),
        ],
    )
    sums_ref[...] += other_sums[...]


def lamb_rest_kernel(corr, keep_ref, came_a, came_b, came_c, *refs):
    heads, merge, norm = refs[0:3] + refs[9:13], refs[3:6] + refs[13:17], refs[6:9] + refs[17:21]
    sums_ref = refs[21]
    summed = (
        keep_ref[0].astype(WIDE)
        + came_a[0].astype(WIDE)
        + came_b[0].astype(WIDE)
        + came_c[0].astype(WIDE)
    )
    norm_width = norm[0].shape[1]
    heads_grad = jnp.stack([summed[:, k * HALF : (k + 1) * HALF] for k in range(3)], 0)
    squares_w, squares_u = lamb_step(corr, heads, heads_grad, DECAY)
    entries = [(k, (squares_w[k], squares_u[k])) for k in range(3)]
    merge_grad = summed[:, 3 * HALF : 4 * HALF]
    entries.append((3, lamb_step(corr, merge, merge_grad, DECAY)))
    norm_grad = summed[:4, 4 * HALF : 4 * HALF + norm_width]
    squares_w, squares_u = lamb_step(corr, norm, norm_grad, 0.0)
    entries += [(6 + k, (squares_w[k : k + 1], squares_u[k : k + 1])) for k in range(4)]
    put_sums(sums_ref, entries)


def lamb_end_kernel(sums_ref, *refs):
    sums = sums_ref[...]
    ratios = jnp.sqrt(sums[0:1, :]) / jnp.sqrt(sums[1:2, :] + 1e-12)
    refs[15][...] = ratios
    weights, updates, outs = refs[0:5], refs[5:10], refs[10:15]

    def moved(index, part, ratio):
        return weights[index][part] - RATE * ratio * updates[index][part]

    for k in range(3):
        outs[0][k] = moved(0, k, ratios[:, k : k + 1])
    for index in range(1, 4):
        outs[index][...] = moved(index, Ellipsis, ratios[:, 2 + index : 3 + index])
    for k in range(4):
        outs[4][k : k + 1] = moved(4, slice(k, k + 1), ratios[:, 6 + k : 7 + k])


ANY = pl.BlockSpec(memory_space=pl.ANY)
SMEM = pl.BlockSpec(memory_space=pltpu.SMEM)
VMEM = pl.BlockSpec(memory_space=pltpu.VMEM)


def shape(dims, kind):
    return jax.ShapeDtypeStruct(dims, kind)


def params(mib):
    return pltpu.CompilerParams(vmem_limit_bytes=mib * MIB)


def cost(flops, moved, hard=0):
    return pl.CostEstimate(
        flops=int(flops) // 50, bytes_accessed=int(moved) // 50, transcendentals=int(hard) // 50
    )


def whole(dims):
    return pl.BlockSpec(dims, lambda *_: (0,) * len(dims))


def near(dims, kind):
    return pltpu.VMEM(dims, kind)


def held(*arrays):
    return [pltpu.with_memory_space_constraint(array, pltpu.VMEM) for array in arrays]


def call(kernel, name, ins, specs, out_shape, out_specs, deps=(), **options):
    count, extra = len(ins), len(deps)

    def body(*refs):
        kernel(*refs[:count], *refs[count + extra :])

    return pl.pallas_call(
        body,
        in_specs=list(specs) + [ANY] * extra,
        out_specs=out_specs,
        out_shape=out_shape,
        name=name,
        **options,
    )(*ins, *deps)


def call_join(parts, deps=(), work=0):
    count = len(parts)
    rows = sum(part.shape[0] for part in parts)
    return call(
        functools.partial(join_kernel, count),
        "join",
        held(*parts),
        [VMEM] * count,
        near((rows,) + parts[0].shape[1:], parts[0].dtype),
        VMEM,
        deps,
        compiler_params=params(SCOPED),
        cost_estimate=cost(work, 4 * rows * parts[0][0].size),
    )


def call_fold(keep, left, right, sends=1, deps=()):
    block = left.shape[1:]
    size = (left.shape[0] - keep) // sends
    return call(
        functools.partial(fold_kernel, keep),
        "fold",
        [left, right],
        [VMEM] * 2,
        [shape((keep,) + block, LOW)] + [shape((size,) + block, LOW)] * sends,
        [VMEM] * (1 + sends),
        deps,
        compiler_params=params(SCOPED),
        cost_estimate=cost(left.size, 4 * left.size),
    )


def call_qkv(info, x, first, deps=()):
    return call(
        qkv_kernel,
        "project",
        [info, x, *held(*first)],
        [SMEM] + [VMEM] * 5,
        [near((SEQ, 3 * D), LOW), near((3, D, D), LOW)],
        [VMEM] * 2,
        deps,
        compiler_params=params(SCOPED),
        cost_estimate=cost(2 * SEQ * D * 3 * D, 10e6),
    )


def call_attend(qkv, seg_row, start, count, deps=()):
    return call(
        functools.partial(attend_kernel, start, count),
        "attend",
        [*held(qkv), seg_row],
        [VMEM] * 2,
        near((SEQ, 128 * count), LOW),
        VMEM,
        deps,
        compiler_params=params(SCOPED),
        cost_estimate=cost(3 * SEQ * SEQ * 128 * 2 * count, 1e6 * count, 1.5e6 * count),
    )


def call_middle(info, sel, x, contexts, norms, second, deps=()):
    ins = [info, sel, x, *held(*contexts)]
    specs = [SMEM] + [VMEM] * 5
    if norms is None:

        def kernel(*refs):
            middle_kernel(*refs[:6], None, *refs[6:])

    else:
        kernel = middle_kernel
        ins.append(norms)
        specs.append(VMEM)
    return call(
        kernel,
        "middle",
        ins + held(*second),
        specs + [VMEM] * 4,
        [
            near((MARKED, D), LOW),
            near((MARKED, D), WIDE),
            near((MARKED, D), WIDE),
            near((MARKED, D), LOW),
            near((MARKED, FF), WIDE),
            near((MARKED, FF), LOW),
            near((4, D), WIDE),
            near((D, D), LOW),
            near((D, FF), LOW),
        ],
        [VMEM] * 9,
        deps,
        compiler_params=params(SCOPED),
        cost_estimate=cost(1.5e9, 10e6, MARKED * FF),
    )


def call_forward_one(x, contexts, norms, merge, expand, deps=()):
    return call(
        forward_one_kernel,
        "forward_one",
        [x, *held(*contexts, norms, merge, expand)],
        [VMEM] * 7,
        [near((SEQ, D), WIDE), near((SEQ, FF), LOW)],
        [VMEM] * 2,
        deps,
        scratch_shapes=[pltpu.VMEM((SEQ, D), LOW)],
        compiler_params=params(SCOPED),
        cost_estimate=cost(2 * SEQ * D * (D + FF), 22e6, SEQ * FF),
    )


def call_turn(info, x_both, sel_both, deps=()):
    return call(
        turn_kernel,
        "turn",
        [info, x_both, sel_both],
        [SMEM] + [VMEM] * 2,
        [near((D, SEQ), LOW)] * 2 + [near((D, MARKED), LOW)] * 2,
        [VMEM] * 4,
        deps,
        compiler_params=params(SCOPED),
        cost_estimate=cost(4 * SEQ * D * D, 6e6),
    )


def call_marked_back(info, sel, cotangent, cot_other, resident, third, last=(), deps=()):
    front = 12 + len(third)

    def kernel(*refs):
        more = (None, None) if not last else ()
        marked_back_kernel(*refs[:front], *more, *refs[front:])

    return call(
        kernel,
        "marked_back",
        [info, sel, cotangent, cot_other, *held(*resident, *third, *last)],
        [SMEM] + [VMEM] * (11 + len(third) + len(last)),
        [
            near((2 * MARKED, D), LOW),
            near((MARKED, D), WIDE),
            near((MARKED, D), LOW),
            near((MARKED, D), LOW),
            near((4, D), WIDE),
            near((D, FF), LOW),
        ],
        [VMEM] * 6,
        deps,
        scratch_shapes=[pltpu.VMEM((MARKED, FF), LOW)],
        compiler_params=params(SCOPED),
        cost_estimate=cost(2.5e9, 15e6),
    )


def call_half_back(other, info, sel, qkv, grad_context, seg_row, deps=(), work=3e9):
    return call(
        functools.partial(half_back_kernel, other),
        "half_back",
        [info, sel, *held(qkv, grad_context), seg_row],
        [SMEM] + [VMEM] * 4,
        [near((MARKED, HALF), LOW), near((SEQ, D), LOW)],
        [VMEM] * 2,
        deps,
        compiler_params=params(SCOPED),
        cost_estimate=cost(work, 6e6, 0.5e6),
    )


def call_heads_grad(info, x_turned, grad_kv, xm_turned, grad_q, dab, cm, ng, deps=()):
    width = 4 * HALF + NORM_COLS
    ins = held(*x_turned, *grad_kv, *xm_turned, *grad_q, *dab, *cm, *ng)
    return call(
        heads_grad_kernel,
        "heads_grad",
        [info, *ins],
        [SMEM] + [VMEM] * len(ins),
        [near((8, ROWS_OF, width), LOW)] * 2,
        [VMEM] * 2,
        deps,
        scratch_shapes=[pltpu.VMEM((BLOCKS, ROWS_OF, NORM_COLS), LOW)],
        compiler_params=params(SCOPED),
        cost_estimate=cost(4 * SEQ * D * D, 10e6),
    )


def call_ffn_grad(info, shared, expand, reduce_w, deps=()):
    tokens = 8 * MARKED
    wide = 4 * ROWS_OF
    return call(
        ffn_grad_kernel,
        "ffn_grad",
        [info, *held(*shared, expand, reduce_w)],
        [SMEM] + [VMEM] * 4,
        [near((2, ROWS_OF, FF), LOW)] * 2,
        [VMEM] * 2,
        deps,
        scratch_shapes=[
            pltpu.VMEM((wide, FF), LOW),
            pltpu.VMEM((tokens, D), LOW),
            pltpu.VMEM((tokens, D), LOW),
            pltpu.VMEM((wide, tokens), LOW),
            pltpu.VMEM((wide, tokens), LOW),
        ],
        compiler_params=params(SCOPED),
        cost_estimate=cost(5e9, 10e6),
    )


def call_place(info, keep, came, deps=()):
    return call(
        place_kernel,
        "place",
        [info, keep, came],
        [SMEM] + [VMEM] * 2,
        [pltpu.HBM((2,) + keep.shape, keep.dtype), near((8, 128), WIDE)],
        [VMEM] * 2,
        deps,
        compiler_params=params(SCOPED),
        cost_estimate=cost(1e6, 3e6),
    )


def call_input_grad(info, grad_kv, sel, grad_a, grad_q, weight, deps=()):
    return call(
        input_grad_kernel,
        "input_grad",
        [info, *held(*grad_kv), sel, *held(grad_a, *grad_q, weight)],
        [SMEM] + [VMEM] * 7,
        [shape((SEQ // 2, D), LOW), shape((SEQ // 2, D), WIDE)],
        [VMEM] * 2,
        deps,
        compiler_params=params(SCOPED),
        cost_estimate=cost(2 * SEQ * D * 2 * D, 10e6),
    )


def call_forward_two(info, y, hidden, norms, reduce_w, deps=()):
    return call(
        forward_two_kernel,
        "forward_two",
        [info, *held(y, hidden, norms, reduce_w)],
        [SMEM] + [VMEM] * 4,
        [shape((SEQ // 2, D), LOW)] * 2,
        [VMEM] * 2,
        deps,
        compiler_params=params(SCOPED),
        cost_estimate=cost(2 * SEQ * D * FF, 16e6),
    )


def like(arrays):
    return [shape(array.shape, WIDE) for array in arrays]


def call_lamb_ffn(corr, keep, came, sums, expand, reduce_w, deps=()):
    ins = [corr, keep, came, sums, *expand, *reduce_w]
    return call(
        lamb_ffn_kernel,
        "lamb_ffn",
        ins,
        [SMEM] + [VMEM] * (len(ins) - 1),
        like([expand[0]] * 4 + [reduce_w[0]] * 4) + [shape((8, 128), WIDE)],
        [VMEM] * 9,
        deps,
        compiler_params=params(SCOPED),
        cost_estimate=cost(3e6, 8e6),
    )


def call_lamb_rest(corr, keep, came, heads, merge, norm, deps):
    ins = [corr, keep, *came, *heads, *merge, *norm]
    return call(
        lamb_rest_kernel,
        "lamb_rest",
        ins,
        [SMEM] + [VMEM] * (len(ins) - 1),
        like([heads[0]] * 4 + [merge[0]] * 4 + [norm[0]] * 4) + [shape((8, 128), WIDE)],
        [VMEM] * 13,
        deps,
        compiler_params=params(SCOPED),
        cost_estimate=cost(LONG, 8e6),
    )


def call_lamb_end(sums, weights, updates, deps):
    return call(
        lamb_end_kernel,
        "lamb_end",
        [sums, *weights, *updates],
        [VMEM] * 11,
        like(weights) + [shape((1, 128), WIDE)],
        [VMEM] * 6,
        deps,
        compiler_params=params(SCOPED),
        cost_estimate=cost(1e6, 4e6),
    )


class Grid:
    def __init__(self, depth, rows, columns):
        self.depth, self.rows, self.columns = depth, rows, columns
        self.chips = depth * rows * columns

    def chip(self, z, y, x):
        return (z * self.rows + y) * self.columns + x

    def perm(self, where):
        pairs = []
        for z in range(self.depth):
            for y in range(self.rows):
                for x in range(self.columns):
                    for t in range(2):
                        z2, y2, x2, t2 = where(z, y, x, t)
                        pairs.append(
                            (self.chip(z, y, x) * 2 + t, self.chip(z2, y2, x2) * 2 + t2)
                        )
        return pairs

    def send(self, value, where):
        return lax.ppermute(value, ALL, self.perm(where))

    def along_z(self, value, step):
        return self.send(value, lambda z, y, x, t: (z ^ step, y, x, t))

    def inner(self, value):
        return self.send(value, lambda z, y, x, t: (z, y ^ (1 - t), x ^ t, t))

    def outer(self, value):
        return self.send(value, lambda z, y, x, t: (z, y ^ t, x ^ (1 - t), t))

    def column(self, value):
        return [value] + [self.along_z(value, step) for step in range(1, self.depth)]


def after(value, *deps):
    return lax.optimization_barrier((value, *deps))[0]


def other_core(value):
    return lax.ppermute(value, "tensor", [(0, 1), (1, 0)])


def shards(
    fast,
    inputs,
    segments,
    token_marks,
    cotangent,
    heads_weight,
    merge_weight,
    expand_weight,
    reduce_weight,
    norm_params,
    first_heads,
    first_merge,
    first_expand,
    first_reduce,
    first_norm,
    second_heads,
    second_merge,
    second_expand,
    second_reduce,
    second_norm,
    step_count,
):
    member = lax.axis_index("tensor")
    here = lax.axis_index("dp")
    grid = Grid(4, 2, 2)
    norm_width = norm_params.shape[1]

    if fast:
        z, y, x = here // 4, (here // 2) % 2, here % 2

        def places(core):
            place = jnp.arange(BLOCKS, dtype=jnp.int32)
            far, near, deep = place // 8, (place // 4) % 2, place % 4
            y_place = jnp.where(core == 0, near, far)
            x_place = jnp.where(core == 0, far, near)
            return (z ^ deep) * 4 + (y ^ y_place) * 2 + (x ^ x_place)

        info = jnp.concatenate([member[None], places(member), places(1 - member), z[None]])
    else:
        order = jnp.arange(BLOCKS, dtype=jnp.int32)
        info = jnp.concatenate([member[None], order, order])
    info = info.astype(jnp.int32)

    first_part = heads_weight.astype(LOW)
    merge_turned = merge_weight.astype(LOW).T
    second_list = [merge_turned, expand_weight.astype(LOW)]
    if fast:
        top = norm_params.astype(LOW)
        rest = norm_params - top.astype(WIDE)
        middle = rest.astype(LOW)
        last = (rest - middle.astype(WIDE)).astype(LOW)
        packed = jnp.concatenate([top, middle, last], 0)
        second_list.append(
            jnp.pad(packed, ((0, ROWS_OF - 12), (0, NORM_COLS - norm_width)))
        )
    second_part = jnp.concatenate(second_list, 1)
    third_part = reduce_weight.astype(LOW).T

    def row_of(array, which):
        return lax.dynamic_index_in_dim(array, which, 0, keepdims=False)

    x_row = row_of(inputs, member)
    segment = row_of(segments, member)
    rank = jnp.cumsum(token_marks, axis=1) - 1
    sel_both = (
        (rank[:, None, :] == jnp.arange(MARKED, dtype=jnp.int32)[None, :, None])
        & (token_marks[:, None, :] == 1)
    ).astype(LOW)
    sel = row_of(sel_both, member)
    seg_row = segment[None, :]
    cot_other = other_core(row_of(cotangent, 1 - member))
    steps_float = step_count.astype(WIDE)
    corr_one = 1.0 - BETA_ONE**steps_float
    corr_two = 1.0 - BETA_TWO**steps_float
    corr = jnp.stack([corr_one, corr_two])

    if fast:
        second_part, third_part = second_part[None], third_part[None]
        last_part, third_part = third_part[:, :, WIDTH_C:], third_part[:, :, :WIDTH_C]
        last_near = grid.inner(last_part)
        four_a = call_join(
            grid.column(first_part[None]),
            [second_part, sel_both, corr, cot_other, info, last_near],
        )
        two_last = call_join([last_part, last_near], [four_a])
        last_far = grid.outer(two_last)
        near_a = grid.inner(four_a)
        second_b = grid.along_z(after(second_part, four_a), 2)
        turned = call_turn(info, inputs, sel_both, [four_a])
        eight_a = call_join([four_a, near_a], [second_b, *turned, last_far])
        four_last = call_join([two_last, last_far], [eight_a])
        far_a = grid.outer(eight_a)
        cross_a = other_core(eight_a)
        late = after(second_part, eight_a)
        four_b = call_join(
            [second_part, grid.along_z(late, 1), second_b, grid.along_z(late, 3)],
            [cross_a, third_part, last_part, x_row, seg_row],
        )
        far_a, four_b = lax.optimization_barrier((far_a, four_b))
        first_w = (eight_a, far_a, cross_a, other_core(far_a))
        near_b = grid.inner(four_b)
        second_c = grid.along_z(after(third_part, four_b), 2)
        qkv, heads_full = call_qkv(info, x_row, first_w, [four_b])
        eight_b = call_join([four_b, near_b], [qkv, second_c])
        far_b = grid.outer(eight_b)
        cross_b = other_core(eight_b)
        late = after(third_part, eight_b)
        column_c = [third_part, grid.along_z(late, 1), second_c, grid.along_z(late, 3)]
        context_a = call_attend(qkv, seg_row, 0, 2, [eight_b])
        four_c = call_join(column_c, [context_a, cross_b])
        near_c = grid.inner(four_c)
        second_last = grid.along_z(after(four_last, four_c), 2)
        context_b = call_attend(qkv, seg_row, 2, 2, [four_c])
        eight_c = call_join([four_c, near_c], [context_b, second_last])
        second_w = (eight_b, far_b, cross_b, other_core(after(far_b, eight_c)))
        late = after(four_last, eight_c)
        column_last = [four_last, grid.along_z(late, 1), second_last, grid.along_z(late, 3)]
        far_c = grid.outer(eight_c)
        cross_c = other_core(eight_c)
        context_c = call_attend(qkv, seg_row, 4, 2, [eight_c])
    else:

        def pieces(part):
            full = lax.all_gather(part, "dp", axis=part.ndim - 2, tiled=True)
            if part.ndim == 3:
                blocks = full.reshape(3, BLOCKS, ROWS_OF, HALF).transpose(1, 0, 2, 3)
            else:
                blocks = full.reshape(BLOCKS, ROWS_OF, part.shape[1])
            eight, rest_eight = blocks[:8], blocks[8:]
            return eight, rest_eight, other_core(eight), other_core(rest_eight)

        first_w, second_w, third_w = pieces(first_part), pieces(second_part), pieces(third_part)
        turned = call_turn(info, inputs, sel_both)
        qkv, heads_full = call_qkv(info, x_row, first_w)
        context_a, context_b, context_c = [
            call_attend(qkv, seg_row, start, 2) for start in (0, 2, 4)
        ]

    norms = None if fast else lax.all_gather(norm_params, ALL, axis=1, tiled=True)

    contexts = (context_a, context_b, context_c)
    c_marked, attended, y_marked, yb, inner, hidden, norms, merge_full, expand_full = call_middle(
        info, sel, x_row, contexts, norms, second_w, [eight_c] if fast else []
    )
    cm_own, cm_par = c_marked, other_core(c_marked)
    if fast:
        third_w = (eight_c, far_c, cross_c, other_core(after(far_c, yb)))
        own_last = call_join(column_last, [yb])
        last_w = (own_last, other_core(own_last))
    else:
        last_w = ()
    shared, grad_a, dab, grad_context, norm_terms, reduce_full = call_marked_back(
        info, sel, cotangent, cot_other,
        (norms, y_marked, yb, hidden, inner, attended, merge_full, expand_full),
        third_w, last_w,
    )
    shared = shared[None]
    early_d = [grid.along_z(shared, step) for step in (1, 2)] if fast else [shared]
    from_other = [other_core(dab), other_core(norm_terms)]
    par_parts = call_half_back(
        True, info, sel, qkv, grad_context, seg_row
    )
    came_parts = [other_core(part) for part in par_parts]
    own_parts = call_half_back(
        False, info, sel, qkv, grad_context, seg_row, par_parts[:1]
    )
    own_q = call_join(own_parts[:1], early_d, LONG)
    keep, give = call_heads_grad(
        info,
        turned[:2],
        (own_parts[1], came_parts[1]),
        turned[2:],
        (own_q, came_parts[0]),
        (dab, from_other[0]),
        (cm_own, cm_par),
        (norm_terms, from_other[1]),
    )
    grad_q, grad_kv = zip(own_parts, par_parts)

    weights = (heads_weight, merge_weight, expand_weight, reduce_weight, norm_params)
    firsts = (first_heads, first_merge, first_expand, first_reduce, first_norm)
    seconds = (second_heads, second_merge, second_expand, second_reduce, second_norm)
    if fast:
        weights, firsts, seconds = [
            tuple(v.T if index in (1, 3) else v for index, v in enumerate(values))
            for values in (weights, firsts, seconds)
        ]
        tensors = list(zip(weights, firsts, seconds))
        far = grid.outer(give)
        late = after(shared, give)
        column_d = [shared, *early_d, grid.along_z(late, 3)]
        input_give, input_keep = call_input_grad(
            info, grad_kv, sel, grad_a, grad_q, heads_full, [give]
        )
        input_came = other_core(input_give)
        y_row, hidden_row = call_forward_one(
            x_row, contexts, norms, merge_full, expand_full, [input_give]
        )
        keep, give = call_fold(4, keep, far, deps=[y_row])
        near_heads = grid.inner(give)
        shared_four = call_join(column_d, [give])
        keep_ffn, give_ffn = call_ffn_grad(
            info, (shared_four, other_core(shared_four)), expand_full, reduce_full, [give]
        )
        keep, *gives = call_fold(1, keep, near_heads, 3, deps=[give_ffn])
        came = [grid.along_z(gives[step], step + 1) for step in range(3)]
        far_ffn = grid.outer(after(give_ffn, keep))
        output_give, output_keep = call_forward_two(
            info, y_row, hidden_row, norms, reduce_full, gives
        )
        output_came = other_core(output_give)
        keep_ffn, give_ffn = call_fold(1, keep_ffn, far_ffn, deps=[output_give])
        came_ffn = grid.inner(give_ffn)
        input_grad, placed = call_place(info, input_keep, input_came, [give_ffn])
        lamb_rest = call_lamb_rest(
            corr, keep, came, tensors[0], tensors[1], tensors[4], [placed]
        )
        lamb_ffn = call_lamb_ffn(
            corr, keep_ffn, came_ffn, lamb_rest[12], tensors[2], tensors[3]
        )
        both = lamb_ffn[8]
        layer_output, placed = call_place(info, output_keep, output_came, [both])
    else:
        both_cores = (shared[0], other_core(shared[0]))
        yb_all = jnp.concatenate([part[:MARKED] for part in both_cores], 0)
        db_all = jnp.concatenate([part[MARKED:] for part in both_cores], 0)
        expand_half = jnp.concatenate(second_w[:2], 0).reshape(D, -1)[:, HALF : HALF + FF_HALF]
        reduce_half = jnp.concatenate(third_w[:2], 0).reshape(D, -1)
        inner_all = dot(yb_all, expand_half)
        back_all = (dot(db_all, reduce_half) * gelu_slope(inner_all)).astype(LOW)
        hidden_all = gelu_tanh(inner_all).astype(LOW)
        part_expand = lax.psum_scatter(
            dot_first(yb_all, back_all), "dp", scatter_dimension=0, tiled=True
        )
        part_reduce = lax.psum_scatter(
            dot_first(db_all, hidden_all), "dp", scatter_dimension=0, tiled=True
        ).T
        full = jnp.concatenate([keep, give], 0).astype(WIDE).reshape(D, -1)
        summed = lax.psum_scatter(full, "dp", scatter_dimension=0, tiled=True)
        part_norm = lax.psum_scatter(norm_terms, ALL, scatter_dimension=1, tiled=True)
        input_give, input_keep = call_input_grad(
            info, grad_kv, sel, grad_a, grad_q, heads_full
        )
        y_row, hidden_row = call_forward_one(x_row, contexts, norms, merge_full, expand_full)
        output_give, output_keep = call_forward_two(info, y_row, hidden_row, norms, reduce_full)
        input_came, output_came = other_core(input_give), other_core(output_give)
        part_heads = jnp.stack([summed[:, k * HALF : (k + 1) * HALF] for k in range(3)], 0)
        part_merge = summed[:, 3 * HALF : 4 * HALF].T

    if not fast:
        layer_output, _unused = call_place(info, output_keep, output_came)
        input_grad, _unused = call_place(info, input_keep, input_came)

    if fast:
        both = both + other_core(both)
        both = (
            both
            + grid.send(both, lambda z, y, x, t: (z, y ^ 1, x, t))
            + grid.send(both, lambda z, y, x, t: (z, y, x ^ 1, t))
            + grid.send(both, lambda z, y, x, t: (z, y ^ 1, x ^ 1, t))
        )
        both = (both + grid.along_z(both, 1)) + (grid.along_z(both, 2) + grid.along_z(both, 3))
        sets = [lamb_rest[0:4], lamb_rest[4:8], lamb_ffn[0:4], lamb_ffn[4:8], lamb_rest[8:12]]
        *nexts, ratios = call_lamb_end(
            both, weights, [values[3] for values in sets], [placed]
        )
        parts, next_firsts, next_seconds = [
            [values[index] for values in sets] for index in range(3)
        ]
        parts, next_firsts, next_seconds, nexts = [
            [v.T if index in (1, 3) else v for index, v in enumerate(values)]
            for values in (parts, next_firsts, next_seconds, nexts)
        ]
        trust_ratios = ratios[0, :10]
    else:
        parts = (part_heads, part_merge, part_expand, part_reduce, part_norm)
        results = [
            moments(*values, decay, corr_one, corr_two)
            for *values, decay in zip(
                weights, parts, firsts, seconds, (DECAY, DECAY, DECAY, DECAY, 0.0)
            )
        ]
        next_firsts, next_seconds, updates = zip(*results)
        weight_total, update_total = lax.psum((squares(*weights), squares(*updates)), ALL)
        trust_ratios = jnp.sqrt(weight_total) / jnp.sqrt(update_total + 1e-12)
        ratios = (
            trust_ratios[0:3, None, None],
            trust_ratios[3],
            trust_ratios[4],
            trust_ratios[5],
            trust_ratios[6:10, None],
        )
        nexts = [
            weight - RATE * ratio * update
            for weight, ratio, update in zip(weights, ratios, updates)
        ]
    return (
        layer_output,
        input_grad,
        *parts,
        *next_firsts,
        *next_seconds,
        *nexts,
        trust_ratios,
    )


def solution(mesh):
    fast = mesh.shape["dp"] == BLOCKS and mesh.shape["tensor"] == 2
    return jax.shard_map(
        functools.partial(shards, fast),
        mesh=mesh,
        in_specs=(
            P("dp", None, None),
            P("dp", None),
            P("dp", None),
            P("dp", "tensor", None),
            P(None, "dp", "tensor"),
            P("tensor", "dp"),
            P("dp", "tensor"),
            P("tensor", "dp"),
            P(None, ("dp", "tensor")),
            P(None, "dp", "tensor"),
            P("tensor", "dp"),
            P("dp", "tensor"),
            P("tensor", "dp"),
            P(None, ("dp", "tensor")),
            P(None, "dp", "tensor"),
            P("tensor", "dp"),
            P("dp", "tensor"),
            P("tensor", "dp"),
            P(None, ("dp", "tensor")),
            P(),
        ),
        out_specs=(
            P("dp", "tensor", None),
            P("dp", "tensor", None),
            P(None, "dp", "tensor"),
            P("tensor", "dp"),
            P("dp", "tensor"),
            P("tensor", "dp"),
            P(None, ("dp", "tensor")),
            P(None, "dp", "tensor"),
            P("tensor", "dp"),
            P("dp", "tensor"),
            P("tensor", "dp"),
            P(None, ("dp", "tensor")),
            P(None, "dp", "tensor"),
            P("tensor", "dp"),
            P("dp", "tensor"),
            P("tensor", "dp"),
            P(None, ("dp", "tensor")),
            P(None, "dp", "tensor"),
            P("tensor", "dp"),
            P("dp", "tensor"),
            P("tensor", "dp"),
            P(None, ("dp", "tensor")),
            P(),
        ),
        check_vma=False,
    )
```

```python
import functools

import jax
import jax.numpy as jnp
from jax import lax
from jax.experimental import pallas as pl
from jax.experimental.pallas import tpu as pltpu
from jax.sharding import PartitionSpec as P

D = 768
HEAD = 64
SEQ = 1024
FF = 3072
HALF = D // 2
FF_HALF = FF // 2
MARKED = 80
BLOCKS = 16
ROWS_OF = D // BLOCKS
NORM_COLS = 128
PAIRS = D // 128
MIB = 1 << 20
SCOPED = 12
LONG = 3e12
WIDTH_C = 1024

NORM_EPS = 1e-12
BETA_ONE = 0.9
BETA_TWO = 0.999
ADAM_EPS = 1e-06
DECAY = 0.01
RATE = 0.25
MASKED = -1000000000.0
SCALE = HEAD ** (-0.5)
GELU_A = 0.7978845608028654
GELU_B = 0.044715
ALL = ("dp", "tensor")
LOW = jnp.bfloat16
WIDE = jnp.float32


def dot(left, right):
    return jnp.dot(left, right, preferred_element_type=WIDE)


def dot_last(left, right):
    return lax.dot_general(left, right, (((1,), (1,)), ((), ())), preferred_element_type=WIDE)


def dot_first(left, right):
    return lax.dot_general(left, right, (((0,), (0,)), ((), ())), preferred_element_type=WIDE)


def layer_norm_parts(values):
    average = jnp.mean(values, axis=-1, keepdims=True)
    centered = values - average
    spread = jnp.mean(centered * centered, axis=-1, keepdims=True)
    inverse = lax.rsqrt(spread + NORM_EPS)
    return centered * inverse, inverse


def norm_back(normed, inverse, gain, grad_out):
    scaled = grad_out * gain
    return inverse * (
        scaled
        - jnp.mean(scaled, axis=-1, keepdims=True)
        - normed * jnp.mean(scaled * normed, axis=-1, keepdims=True)
    )


def gelu_tanh(values):
    half = 0.5 * values
    return half + half * jnp.tanh(values * (GELU_A + (GELU_A * GELU_B) * (values * values)))


def gelu_slope(values):
    square = values * values
    bent = jnp.tanh(values * (GELU_A + (GELU_A * GELU_B) * square))
    return 0.5 * (1.0 + bent) + (0.5 * values) * (1.0 - bent * bent) * (
        GELU_A + (3.0 * GELU_A * GELU_B) * square
    )


def moments(weight, gradient, first, second, decay, corr_one, corr_two):
    next_first = BETA_ONE * first + (1.0 - BETA_ONE) * gradient
    next_second = BETA_TWO * second + (1.0 - BETA_TWO) * gradient * gradient
    update = next_first / corr_one / (jnp.sqrt(next_second / corr_two) + ADAM_EPS) + decay * weight
    return (next_first, next_second, update)


def squares(heads_part, merge_part, expand_part, reduce_part, norm_part):
    return jnp.concatenate(
        [
            jnp.sum(heads_part * heads_part, axis=(1, 2)),
            jnp.sum(merge_part * merge_part)[None],
            jnp.sum(expand_part * expand_part)[None],
            jnp.sum(reduce_part * reduce_part)[None],
            jnp.sum(norm_part * norm_part, axis=1),
        ]
    )


def place_weights(info, pieces, columns, target, span=None):
    member = info[0]
    width = columns[1] - columns[0]
    for place in range(2 * BLOCKS):
        row = pl.multiple_of(info[1 + place] * ROWS_OF, 16)
        side = member if place < BLOCKS else 1 - member
        start = pl.multiple_of(side * (span or width), 128)
        target[pl.ds(row, ROWS_OF), pl.ds(start, width)] = pieces[place // 8][
            place % 8, :, columns[0] : columns[1]
        ]


def place_last(info, halves, target, span, offset):
    width = span - offset
    for half, blocks in enumerate(halves):
        side = info[0] if half == 0 else 1 - info[0]
        start = pl.multiple_of(side * span + offset, 128)
        for index in range(BLOCKS):
            place = (index % 4) * 4 + index // 4
            row = pl.multiple_of(info[1 + half * BLOCKS + place] * ROWS_OF, 16)
            target[pl.ds(row, ROWS_OF), pl.ds(start, width)] = blocks[index]


def qkv_kernel(info, x_ref, a, b, c, d, out_ref, weight):
    member = info[0]
    for which in range(3):
        for place in range(2 * BLOCKS):
            side = member if place < BLOCKS else 1 - member
            row = pl.multiple_of(info[1 + place] * ROWS_OF, 16)
            column = pl.multiple_of(side * HALF, 128)
            weight[which, pl.ds(row, ROWS_OF), pl.ds(column, HALF)] = (a, b, c, d)[place // 8][
                place % 8, which
            ]
        out_ref[:, which * D : (which + 1) * D] = dot(x_ref[...], weight[which]).astype(LOW)


def lane_mask(rows, which):
    lanes = lax.broadcasted_iota(jnp.int32, (rows, 128), 1)
    return (lanes < HEAD) if which == 0 else (lanes >= HEAD)


def attend_kernel(start, count, qkv_ref, seg_row_ref, out_ref):
    seg_row = seg_row_ref[...]
    zero = jnp.float32(0)
    one = jnp.asarray(1, LOW)
    edge = seg_row[:, 256:512]
    diagonal = lax.broadcasted_iota(jnp.int32, (256, 256), 0) == lax.broadcasted_iota(
        jnp.int32, (256, 256), 1
    )
    edge_column = jnp.sum(jnp.where(diagonal, edge, 0), axis=1, keepdims=True)
    tiles = ((0, 256, 0, 512), (256, 256, 0, 1024), (512, 512, 256, 1024))

    @pl.loop(0, count)
    def _(pair):
        def lanes(base):
            return pl.ds(pl.multiple_of((base + start + pair) * 128, 128), 128)

        q_lanes, k_lanes, v_lanes = lanes(0), lanes(PAIRS), lanes(2 * PAIRS)
        values = qkv_ref[:, v_lanes]
        with_sum = [jnp.where(lane_mask(SEQ, which), values, one) for which in range(2)]
        for first, rows, low, high in tiles:
            if first == 256:
                bias = jnp.where(edge_column == seg_row, zero, MASKED)
            else:
                bias = jnp.where(edge == (0 if first == 0 else 1), zero, MASKED)
            queries = qkv_ref[first : first + rows, q_lanes] * jnp.asarray(SCALE, LOW)
            result = None
            for which in range(2):
                mask = lane_mask(rows, which)
                own = jnp.where(mask, queries, jnp.zeros_like(queries))
                scores = dot_last(own, qkv_ref[low:high, k_lanes])
                if first == 0:
                    scores = jnp.concatenate([scores[:, :256], scores[:, 256:] + bias], 1)
                elif first == 256:
                    scores = scores + bias
                else:
                    scores = jnp.concatenate([scores[:, :256] + bias, scores[:, 256:]], 1)
                top = jnp.max(scores, axis=-1, keepdims=True)
                weights = jnp.exp(scores - top).astype(LOW)
                context = dot(weights, with_sum[which][low:high, :])
                context = context / pltpu.roll(context, HEAD, 1)
                result = context if which == 0 else jnp.where(mask, context, result)
            out_ref[first : first + rows, pl.ds(pl.multiple_of(pair * 128, 128), 128)] = (
                result.astype(LOW)
            )


def middle_kernel(
    info, sel_ref, x_ref, ctx_a, ctx_b, ctx_c, norms_in, a, b, c, d,
    cm_ref, att_ref, ym_ref, yb_ref, norms, merge,
):
    contexts = (ctx_a, ctx_b, ctx_c)
    third = D // 3
    place_weights(info, (a, b, c, d), (0, HALF), merge)
    chosen = sel_ref[...]
    x_marked = dot(chosen, x_ref[...])
    c_marked = [dot(chosen, part[...]).astype(LOW) for part in contexts]
    for index, part in enumerate(c_marked):
        cm_ref[:, index * third : (index + 1) * third] = part
    if norms_in is None:
        first = info[0] == 0
        sides = [
            [
                pieces[place // 8][place % 8, 0:16, HALF + FF_HALF :].astype(WIDE)
                for place in range(BLOCKS)
            ]
            for pieces in ((a, b), (c, d))
        ]
        summed = [[p[0:4] + p[4:8] + p[8:12] for p in side] for side in sides]
        lanes = lax.broadcasted_iota(jnp.int32, (4, D), 1)
        total = jnp.zeros((4, D), WIDE)
        for half in range(2):
            side = info[0] if half == 0 else 1 - info[0]
            for place in range(BLOCKS):
                start = (2 * info[1 + half * BLOCKS + place] + side) * 24
                wide = jnp.concatenate([summed[half][place]] * (D // NORM_COLS), 1)
                moved = pltpu.roll(wide, start, 1)
                total = jnp.where((lanes >= start) & (lanes < start + 24), moved, total)
        norms[...] = total
    else:
        norms[...] = norms_in[...]
    attended, y = first_norm(x_marked, c_marked, merge, norms)
    att_ref[...] = attended
    ym_ref[...] = y
    yb_ref[...] = y.astype(LOW)


def inner_kernel(info, yb_ref, a, b, c, d, u_ref, hm_ref, expand):
    place_weights(info, (a, b, c, d), (HALF, HALF + FF_HALF), expand)
    low = yb_ref[...]

    @pl.loop(0, FF // 512)
    def _(part):
        columns = pl.ds(pl.multiple_of(part * 512, 512), 512)
        inner = dot(low, expand[:, columns])
        u_ref[:, columns] = inner
        hm_ref[:, columns] = gelu_tanh(inner).astype(LOW)


def first_norm(x, contexts, merge, norms):
    third = D // 3
    attended = x
    for index, part in enumerate(contexts):
        attended = attended + dot_last(part, merge[:, index * third : (index + 1) * third])
    normed, _unused = layer_norm_parts(attended)
    return attended, normed * norms[0:1, :] + norms[1:2, :]


def forward_one_kernel(
    x_ref, ctx_a, ctx_b, ctx_c, norms, merge, expand, y_ref, h_ref, low
):
    for tile in range(SEQ // 256):
        rows = slice(tile * 256, (tile + 1) * 256)
        _unused, y = first_norm(
            x_ref[rows, :].astype(WIDE),
            [part[rows, :] for part in (ctx_a, ctx_b, ctx_c)],
            merge,
            norms,
        )
        y_ref[rows, :] = y
        low[rows, :] = y.astype(LOW)

    @pl.loop(0, FF // 256)
    def _(part):
        columns = pl.ds(pl.multiple_of(part * 256, 256), 256)
        h_ref[:, columns] = gelu_tanh(dot(low[...], expand[:, columns])).astype(LOW)


def turn_kernel(info, x_ref, sel_ref, own_ref, par_ref, own_m_ref, par_m_ref):
    picks = pick_rows(info, 0, BLOCKS)
    for which, full_ref, marked_ref in (
        (info[0], own_ref, own_m_ref),
        (1 - info[0], par_ref, par_m_ref),
    ):
        full = dot_last(picks, x_ref[which]).astype(LOW)
        full_ref[...] = full
        marked_ref[...] = dot_last(full, sel_ref[which]).astype(LOW)


def pick_rows(info, first, count):
    within = lax.broadcasted_iota(jnp.int32, (ROWS_OF, D), 0)
    lanes = lax.broadcasted_iota(jnp.int32, (ROWS_OF, D), 1)
    return jnp.concatenate(
        [
            jnp.where(lanes == within + info[1 + place] * ROWS_OF, 1.0, 0.0)
            for place in range(first, first + count)
        ],
        0,
    ).astype(LOW)


def marked_back_kernel(
    info, sel_ref, cot_ref, cot_b, norms, y_ref, yb_ref, h_ref, u_ref, att_ref, merge, expand,
    e, f, g, h, last_a, last_b,
    yd_ref, da_ref, dab_ref, dc_ref, ng_ref, reduce_w, du,
):
    width = e.shape[2]
    place_weights(info, (e, f, g, h), (0, width), reduce_w, FF_HALF)
    if last_a is not None:
        place_last(info, (last_a, last_b), reduce_w, FF_HALF, width)
    first = info[0] == 0
    half = SEQ // 2
    chosen = sel_ref[...]
    cot_own = cot_ref[info[0]]
    cot_low = jnp.where(first, cot_own, cot_b[...])
    cot_high = jnp.where(first, cot_b[...], cot_own)
    grad = dot(chosen[:, :half], cot_low) + dot(chosen[:, half:], cot_high)
    joined = y_ref[...] + dot_last(h_ref[...], reduce_w[...])
    normed, inverse = layer_norm_parts(joined)
    back = norm_back(normed, inverse, norms[2:3, :], grad)
    low = back.astype(LOW)
    yd_ref[:MARKED] = yb_ref[...]
    yd_ref[MARKED:] = low
    ng_ref[2:3, :] = jnp.sum(grad * normed, axis=0, keepdims=True)
    ng_ref[3:4, :] = jnp.sum(grad, axis=0, keepdims=True)
    for step in range(FF // 512):
        columns = slice(step * 512, (step + 1) * 512)
        du[:, columns] = (
            dot(low, reduce_w[:, columns]) * gelu_slope(u_ref[:, columns])
        ).astype(LOW)
    grad_y = back + dot_last(du[...], expand[...])
    normed_one, inverse_one = layer_norm_parts(att_ref[...])
    grad_a = norm_back(normed_one, inverse_one, norms[0:1, :], grad_y)
    da_ref[...] = grad_a
    grad_low = grad_a.astype(LOW)
    dab_ref[...] = grad_low
    ng_ref[0:1, :] = jnp.sum(grad_y * normed_one, axis=0, keepdims=True)
    ng_ref[1:2, :] = jnp.sum(grad_y, axis=0, keepdims=True)
    dc_ref[...] = dot(grad_low, merge[...]).astype(LOW)


def half_back_kernel(
    other, info, sel_ref, qkv_ref, dc_ref, seg_row_ref, dq_ref, dkv_ref
):
    half = 1 - info[0] if other else info[0]
    mask = lane_mask(MARKED, 0)
    seg_row = seg_row_ref[...].astype(WIDE)
    mark_segs = jnp.sum(sel_ref[...].astype(WIDE) * seg_row, axis=1, keepdims=True)
    same = jnp.concatenate([mark_segs, mark_segs], 0) == seg_row
    for pair in range(PAIRS // 2):
        first = half * (PAIRS // 2) + pair

        def lanes(base):
            return pl.ds(pl.multiple_of((base + first) * 128, 128), 128)

        out = slice(pair * 128, (pair + 1) * 128)
        queries = dot(sel_ref[...], qkv_ref[:, lanes(0)]).astype(LOW)
        keys, values = qkv_ref[:, lanes(PAIRS)], qkv_ref[:, lanes(2 * PAIRS)]
        grads = dc_ref[:, lanes(0)]
        none = jnp.zeros_like(queries)
        query_both = jnp.concatenate(
            [jnp.where(mask, queries, none), jnp.where(mask, none, queries)], 0
        )
        grad_both = jnp.concatenate(
            [jnp.where(mask, grads, none), jnp.where(mask, none, grads)], 0
        )
        scores = dot_last(query_both * jnp.asarray(SCALE, LOW), keys)
        scores = jnp.where(same, scores, MASKED)
        top = jnp.max(scores, axis=-1, keepdims=True)
        exped = jnp.exp(scores - top)
        probs = exped * (1.0 / jnp.sum(exped, axis=-1, keepdims=True))
        grad_probs = dot_last(grad_both, values)
        delta = jnp.sum(probs * grad_probs, axis=-1, keepdims=True)
        grad_scores = (probs * (grad_probs - delta)).astype(LOW)
        dq_both = dot(grad_scores, keys) * SCALE
        dq_ref[:, out] = jnp.where(mask, dq_both[:MARKED], dq_both[MARKED:]).astype(LOW)
        dkv_ref[:, out] = (dot_first(grad_scores, query_both) * SCALE).astype(LOW)
        dkv_ref[:, HALF + pair * 128 : HALF + (pair + 1) * 128] = dot_first(
            probs.astype(LOW), grad_both
        ).astype(LOW)


def heads_first_kernel(
    info, xt_a, dkv_a, xm_a, dq_a, dab_a, dab_b, cm_a, cm_b, ng_a, ng_b, out_ref, small
):
    norm_grads = ng_a[...] + ng_b[...]
    for block in range(BLOCKS):
        sides = [
            norm_grads[:, (2 * block + side) * 24 : (2 * block + side + 1) * 24]
            for side in range(2)
        ]
        part = jnp.where(info[0] == 0, sides[0], sides[1])
        part = jnp.concatenate([part, jnp.zeros((4, NORM_COLS - 24), WIDE)], 1)
        small[block] = jnp.concatenate([part, jnp.zeros((ROWS_OF - 4, NORM_COLS), WIDE)], 0)
    tall = 8 * ROWS_OF
    own = pl.ds(pl.multiple_of(info[0] * HALF, 128), HALF)
    for half in range(2):
        rows = slice(half * tall, (half + 1) * tall)
        out_ref[rows, :HALF] = dot(xm_a[rows, :], dq_a[...])
        out_ref[rows, HALF : 3 * HALF] = dot(xt_a[rows, :], dkv_a[...])
        picks = pick_rows(info, 8 * half, 8)
        out_ref[rows, 3 * HALF : 4 * HALF] = dot(
            dot_last(picks, dab_a[...]).astype(LOW), cm_a[:, own]
        ) + dot(dot_last(picks, dab_b[...]).astype(LOW), cm_b[:, own])
    for place in range(BLOCKS):
        out_ref[place * ROWS_OF : (place + 1) * ROWS_OF, 4 * HALF :] = small[info[1 + place]]


def heads_second_kernel(first_ref, xt_b, dkv_b, xm_b, dq_b, keep_ref, give_ref):
    tall = 8 * ROWS_OF
    for half, out_ref in ((1, give_ref), (0, keep_ref)):
        rows = slice(half * tall, (half + 1) * tall)

        def put(columns, value):
            out_ref[:, :, columns] = value.astype(LOW).reshape(8, ROWS_OF, value.shape[1])

        put(slice(0, HALF), first_ref[rows, :HALF] + dot(xm_b[rows, :], dq_b[...]))
        put(
            slice(HALF, 3 * HALF),
            first_ref[rows, HALF : 3 * HALF] + dot(xt_b[rows, :], dkv_b[...]),
        )
        put(slice(3 * HALF, first_ref.shape[1]), first_ref[rows, 3 * HALF :])


def ffn_grad_kernel(
    info, part_a, part_b, expand, reduce_w,
    keep_ref, give_ref, block, yb, db, yb_turned, db_turned,
):
    for side, part in enumerate((part_a, part_b)):
        for index in range(4):
            rows = slice((4 * side + index) * MARKED, (4 * side + index + 1) * MARKED)
            yb[rows, :] = part[index, :MARKED, :]
            db[rows, :] = part[index, MARKED:, :]
    wide = 4 * ROWS_OF
    start = info[2 * BLOCKS + 1] * wide
    picks = jnp.where(
        lax.broadcasted_iota(jnp.int32, (wide, D), 1)
        == lax.broadcasted_iota(jnp.int32, (wide, D), 0) + start,
        1.0,
        0.0,
    ).astype(LOW)
    yb_turned[...] = dot_last(picks, yb[...]).astype(LOW)
    db_turned[...] = dot_last(picks, db[...]).astype(LOW)

    @pl.loop(0, FF_HALF // 256)
    def _(step):
        columns = pl.ds(pl.multiple_of(step * 256, 256), 256)
        later = pl.ds(pl.multiple_of(FF_HALF + step * 256, 256), 256)
        own = pl.ds(pl.multiple_of(info[0] * FF_HALF + step * 256, 256), 256)
        inner = dot(yb[...], expand[:, own])
        hidden = gelu_tanh(inner).astype(LOW)
        back = (dot(db[...], reduce_w[:, own]) * gelu_slope(inner)).astype(LOW)
        block[:, columns] = dot(yb_turned[...], back).astype(LOW)
        block[:, later] = dot(db_turned[...], hidden).astype(LOW)

    for place in range(4):
        row = pl.multiple_of(lax.rem(info[1 + 4 * place], 4) * ROWS_OF, 16)
        (keep_ref, give_ref)[place // 2][place % 2] = block[pl.ds(row, ROWS_OF), :]


def input_grad_kernel(
    info, own_ref, par_ref, sel_ref, da_ref, dq_own, dq_par, weight,
    give_ref, keep_ref,
):
    member = info[0]

    def ordered(own, par):
        first = member == 0
        return jnp.concatenate([jnp.where(first, own, par), jnp.where(first, par, own)], 1)

    extra = da_ref[...] + dot_last(ordered(dq_own[...], dq_par[...]), weight[0])
    high = extra.astype(LOW)
    low = (extra - high.astype(WIDE)).astype(LOW)
    for tile in range(4):
        rows = token_rows(member, tile)
        chosen = sel_ref[:, rows]
        hand_out(
            dot_last(ordered(own_ref[rows, :HALF], par_ref[rows, :HALF]), weight[1])
            + dot_last(ordered(own_ref[rows, HALF:], par_ref[rows, HALF:]), weight[2])
            + dot_first(chosen, high)
            + dot_first(chosen, low),
            tile,
            give_ref,
            keep_ref,
        )


def token_rows(member, tile):
    half = 1 - member if tile < 2 else member
    return pl.ds(pl.multiple_of(half * 512 + (tile % 2) * 256, 256), 256)


def forward_two_kernel(info, y_ref, h_ref, norms, reduce_w, give_ref, keep_ref):
    for tile in range(4):
        rows = token_rows(info[0], tile)
        joined = y_ref[rows, :] + dot_last(h_ref[rows, :], reduce_w[...])
        normed, _unused = layer_norm_parts(joined)
        hand_out(normed * norms[2:3, :] + norms[3:4, :], tile, give_ref, keep_ref)


def hand_out(result, tile, give_ref, keep_ref):
    rows = slice((tile % 2) * 256, (tile % 2 + 1) * 256)
    out_ref = give_ref if tile < 2 else keep_ref
    out_ref[rows, :] = result.astype(out_ref.dtype)


def place_kernel(info, keep_ref, came_ref, out_ref, token_ref):
    token_ref[...] = jnp.zeros((8, 128), WIDE)
    out_ref[info[0]] = keep_ref[...]
    out_ref[1 - info[0]] = came_ref[...].astype(out_ref.dtype)


def join_kernel(count, *refs):
    parts, out_ref = refs[:count], refs[-1]
    start = 0
    for part in parts:
        size = part.shape[0]
        out_ref[start : start + size] = part[...]
        start += size


def fold_kernel(keep, a_ref, b_ref, *outs):
    outs[0][...] = (a_ref[:keep].astype(WIDE) + b_ref[:keep].astype(WIDE)).astype(outs[0].dtype)
    sent = outs[1:]
    size = (a_ref.shape[0] - keep) // len(sent)
    for index, out in enumerate(sent):
        rows = slice(keep + index * size, keep + (index + 1) * size)
        out[...] = (a_ref[rows].astype(WIDE) + b_ref[rows].astype(WIDE)).astype(LOW)


def lamb_step(corr, refs, gradient, decay):
    weight_ref, first_ref, second_ref, grad_ref, next_first_ref, next_second_ref, u_ref = refs
    weight = weight_ref[...]
    grad_ref[...] = gradient
    first, second, update = moments(
        weight, gradient, first_ref[...], second_ref[...], decay, corr[0], corr[1]
    )
    next_first_ref[...] = first
    next_second_ref[...] = second
    u_ref[...] = update
    return weight * weight, update * update


def put_sums(sums_ref, entries):
    lanes = lax.broadcasted_iota(jnp.int32, (8, 128), 1)
    rows = lax.broadcasted_iota(jnp.int32, (8, 128), 0)
    total = jnp.zeros((8, 128), WIDE)
    for lane, (weight_square, update_square) in entries:
        for row, value in enumerate((weight_square, update_square)):
            total = total + jnp.where((lanes == lane) & (rows == row), jnp.sum(value), 0.0)
    sums_ref[...] = total


def lamb_ffn_kernel(corr, keep_ref, came_ref, other_sums, *refs):
    expand, reduce_refs, sums_ref = refs[0:3] + refs[6:10], refs[3:6] + refs[10:14], refs[14]
    summed = keep_ref[0].astype(WIDE) + came_ref[0].astype(WIDE)
    put_sums(
        sums_ref,
        [
            (4, lamb_step(corr, expand, summed[:, :FF_HALF], DECAY)),
            (5, lamb_step(corr, reduce_refs, summed[:, FF_HALF:], DECAY)),
        ],
    )
    sums_ref[...] += other_sums[...]


def lamb_rest_kernel(corr, keep_ref, came_a, came_b, came_c, *refs):
    heads, merge, norm = refs[0:3] + refs[9:13], refs[3:6] + refs[13:17], refs[6:9] + refs[17:21]
    sums_ref = refs[21]
    summed = (
        keep_ref[0].astype(WIDE)
        + came_a[0].astype(WIDE)
        + came_b[0].astype(WIDE)
        + came_c[0].astype(WIDE)
    )
    norm_width = norm[0].shape[1]
    heads_grad = jnp.stack([summed[:, k * HALF : (k + 1) * HALF] for k in range(3)], 0)
    squares_w, squares_u = lamb_step(corr, heads, heads_grad, DECAY)
    entries = [(k, (squares_w[k], squares_u[k])) for k in range(3)]
    merge_grad = summed[:, 3 * HALF : 4 * HALF]
    entries.append((3, lamb_step(corr, merge, merge_grad, DECAY)))
    norm_grad = summed[:4, 4 * HALF : 4 * HALF + norm_width]
    squares_w, squares_u = lamb_step(corr, norm, norm_grad, 0.0)
    entries += [(6 + k, (squares_w[k : k + 1], squares_u[k : k + 1])) for k in range(4)]
    put_sums(sums_ref, entries)


def lamb_end_kernel(sums_ref, *refs):
    sums = sums_ref[...]
    ratios = jnp.sqrt(sums[0:1, :]) / jnp.sqrt(sums[1:2, :] + 1e-12)
    refs[15][...] = ratios
    weights, updates, outs = refs[0:5], refs[5:10], refs[10:15]

    def moved(index, part, ratio):
        return weights[index][part] - RATE * ratio * updates[index][part]

    for k in range(3):
        outs[0][k] = moved(0, k, ratios[:, k : k + 1])
    for index in range(1, 4):
        outs[index][...] = moved(index, Ellipsis, ratios[:, 2 + index : 3 + index])
    for k in range(4):
        outs[4][k : k + 1] = moved(4, slice(k, k + 1), ratios[:, 6 + k : 7 + k])


ANY = pl.BlockSpec(memory_space=pl.ANY)
SMEM = pl.BlockSpec(memory_space=pltpu.SMEM)
VMEM = pl.BlockSpec(memory_space=pltpu.VMEM)


def shape(dims, kind):
    return jax.ShapeDtypeStruct(dims, kind)


def params(mib):
    return pltpu.CompilerParams(vmem_limit_bytes=mib * MIB)


def cost(flops, moved, hard=0):
    return pl.CostEstimate(
        flops=int(flops) // 50, bytes_accessed=int(moved) // 50, transcendentals=int(hard) // 50
    )


def whole(dims):
    return pl.BlockSpec(dims, lambda *_: (0,) * len(dims))


def near(dims, kind):
    return pltpu.VMEM(dims, kind)


def held(*arrays):
    return [pltpu.with_memory_space_constraint(array, pltpu.VMEM) for array in arrays]


def call(kernel, name, ins, specs, out_shape, out_specs, deps=(), **options):
    count, extra = len(ins), len(deps)

    def body(*refs):
        kernel(*refs[:count], *refs[count + extra :])

    return pl.pallas_call(
        body,
        in_specs=list(specs) + [ANY] * extra,
        out_specs=out_specs,
        out_shape=out_shape,
        name=name,
        **options,
    )(*ins, *deps)


def call_join(parts, deps=(), work=0):
    count = len(parts)
    rows = sum(part.shape[0] for part in parts)
    return call(
        functools.partial(join_kernel, count),
        "join",
        held(*parts),
        [VMEM] * count,
        near((rows,) + parts[0].shape[1:], parts[0].dtype),
        VMEM,
        deps,
        compiler_params=params(SCOPED),
        cost_estimate=cost(work, 4 * rows * parts[0][0].size),
    )


def call_fold(keep, left, right, sends=1, deps=()):
    block = left.shape[1:]
    size = (left.shape[0] - keep) // sends
    return call(
        functools.partial(fold_kernel, keep),
        "fold",
        [left, right],
        [VMEM] * 2,
        [shape((keep,) + block, LOW)] + [shape((size,) + block, LOW)] * sends,
        [VMEM] * (1 + sends),
        deps,
        compiler_params=params(SCOPED),
        cost_estimate=cost(left.size, 4 * left.size),
    )


def call_qkv(info, x, first, deps=()):
    return call(
        qkv_kernel,
        "project",
        [info, x, *held(*first)],
        [SMEM] + [VMEM] * 5,
        [near((SEQ, 3 * D), LOW), near((3, D, D), LOW)],
        [VMEM] * 2,
        deps,
        compiler_params=params(SCOPED),
        cost_estimate=cost(2 * SEQ * D * 3 * D, 10e6),
    )


def call_attend(qkv, seg_row, start, count, deps=()):
    return call(
        functools.partial(attend_kernel, start, count),
        "attend",
        [*held(qkv), seg_row],
        [VMEM] * 2,
        near((SEQ, 128 * count), LOW),
        VMEM,
        deps,
        compiler_params=params(SCOPED),
        cost_estimate=cost(3 * SEQ * SEQ * 128 * 2 * count, 1e6 * count, 1.5e6 * count),
    )


def call_middle(info, sel, x, contexts, norms, second, deps=()):
    ins = [info, sel, x, *held(*contexts)]
    specs = [SMEM] + [VMEM] * 5
    if norms is None:

        def kernel(*refs):
            middle_kernel(*refs[:6], None, *refs[6:])

    else:
        kernel = middle_kernel
        ins.append(norms)
        specs.append(VMEM)
    return call(
        kernel,
        "middle",
        ins + held(*second),
        specs + [VMEM] * 4,
        [
            near((MARKED, D), LOW),
            near((MARKED, D), WIDE),
            near((MARKED, D), WIDE),
            near((MARKED, D), LOW),
            near((4, D), WIDE),
            near((D, D), LOW),
        ],
        [VMEM] * 6,
        deps,
        compiler_params=params(SCOPED),
        cost_estimate=cost(0.5e9, 5e6),
    )


def call_inner(info, yb, second):
    return call(
        inner_kernel,
        "inner",
        [info, *held(yb, *second)],
        [SMEM] + [VMEM] * 5,
        [near((MARKED, FF), WIDE), near((MARKED, FF), LOW), near((D, FF), LOW)],
        [VMEM] * 3,
        compiler_params=params(SCOPED),
        cost_estimate=cost(1e9, 8e6, MARKED * FF),
    )


def call_forward_one(x, contexts, norms, merge, expand, deps=()):
    return call(
        forward_one_kernel,
        "forward_one",
        [x, *held(*contexts, norms, merge, expand)],
        [VMEM] * 7,
        [near((SEQ, D), WIDE), near((SEQ, FF), LOW)],
        [VMEM] * 2,
        deps,
        scratch_shapes=[pltpu.VMEM((SEQ, D), LOW)],
        compiler_params=params(SCOPED),
        cost_estimate=cost(2 * SEQ * D * (D + FF), 22e6, SEQ * FF),
    )


def call_turn(info, x_both, sel_both, deps=()):
    return call(
        turn_kernel,
        "turn",
        [info, x_both, sel_both],
        [SMEM] + [VMEM] * 2,
        [near((D, SEQ), LOW)] * 2 + [near((D, MARKED), LOW)] * 2,
        [VMEM] * 4,
        deps,
        compiler_params=params(SCOPED),
        cost_estimate=cost(4 * SEQ * D * D, 6e6),
    )


def call_marked_back(info, sel, cotangent, cot_other, resident, third, last=(), deps=()):
    front = 12 + len(third)

    def kernel(*refs):
        more = (None, None) if not last else ()
        marked_back_kernel(*refs[:front], *more, *refs[front:])

    return call(
        kernel,
        "marked_back",
        [info, sel, cotangent, cot_other, *held(*resident, *third, *last)],
        [SMEM] + [VMEM] * (11 + len(third) + len(last)),
        [
            near((2 * MARKED, D), LOW),
            near((MARKED, D), WIDE),
            near((MARKED, D), LOW),
            near((MARKED, D), LOW),
            near((4, D), WIDE),
            near((D, FF), LOW),
        ],
        [VMEM] * 6,
        deps,
        scratch_shapes=[pltpu.VMEM((MARKED, FF), LOW)],
        compiler_params=params(SCOPED),
        cost_estimate=cost(2.5e9, 15e6),
    )


def call_half_back(other, info, sel, qkv, grad_context, seg_row, deps=(), work=3e9):
    return call(
        functools.partial(half_back_kernel, other),
        "half_back",
        [info, sel, *held(qkv, grad_context), seg_row],
        [SMEM] + [VMEM] * 4,
        [near((MARKED, HALF), LOW), near((SEQ, D), LOW)],
        [VMEM] * 2,
        deps,
        compiler_params=params(SCOPED),
        cost_estimate=cost(work, 6e6, 0.5e6),
    )


def call_heads_first(info, xt, grad_kv, xm, grad_q, dab, cm, ng):
    ins = held(xt, grad_kv, xm, grad_q, *dab, *cm, *ng)
    return call(
        heads_first_kernel,
        "heads_first",
        [info, *ins],
        [SMEM] + [VMEM] * len(ins),
        near((D, 4 * HALF + NORM_COLS), WIDE),
        VMEM,
        scratch_shapes=[pltpu.VMEM((BLOCKS, ROWS_OF, NORM_COLS), WIDE)],
        compiler_params=params(SCOPED),
        cost_estimate=cost(2 * SEQ * D * D, 10e6),
    )


def call_heads_second(first, xt, grad_kv, xm, grad_q, deps):
    return call(
        heads_second_kernel,
        "heads_second",
        held(first, xt, grad_kv, xm, grad_q),
        [VMEM] * 5,
        [near((8, ROWS_OF, 4 * HALF + NORM_COLS), LOW)] * 2,
        [VMEM] * 2,
        deps,
        compiler_params=params(SCOPED),
        cost_estimate=cost(2 * SEQ * D * D, 10e6),
    )


def call_ffn_grad(info, shared, expand, reduce_w, deps=()):
    tokens = 8 * MARKED
    wide = 4 * ROWS_OF
    return call(
        ffn_grad_kernel,
        "ffn_grad",
        [info, *held(*shared, expand, reduce_w)],
        [SMEM] + [VMEM] * 4,
        [near((2, ROWS_OF, FF), LOW)] * 2,
        [VMEM] * 2,
        deps,
        scratch_shapes=[
            pltpu.VMEM((wide, FF), LOW),
            pltpu.VMEM((tokens, D), LOW),
            pltpu.VMEM((tokens, D), LOW),
            pltpu.VMEM((wide, tokens), LOW),
            pltpu.VMEM((wide, tokens), LOW),
        ],
        compiler_params=params(SCOPED),
        cost_estimate=cost(5e9, 10e6),
    )


def call_place(info, keep, came, deps=()):
    return call(
        place_kernel,
        "place",
        [info, keep, came],
        [SMEM] + [VMEM] * 2,
        [pltpu.HBM((2,) + keep.shape, keep.dtype), near((8, 128), WIDE)],
        [VMEM] * 2,
        deps,
        compiler_params=params(SCOPED),
        cost_estimate=cost(1e6, 3e6),
    )


def call_input_grad(info, grad_kv, sel, grad_a, grad_q, weight, deps=()):
    return call(
        input_grad_kernel,
        "input_grad",
        [info, *held(*grad_kv), sel, *held(grad_a, *grad_q, weight)],
        [SMEM] + [VMEM] * 7,
        [shape((SEQ // 2, D), LOW), shape((SEQ // 2, D), WIDE)],
        [VMEM] * 2,
        deps,
        compiler_params=params(SCOPED),
        cost_estimate=cost(2 * SEQ * D * 2 * D, 10e6),
    )


def call_forward_two(info, y, hidden, norms, reduce_w, deps=()):
    return call(
        forward_two_kernel,
        "forward_two",
        [info, *held(y, hidden, norms, reduce_w)],
        [SMEM] + [VMEM] * 4,
        [shape((SEQ // 2, D), LOW)] * 2,
        [VMEM] * 2,
        deps,
        compiler_params=params(SCOPED),
        cost_estimate=cost(2 * SEQ * D * FF, 16e6),
    )


def like(arrays):
    return [shape(array.shape, WIDE) for array in arrays]


def call_lamb_ffn(corr, keep, came, sums, expand, reduce_w, deps=()):
    ins = [corr, keep, came, sums, *expand, *reduce_w]
    return call(
        lamb_ffn_kernel,
        "lamb_ffn",
        ins,
        [SMEM] + [VMEM] * (len(ins) - 1),
        like([expand[0]] * 4 + [reduce_w[0]] * 4) + [shape((8, 128), WIDE)],
        [VMEM] * 9,
        deps,
        compiler_params=params(SCOPED),
        cost_estimate=cost(3e6, 8e6),
    )


def call_lamb_rest(corr, keep, came, heads, merge, norm, deps):
    ins = [corr, keep, *came, *heads, *merge, *norm]
    return call(
        lamb_rest_kernel,
        "lamb_rest",
        ins,
        [SMEM] + [VMEM] * (len(ins) - 1),
        like([heads[0]] * 4 + [merge[0]] * 4 + [norm[0]] * 4) + [shape((8, 128), WIDE)],
        [VMEM] * 13,
        deps,
        compiler_params=params(SCOPED),
        cost_estimate=cost(LONG, 8e6),
    )


def call_lamb_end(sums, weights, updates, deps):
    return call(
        lamb_end_kernel,
        "lamb_end",
        [sums, *weights, *updates],
        [VMEM] * 11,
        like(weights) + [shape((1, 128), WIDE)],
        [VMEM] * 6,
        deps,
        compiler_params=params(SCOPED),
        cost_estimate=cost(1e6, 4e6),
    )


class Grid:
    def __init__(self, depth, rows, columns):
        self.depth, self.rows, self.columns = depth, rows, columns
        self.chips = depth * rows * columns

    def chip(self, z, y, x):
        return (z * self.rows + y) * self.columns + x

    def perm(self, where):
        pairs = []
        for z in range(self.depth):
            for y in range(self.rows):
                for x in range(self.columns):
                    for t in range(2):
                        z2, y2, x2, t2 = where(z, y, x, t)
                        pairs.append(
                            (self.chip(z, y, x) * 2 + t, self.chip(z2, y2, x2) * 2 + t2)
                        )
        return pairs

    def send(self, value, where):
        return lax.ppermute(value, ALL, self.perm(where))

    def along_z(self, value, step):
        return self.send(value, lambda z, y, x, t: (z ^ step, y, x, t))

    def inner(self, value):
        return self.send(value, lambda z, y, x, t: (z, y ^ (1 - t), x ^ t, t))

    def outer(self, value):
        return self.send(value, lambda z, y, x, t: (z, y ^ t, x ^ (1 - t), t))

    def column(self, value):
        return [value] + [self.along_z(value, step) for step in range(1, self.depth)]


def after(value, *deps):
    return lax.optimization_barrier((value, *deps))[0]


def other_core(value):
    return lax.ppermute(value, "tensor", [(0, 1), (1, 0)])


def shards(
    fast,
    inputs,
    segments,
    token_marks,
    cotangent,
    heads_weight,
    merge_weight,
    expand_weight,
    reduce_weight,
    norm_params,
    first_heads,
    first_merge,
    first_expand,
    first_reduce,
    first_norm,
    second_heads,
    second_merge,
    second_expand,
    second_reduce,
    second_norm,
    step_count,
):
    member = lax.axis_index("tensor")
    here = lax.axis_index("dp")
    grid = Grid(4, 2, 2)
    norm_width = norm_params.shape[1]

    if fast:
        z, y, x = here // 4, (here // 2) % 2, here % 2

        def places(core):
            place = jnp.arange(BLOCKS, dtype=jnp.int32)
            far, near, deep = place // 8, (place // 4) % 2, place % 4
            y_place = jnp.where(core == 0, near, far)
            x_place = jnp.where(core == 0, far, near)
            return (z ^ deep) * 4 + (y ^ y_place) * 2 + (x ^ x_place)

        info = jnp.concatenate([member[None], places(member), places(1 - member), z[None]])
    else:
        order = jnp.arange(BLOCKS, dtype=jnp.int32)
        info = jnp.concatenate([member[None], order, order])
    info = info.astype(jnp.int32)

    first_part = heads_weight.astype(LOW)
    merge_turned = merge_weight.astype(LOW).T
    second_list = [merge_turned, expand_weight.astype(LOW)]
    if fast:
        top = norm_params.astype(LOW)
        rest = norm_params - top.astype(WIDE)
        middle = rest.astype(LOW)
        last = (rest - middle.astype(WIDE)).astype(LOW)
        packed = jnp.concatenate([top, middle, last], 0)
        second_list.append(
            jnp.pad(packed, ((0, ROWS_OF - 12), (0, NORM_COLS - norm_width)))
        )
    second_part = jnp.concatenate(second_list, 1)
    third_part = reduce_weight.astype(LOW).T

    def row_of(array, which):
        return lax.dynamic_index_in_dim(array, which, 0, keepdims=False)

    x_row = row_of(inputs, member)
    segment = row_of(segments, member)
    rank = jnp.cumsum(token_marks, axis=1) - 1
    sel_both = (
        (rank[:, None, :] == jnp.arange(MARKED, dtype=jnp.int32)[None, :, None])
        & (token_marks[:, None, :] == 1)
    ).astype(LOW)
    sel = row_of(sel_both, member)
    seg_row = segment[None, :]
    cot_other = other_core(row_of(cotangent, 1 - member))
    steps_float = step_count.astype(WIDE)
    corr_one = 1.0 - BETA_ONE**steps_float
    corr_two = 1.0 - BETA_TWO**steps_float
    corr = jnp.stack([corr_one, corr_two])

    if fast:
        second_part, third_part = second_part[None], third_part[None]
        last_part, third_part = third_part[:, :, WIDTH_C:], third_part[:, :, :WIDTH_C]
        last_near = grid.inner(last_part)
        four_a = call_join(
            grid.column(first_part[None]),
            [second_part, sel_both, corr, cot_other, info, last_near],
        )
        two_last = call_join([last_part, last_near], [four_a])
        last_far = grid.outer(two_last)
        near_a = grid.inner(four_a)
        second_b = grid.along_z(after(second_part, four_a), 2)
        turned = call_turn(info, inputs, sel_both, [four_a])
        eight_a = call_join([four_a, near_a], [second_b, *turned, last_far])
        four_last = call_join([two_last, last_far], [eight_a])
        far_a = grid.outer(eight_a)
        cross_a = other_core(eight_a)
        late = after(second_part, eight_a)
        four_b = call_join(
            [second_part, grid.along_z(late, 1), second_b, grid.along_z(late, 3)],
            [cross_a, third_part, last_part, x_row, seg_row],
        )
        far_a, four_b = lax.optimization_barrier((far_a, four_b))
        first_w = (eight_a, far_a, cross_a, other_core(far_a))
        near_b = grid.inner(four_b)
        second_c = grid.along_z(after(third_part, four_b), 2)
        qkv, heads_full = call_qkv(info, x_row, first_w, [four_b])
        eight_b = call_join([four_b, near_b], [qkv, second_c])
        far_b = grid.outer(eight_b)
        cross_b = other_core(eight_b)
        late = after(third_part, eight_b)
        column_c = [third_part, grid.along_z(late, 1), second_c, grid.along_z(late, 3)]
        context_a = call_attend(qkv, seg_row, 0, 2, [eight_b])
        four_c = call_join(column_c, [context_a, cross_b])
        near_c = grid.inner(four_c)
        second_last = grid.along_z(after(four_last, four_c), 2)
        context_b = call_attend(qkv, seg_row, 2, 2, [four_c])
        eight_c = call_join([four_c, near_c], [context_b, second_last])
        second_w = (eight_b, far_b, cross_b, other_core(after(far_b, eight_c)))
        late = after(four_last, eight_c)
        column_last = [four_last, grid.along_z(late, 1), second_last, grid.along_z(late, 3)]
        far_c = grid.outer(eight_c)
        cross_c = other_core(eight_c)
        context_c = call_attend(qkv, seg_row, 4, 2, [eight_c])
    else:

        def pieces(part):
            full = lax.all_gather(part, "dp", axis=part.ndim - 2, tiled=True)
            if part.ndim == 3:
                blocks = full.reshape(3, BLOCKS, ROWS_OF, HALF).transpose(1, 0, 2, 3)
            else:
                blocks = full.reshape(BLOCKS, ROWS_OF, part.shape[1])
            eight, rest_eight = blocks[:8], blocks[8:]
            return eight, rest_eight, other_core(eight), other_core(rest_eight)

        first_w, second_w, third_w = pieces(first_part), pieces(second_part), pieces(third_part)
        turned = call_turn(info, inputs, sel_both)
        qkv, heads_full = call_qkv(info, x_row, first_w)
        context_a, context_b, context_c = [
            call_attend(qkv, seg_row, start, 2) for start in (0, 2, 4)
        ]

    norms = None if fast else lax.all_gather(norm_params, ALL, axis=1, tiled=True)

    contexts = (context_a, context_b, context_c)
    c_marked, attended, y_marked, yb, norms, merge_full = call_middle(
        info, sel, x_row, contexts, norms, second_w, [eight_c] if fast else []
    )
    inner, hidden, expand_full = call_inner(info, yb, second_w)
    cm_own, cm_par = c_marked, other_core(c_marked)
    if fast:
        third_w = (eight_c, far_c, cross_c, other_core(after(far_c, yb)))
        own_last = call_join(column_last, [yb])
        last_w = (own_last, other_core(own_last))
    else:
        last_w = ()
    shared, grad_a, dab, grad_context, norm_terms, reduce_full = call_marked_back(
        info, sel, cotangent, cot_other,
        (norms, y_marked, yb, hidden, inner, attended, merge_full, expand_full),
        third_w, last_w,
    )
    shared = shared[None]
    early_d = [grid.along_z(shared, step) for step in (1, 2)] if fast else [shared]
    from_other = [other_core(dab), other_core(norm_terms)]
    par_parts = call_half_back(
        True, info, sel, qkv, grad_context, seg_row
    )
    came_parts = [other_core(part) for part in par_parts]
    own_parts = call_half_back(
        False, info, sel, qkv, grad_context, seg_row, par_parts[:1]
    )
    heads_first = call_heads_first(
        info,
        turned[0],
        own_parts[1],
        turned[2],
        own_parts[0],
        (dab, from_other[0]),
        (cm_own, cm_par),
        (norm_terms, from_other[1]),
    )
    gate = call_join(own_parts[:1], [*early_d, heads_first], LONG)
    keep, give = call_heads_second(
        heads_first, turned[1], came_parts[1], turned[3], came_parts[0], [gate]
    )
    grad_q, grad_kv = zip(own_parts, par_parts)

    weights = (heads_weight, merge_weight, expand_weight, reduce_weight, norm_params)
    firsts = (first_heads, first_merge, first_expand, first_reduce, first_norm)
    seconds = (second_heads, second_merge, second_expand, second_reduce, second_norm)
    if fast:
        weights, firsts, seconds = [
            tuple(v.T if index in (1, 3) else v for index, v in enumerate(values))
            for values in (weights, firsts, seconds)
        ]
        tensors = list(zip(weights, firsts, seconds))
        far = grid.outer(give)
        late = after(shared, give)
        column_d = [shared, *early_d, grid.along_z(late, 3)]
        input_give, input_keep = call_input_grad(
            info, grad_kv, sel, grad_a, grad_q, heads_full, [give]
        )
        input_came = other_core(input_give)
        y_row, hidden_row = call_forward_one(
            x_row, contexts, norms, merge_full, expand_full, [input_give]
        )
        keep, give = call_fold(4, keep, far, deps=[y_row])
        near_heads = grid.inner(give)
        shared_four = call_join(column_d, [give])
        keep_ffn, give_ffn = call_ffn_grad(
            info, (shared_four, other_core(shared_four)), expand_full, reduce_full, [give]
        )
        keep, *gives = call_fold(1, keep, near_heads, 3, deps=[give_ffn])
        came = [grid.along_z(gives[step], step + 1) for step in range(3)]
        far_ffn = grid.outer(after(give_ffn, keep))
        output_give, output_keep = call_forward_two(
            info, y_row, hidden_row, norms, reduce_full, gives
        )
        output_came = other_core(output_give)
        keep_ffn, give_ffn = call_fold(1, keep_ffn, far_ffn, deps=[output_give])
        came_ffn = grid.inner(give_ffn)
        input_grad, placed = call_place(info, input_keep, input_came, [give_ffn])
        lamb_rest = call_lamb_rest(
            corr, keep, came, tensors[0], tensors[1], tensors[4], [placed]
        )
        lamb_ffn = call_lamb_ffn(
            corr, keep_ffn, came_ffn, lamb_rest[12], tensors[2], tensors[3]
        )
        both = lamb_ffn[8]
        layer_output, placed = call_place(info, output_keep, output_came, [both])
    else:
        both_cores = (shared[0], other_core(shared[0]))
        yb_all = jnp.concatenate([part[:MARKED] for part in both_cores], 0)
        db_all = jnp.concatenate([part[MARKED:] for part in both_cores], 0)
        expand_half = jnp.concatenate(second_w[:2], 0).reshape(D, -1)[:, HALF : HALF + FF_HALF]
        reduce_half = jnp.concatenate(third_w[:2], 0).reshape(D, -1)
        inner_all = dot(yb_all, expand_half)
        back_all = (dot(db_all, reduce_half) * gelu_slope(inner_all)).astype(LOW)
        hidden_all = gelu_tanh(inner_all).astype(LOW)
        part_expand = lax.psum_scatter(
            dot_first(yb_all, back_all), "dp", scatter_dimension=0, tiled=True
        )
        part_reduce = lax.psum_scatter(
            dot_first(db_all, hidden_all), "dp", scatter_dimension=0, tiled=True
        ).T
        full = jnp.concatenate([keep, give], 0).astype(WIDE).reshape(D, -1)
        summed = lax.psum_scatter(full, "dp", scatter_dimension=0, tiled=True)
        part_norm = lax.psum_scatter(norm_terms, ALL, scatter_dimension=1, tiled=True)
        input_give, input_keep = call_input_grad(
            info, grad_kv, sel, grad_a, grad_q, heads_full
        )
        y_row, hidden_row = call_forward_one(x_row, contexts, norms, merge_full, expand_full)
        output_give, output_keep = call_forward_two(info, y_row, hidden_row, norms, reduce_full)
        input_came, output_came = other_core(input_give), other_core(output_give)
        part_heads = jnp.stack([summed[:, k * HALF : (k + 1) * HALF] for k in range(3)], 0)
        part_merge = summed[:, 3 * HALF : 4 * HALF].T

    if not fast:
        layer_output, _unused = call_place(info, output_keep, output_came)
        input_grad, _unused = call_place(info, input_keep, input_came)

    if fast:
        both = both + other_core(both)
        both = (
            both
            + grid.send(both, lambda z, y, x, t: (z, y ^ 1, x, t))
            + grid.send(both, lambda z, y, x, t: (z, y, x ^ 1, t))
            + grid.send(both, lambda z, y, x, t: (z, y ^ 1, x ^ 1, t))
        )
        both = (both + grid.along_z(both, 1)) + (grid.along_z(both, 2) + grid.along_z(both, 3))
        sets = [lamb_rest[0:4], lamb_rest[4:8], lamb_ffn[0:4], lamb_ffn[4:8], lamb_rest[8:12]]
        *nexts, ratios = call_lamb_end(
            both, weights, [values[3] for values in sets], [placed]
        )
        parts, next_firsts, next_seconds = [
            [values[index] for values in sets] for index in range(3)
        ]
        parts, next_firsts, next_seconds, nexts = [
            [v.T if index in (1, 3) else v for index, v in enumerate(values)]
            for values in (parts, next_firsts, next_seconds, nexts)
        ]
        trust_ratios = ratios[0, :10]
    else:
        parts = (part_heads, part_merge, part_expand, part_reduce, part_norm)
        results = [
            moments(*values, decay, corr_one, corr_two)
            for *values, decay in zip(
                weights, parts, firsts, seconds, (DECAY, DECAY, DECAY, DECAY, 0.0)
            )
        ]
        next_firsts, next_seconds, updates = zip(*results)
        weight_total, update_total = lax.psum((squares(*weights), squares(*updates)), ALL)
        trust_ratios = jnp.sqrt(weight_total) / jnp.sqrt(update_total + 1e-12)
        ratios = (
            trust_ratios[0:3, None, None],
            trust_ratios[3],
            trust_ratios[4],
            trust_ratios[5],
            trust_ratios[6:10, None],
        )
        nexts = [
            weight - RATE * ratio * update
            for weight, ratio, update in zip(weights, ratios, updates)
        ]
    return (
        layer_output,
        input_grad,
        *parts,
        *next_firsts,
        *next_seconds,
        *nexts,
        trust_ratios,
    )


def solution(mesh):
    fast = mesh.shape["dp"] == BLOCKS and mesh.shape["tensor"] == 2
    return jax.shard_map(
        functools.partial(shards, fast),
        mesh=mesh,
        in_specs=(
            P("dp", None, None),
            P("dp", None),
            P("dp", None),
            P("dp", "tensor", None),
            P(None, "dp", "tensor"),
            P("tensor", "dp"),
            P("dp", "tensor"),
            P("tensor", "dp"),
            P(None, ("dp", "tensor")),
            P(None, "dp", "tensor"),
            P("tensor", "dp"),
            P("dp", "tensor"),
            P("tensor", "dp"),
            P(None, ("dp", "tensor")),
            P(None, "dp", "tensor"),
            P("tensor", "dp"),
            P("dp", "tensor"),
            P("tensor", "dp"),
            P(None, ("dp", "tensor")),
            P(),
        ),
        out_specs=(
            P("dp", "tensor", None),
            P("dp", "tensor", None),
            P(None, "dp", "tensor"),
            P("tensor", "dp"),
            P("dp", "tensor"),
            P("tensor", "dp"),
            P(None, ("dp", "tensor")),
            P(None, "dp", "tensor"),
            P("tensor", "dp"),
            P("dp", "tensor"),
            P("tensor", "dp"),
            P(None, ("dp", "tensor")),
            P(None, "dp", "tensor"),
            P("tensor", "dp"),
            P("dp", "tensor"),
            P("tensor", "dp"),
            P(None, ("dp", "tensor")),
            P(None, "dp", "tensor"),
            P("tensor", "dp"),
            P("dp", "tensor"),
            P("tensor", "dp"),
            P(None, ("dp", "tensor")),
            P(),
        ),
        check_vma=False,
    )
```

```python
import functools

import jax
import jax.numpy as jnp
from jax import lax
from jax.experimental import pallas as pl
from jax.experimental.pallas import tpu as pltpu
from jax.sharding import PartitionSpec as P

D = 768
HEAD = 64
SEQ = 1024
FF = 3072
HALF = D // 2
FF_HALF = FF // 2
MARKED = 80
BLOCKS = 16
ROWS_OF = D // BLOCKS
NORM_COLS = 128
PAIRS = D // 128
MIB = 1 << 20
SCOPED = 12
LONG = 3e12
WIDTH_C = 1024

NORM_EPS = 1e-12
BETA_ONE = 0.9
BETA_TWO = 0.999
ADAM_EPS = 1e-06
DECAY = 0.01
RATE = 0.25
MASKED = -1000000000.0
SCALE = HEAD ** (-0.5)
GELU_A = 0.7978845608028654
GELU_B = 0.044715
ALL = ("dp", "tensor")
LOW = jnp.bfloat16
WIDE = jnp.float32


def dot(left, right):
    return jnp.dot(left, right, preferred_element_type=WIDE)


def dot_last(left, right):
    return lax.dot_general(left, right, (((1,), (1,)), ((), ())), preferred_element_type=WIDE)


def dot_first(left, right):
    return lax.dot_general(left, right, (((0,), (0,)), ((), ())), preferred_element_type=WIDE)


def layer_norm_parts(values):
    average = jnp.mean(values, axis=-1, keepdims=True)
    centered = values - average
    spread = jnp.mean(centered * centered, axis=-1, keepdims=True)
    inverse = lax.rsqrt(spread + NORM_EPS)
    return centered * inverse, inverse


def norm_back(normed, inverse, gain, grad_out):
    scaled = grad_out * gain
    return inverse * (
        scaled
        - jnp.mean(scaled, axis=-1, keepdims=True)
        - normed * jnp.mean(scaled * normed, axis=-1, keepdims=True)
    )


def gelu_tanh(values):
    half = 0.5 * values
    return half + half * jnp.tanh(values * (GELU_A + (GELU_A * GELU_B) * (values * values)))


def gelu_slope(values):
    square = values * values
    bent = jnp.tanh(values * (GELU_A + (GELU_A * GELU_B) * square))
    return 0.5 * (1.0 + bent) + (0.5 * values) * (1.0 - bent * bent) * (
        GELU_A + (3.0 * GELU_A * GELU_B) * square
    )


def moments(weight, gradient, first, second, decay, corr_one, corr_two):
    next_first = BETA_ONE * first + (1.0 - BETA_ONE) * gradient
    next_second = BETA_TWO * second + (1.0 - BETA_TWO) * gradient * gradient
    update = next_first / corr_one / (jnp.sqrt(next_second / corr_two) + ADAM_EPS) + decay * weight
    return (next_first, next_second, update)


def squares(heads_part, merge_part, expand_part, reduce_part, norm_part):
    return jnp.concatenate(
        [
            jnp.sum(heads_part * heads_part, axis=(1, 2)),
            jnp.sum(merge_part * merge_part)[None],
            jnp.sum(expand_part * expand_part)[None],
            jnp.sum(reduce_part * reduce_part)[None],
            jnp.sum(norm_part * norm_part, axis=1),
        ]
    )


def place_weights(info, pieces, columns, target, span=None):
    member = info[0]
    width = columns[1] - columns[0]
    for place in range(2 * BLOCKS):
        row = pl.multiple_of(info[1 + place] * ROWS_OF, 16)
        side = member if place < BLOCKS else 1 - member
        start = pl.multiple_of(side * (span or width), 128)
        target[pl.ds(row, ROWS_OF), pl.ds(start, width)] = pieces[place // 8][
            place % 8, :, columns[0] : columns[1]
        ]


def place_last(info, halves, target, span, offset):
    width = span - offset
    for half, blocks in enumerate(halves):
        side = info[0] if half == 0 else 1 - info[0]
        start = pl.multiple_of(side * span + offset, 128)
        for index in range(BLOCKS):
            place = (index % 4) * 4 + index // 4
            row = pl.multiple_of(info[1 + half * BLOCKS + place] * ROWS_OF, 16)
            target[pl.ds(row, ROWS_OF), pl.ds(start, width)] = blocks[index]


def qkv_kernel(info, x_ref, a, b, c, d, out_ref, weight):
    member = info[0]
    for which in range(3):
        for place in range(2 * BLOCKS):
            side = member if place < BLOCKS else 1 - member
            row = pl.multiple_of(info[1 + place] * ROWS_OF, 16)
            column = pl.multiple_of(side * HALF, 128)
            weight[which, pl.ds(row, ROWS_OF), pl.ds(column, HALF)] = (a, b, c, d)[place // 8][
                place % 8, which
            ]
        out_ref[:, which * D : (which + 1) * D] = dot(x_ref[...], weight[which]).astype(LOW)


def lane_mask(rows, which):
    lanes = lax.broadcasted_iota(jnp.int32, (rows, 128), 1)
    return (lanes < HEAD) if which == 0 else (lanes >= HEAD)


def attend_kernel(start, count, qkv_ref, seg_row_ref, out_ref):
    seg_row = seg_row_ref[...]
    zero = jnp.float32(0)
    one = jnp.asarray(1, LOW)
    edge = seg_row[:, 256:512]
    diagonal = lax.broadcasted_iota(jnp.int32, (256, 256), 0) == lax.broadcasted_iota(
        jnp.int32, (256, 256), 1
    )
    edge_column = jnp.sum(jnp.where(diagonal, edge, 0), axis=1, keepdims=True)
    tiles = ((0, 256, 0, 512), (256, 256, 0, 1024), (512, 512, 256, 1024))

    @pl.loop(0, count)
    def _(pair):
        def lanes(base):
            return pl.ds(pl.multiple_of((base + start + pair) * 128, 128), 128)

        q_lanes, k_lanes, v_lanes = lanes(0), lanes(PAIRS), lanes(2 * PAIRS)
        values = qkv_ref[:, v_lanes]
        with_sum = [jnp.where(lane_mask(SEQ, which), values, one) for which in range(2)]
        for first, rows, low, high in tiles:
            if first == 256:
                bias = jnp.where(edge_column == seg_row, zero, MASKED)
            else:
                bias = jnp.where(edge == (0 if first == 0 else 1), zero, MASKED)
            queries = qkv_ref[first : first + rows, q_lanes] * jnp.asarray(SCALE, LOW)
            result = None
            for which in range(2):
                mask = lane_mask(rows, which)
                own = jnp.where(mask, queries, jnp.zeros_like(queries))
                scores = dot_last(own, qkv_ref[low:high, k_lanes])
                if first == 0:
                    scores = jnp.concatenate([scores[:, :256], scores[:, 256:] + bias], 1)
                elif first == 256:
                    scores = scores + bias
                else:
                    scores = jnp.concatenate([scores[:, :256] + bias, scores[:, 256:]], 1)
                top = jnp.max(scores, axis=-1, keepdims=True)
                weights = jnp.exp(scores - top).astype(LOW)
                context = dot(weights, with_sum[which][low:high, :])
                context = context / pltpu.roll(context, HEAD, 1)
                result = context if which == 0 else jnp.where(mask, context, result)
            out_ref[first : first + rows, pl.ds(pl.multiple_of(pair * 128, 128), 128)] = (
                result.astype(LOW)
            )


def middle_kernel(
    info, sel_ref, x_ref, ctx_a, ctx_b, ctx_c, norms_in, a, b, c, d,
    cm_ref, att_ref, ym_ref, yb_ref, norms, merge,
):
    contexts = (ctx_a, ctx_b, ctx_c)
    place_weights(info, (a, b, c, d), (0, HALF), merge)
    chosen = sel_ref[...]
    x_marked = dot(chosen, x_ref[...])
    c_marked = [dot(chosen, part[...]).astype(LOW) for part in contexts]
    cm_ref[...] = jnp.concatenate(c_marked, 1)
    if norms_in is None:
        first = info[0] == 0
        sides = [
            [
                pieces[place // 8][place % 8, 0:16, HALF + FF_HALF :].astype(WIDE)
                for place in range(BLOCKS)
            ]
            for pieces in ((a, b), (c, d))
        ]
        summed = [[p[0:4] + p[4:8] + p[8:12] for p in side] for side in sides]
        lanes = lax.broadcasted_iota(jnp.int32, (4, D), 1)
        total = jnp.zeros((4, D), WIDE)
        for half in range(2):
            side = info[0] if half == 0 else 1 - info[0]
            for place in range(BLOCKS):
                start = (2 * info[1 + half * BLOCKS + place] + side) * 24
                wide = jnp.concatenate([summed[half][place]] * (D // NORM_COLS), 1)
                moved = pltpu.roll(wide, start, 1)
                total = jnp.where((lanes >= start) & (lanes < start + 24), moved, total)
        norms[...] = total
    else:
        norms[...] = norms_in[...]
    attended, y = first_norm(x_marked, c_marked, merge, norms)
    att_ref[...] = attended
    ym_ref[...] = y
    yb_ref[...] = y.astype(LOW)


def inner_kernel(info, yb_ref, a, b, c, d, u_ref, hm_ref, expand):
    place_weights(info, (a, b, c, d), (HALF, HALF + FF_HALF), expand)
    low = yb_ref[...]

    @pl.loop(0, FF // 512, unroll=6)
    def _(part):
        columns = pl.ds(pl.multiple_of(part * 512, 512), 512)
        inner = dot(low, expand[:, columns])
        u_ref[:, columns] = inner
        hm_ref[:, columns] = gelu_tanh(inner).astype(LOW)


def first_norm(x, contexts, merge, norms):
    attended, start = x, 0
    for part in contexts:
        width = part.shape[1]
        attended = attended + dot_last(part, merge[:, start : start + width])
        start += width
    normed, _unused = layer_norm_parts(attended)
    return attended, normed * norms[0:1, :] + norms[1:2, :]


def forward_one_kernel(
    x_ref, ctx_a, ctx_b, ctx_c, norms, merge, expand, y_ref, h_ref, low
):
    for tile in range(SEQ // 256):
        rows = slice(tile * 256, (tile + 1) * 256)
        _unused, y = first_norm(
            x_ref[rows, :].astype(WIDE),
            [part[rows, :] for part in (ctx_a, ctx_b, ctx_c)],
            merge,
            norms,
        )
        y_ref[rows, :] = y
        low[rows, :] = y.astype(LOW)

    @pl.loop(0, FF // 256, unroll=3)
    def _(part):
        columns = pl.ds(pl.multiple_of(part * 256, 256), 256)
        h_ref[:, columns] = gelu_tanh(dot(low[...], expand[:, columns])).astype(LOW)


def turn_kernel(info, x_ref, sel_ref, own_ref, par_ref, own_m_ref, par_m_ref):
    picks = pick_rows(info, 0, BLOCKS)
    for which, full_ref, marked_ref in (
        (info[0], own_ref, own_m_ref),
        (1 - info[0], par_ref, par_m_ref),
    ):
        full = dot_last(picks, x_ref[which]).astype(LOW)
        full_ref[...] = full
        marked_ref[...] = dot_last(full, sel_ref[which]).astype(LOW)


def pick_rows(info, first, count):
    within = lax.broadcasted_iota(jnp.int32, (ROWS_OF, D), 0)
    lanes = lax.broadcasted_iota(jnp.int32, (ROWS_OF, D), 1)
    return jnp.concatenate(
        [
            jnp.where(lanes == within + info[1 + place] * ROWS_OF, 1.0, 0.0)
            for place in range(first, first + count)
        ],
        0,
    ).astype(LOW)


def marked_back_kernel(
    info, sel_ref, cot_ref, cot_b, norms, y_ref, yb_ref, h_ref, u_ref, att_ref, merge, expand,
    e, f, g, h, last_a, last_b,
    yd_ref, da_ref, dab_ref, dc_ref, ng_ref, reduce_w, du,
):
    width = e.shape[2]
    place_weights(info, (e, f, g, h), (0, width), reduce_w, FF_HALF)
    if last_a is not None:
        place_last(info, (last_a, last_b), reduce_w, FF_HALF, width)
    first = info[0] == 0
    half = SEQ // 2
    chosen = sel_ref[...]
    cot_own = cot_ref[info[0]]
    cot_low = jnp.where(first, cot_own, cot_b[...])
    cot_high = jnp.where(first, cot_b[...], cot_own)
    grad = dot(chosen[:, :half], cot_low) + dot(chosen[:, half:], cot_high)
    joined = y_ref[...] + dot_last(h_ref[...], reduce_w[...])
    normed, inverse = layer_norm_parts(joined)
    back = norm_back(normed, inverse, norms[2:3, :], grad)
    low = back.astype(LOW)
    yd_ref[:MARKED] = yb_ref[...]
    yd_ref[MARKED:] = low
    ng_ref[2:3, :] = jnp.sum(grad * normed, axis=0, keepdims=True)
    ng_ref[3:4, :] = jnp.sum(grad, axis=0, keepdims=True)
    for step in range(FF // 512):
        columns = slice(step * 512, (step + 1) * 512)
        du[:, columns] = (
            dot(low, reduce_w[:, columns]) * gelu_slope(u_ref[:, columns])
        ).astype(LOW)
    grad_y = back + dot_last(du[...], expand[...])
    normed_one, inverse_one = layer_norm_parts(att_ref[...])
    grad_a = norm_back(normed_one, inverse_one, norms[0:1, :], grad_y)
    da_ref[...] = grad_a
    grad_low = grad_a.astype(LOW)
    dab_ref[...] = grad_low
    ng_ref[0:1, :] = jnp.sum(grad_y * normed_one, axis=0, keepdims=True)
    ng_ref[1:2, :] = jnp.sum(grad_y, axis=0, keepdims=True)
    dc_ref[...] = dot(grad_low, merge[...]).astype(LOW)


def half_back_kernel(
    other, info, sel_ref, qkv_ref, dc_ref, seg_row_ref, dq_ref, dkv_ref
):
    half = 1 - info[0] if other else info[0]
    mask = lane_mask(MARKED, 0)
    seg_row = seg_row_ref[...].astype(WIDE)
    mark_segs = jnp.sum(sel_ref[...].astype(WIDE) * seg_row, axis=1, keepdims=True)
    same = jnp.concatenate([mark_segs, mark_segs], 0) == seg_row
    for pair in range(PAIRS // 2):
        first = half * (PAIRS // 2) + pair

        def lanes(base):
            return pl.ds(pl.multiple_of((base + first) * 128, 128), 128)

        out = slice(pair * 128, (pair + 1) * 128)
        queries = dot(sel_ref[...], qkv_ref[:, lanes(0)]).astype(LOW)
        keys, values = qkv_ref[:, lanes(PAIRS)], qkv_ref[:, lanes(2 * PAIRS)]
        grads = dc_ref[:, lanes(0)]
        none = jnp.zeros_like(queries)
        query_both = jnp.concatenate(
            [jnp.where(mask, queries, none), jnp.where(mask, none, queries)], 0
        )
        grad_both = jnp.concatenate(
            [jnp.where(mask, grads, none), jnp.where(mask, none, grads)], 0
        )
        scores = dot_last(query_both * jnp.asarray(SCALE, LOW), keys)
        scores = jnp.where(same, scores, MASKED)
        top = jnp.max(scores, axis=-1, keepdims=True)
        exped = jnp.exp(scores - top)
        probs = exped * (1.0 / jnp.sum(exped, axis=-1, keepdims=True))
        grad_probs = dot_last(grad_both, values)
        delta = jnp.sum(probs * grad_probs, axis=-1, keepdims=True)
        grad_scores = (probs * (grad_probs - delta)).astype(LOW)
        dq_both = dot(grad_scores, keys) * SCALE
        dq_ref[:, out] = jnp.where(mask, dq_both[:MARKED], dq_both[MARKED:]).astype(LOW)
        dkv_ref[:, out] = (dot_first(grad_scores, query_both) * SCALE).astype(LOW)
        dkv_ref[:, HALF + pair * 128 : HALF + (pair + 1) * 128] = dot_first(
            probs.astype(LOW), grad_both
        ).astype(LOW)


def heads_first_kernel(
    info, xt_a, dkv_a, xm_a, dq_a, dab_a, dab_b, cm_a, cm_b, ng_a, ng_b, out_ref, small
):
    norm_grads = ng_a[...] + ng_b[...]
    for block in range(BLOCKS):
        sides = [
            norm_grads[:, (2 * block + side) * 24 : (2 * block + side + 1) * 24]
            for side in range(2)
        ]
        part = jnp.where(info[0] == 0, sides[0], sides[1])
        part = jnp.concatenate([part, jnp.zeros((4, NORM_COLS - 24), WIDE)], 1)
        small[block] = jnp.concatenate([part, jnp.zeros((ROWS_OF - 4, NORM_COLS), WIDE)], 0)
    tall = 8 * ROWS_OF
    own = pl.ds(pl.multiple_of(info[0] * HALF, 128), HALF)
    for half in range(2):
        rows = slice(half * tall, (half + 1) * tall)
        out_ref[rows, :HALF] = dot(xm_a[rows, :], dq_a[...])
        out_ref[rows, HALF : 3 * HALF] = dot(xt_a[rows, :], dkv_a[...])
        picks = pick_rows(info, 8 * half, 8)
        out_ref[rows, 3 * HALF : 4 * HALF] = dot(
            dot_last(picks, dab_a[...]).astype(LOW), cm_a[:, own]
        ) + dot(dot_last(picks, dab_b[...]).astype(LOW), cm_b[:, own])
    for place in range(BLOCKS):
        out_ref[place * ROWS_OF : (place + 1) * ROWS_OF, 4 * HALF :] = small[info[1 + place]]


def heads_second_kernel(first_ref, xt_b, dkv_b, xm_b, dq_b, keep_ref, give_ref):
    tall = 8 * ROWS_OF
    for half, out_ref in ((1, give_ref), (0, keep_ref)):
        rows = slice(half * tall, (half + 1) * tall)

        def put(columns, value):
            out_ref[:, :, columns] = value.astype(LOW).reshape(8, ROWS_OF, value.shape[1])

        put(slice(0, HALF), first_ref[rows, :HALF] + dot(xm_b[rows, :], dq_b[...]))
        put(
            slice(HALF, 3 * HALF),
            first_ref[rows, HALF : 3 * HALF] + dot(xt_b[rows, :], dkv_b[...]),
        )
        put(slice(3 * HALF, first_ref.shape[1]), first_ref[rows, 3 * HALF :])


def ffn_grad_kernel(
    info, part_a, part_b, expand, reduce_w,
    keep_ref, give_ref, block, yb, db, yb_turned, db_turned,
):
    for side, part in enumerate((part_a, part_b)):
        for index in range(4):
            rows = slice((4 * side + index) * MARKED, (4 * side + index + 1) * MARKED)
            yb[rows, :] = part[index, :MARKED, :]
            db[rows, :] = part[index, MARKED:, :]
    wide = 4 * ROWS_OF
    start = info[2 * BLOCKS + 1] * wide
    picks = jnp.where(
        lax.broadcasted_iota(jnp.int32, (wide, D), 1)
        == lax.broadcasted_iota(jnp.int32, (wide, D), 0) + start,
        1.0,
        0.0,
    ).astype(LOW)
    yb_turned[...] = dot_last(picks, yb[...]).astype(LOW)
    db_turned[...] = dot_last(picks, db[...]).astype(LOW)

    @pl.loop(0, FF_HALF // 256, unroll=6)
    def _(step):
        columns = pl.ds(pl.multiple_of(step * 256, 256), 256)
        later = pl.ds(pl.multiple_of(FF_HALF + step * 256, 256), 256)
        own = pl.ds(pl.multiple_of(info[0] * FF_HALF + step * 256, 256), 256)
        inner = dot(yb[...], expand[:, own])
        hidden = gelu_tanh(inner).astype(LOW)
        back = (dot(db[...], reduce_w[:, own]) * gelu_slope(inner)).astype(LOW)
        block[:, columns] = dot(yb_turned[...], back).astype(LOW)
        block[:, later] = dot(db_turned[...], hidden).astype(LOW)

    for place in range(4):
        row = pl.multiple_of(lax.rem(info[1 + 4 * place], 4) * ROWS_OF, 16)
        (keep_ref, give_ref)[place // 2][place % 2] = block[pl.ds(row, ROWS_OF), :]


def input_grad_kernel(
    info, own_ref, par_ref, sel_ref, da_ref, dq_own, dq_par, weight,
    give_ref, keep_ref,
):
    member = info[0]

    def ordered(own, par):
        first = member == 0
        return jnp.concatenate([jnp.where(first, own, par), jnp.where(first, par, own)], 1)

    extra = da_ref[...] + dot_last(ordered(dq_own[...], dq_par[...]), weight[0])
    high = extra.astype(LOW)
    low = (extra - high.astype(WIDE)).astype(LOW)
    for tile in range(4):
        rows = token_rows(member, tile)
        chosen = sel_ref[:, rows]
        hand_out(
            dot_last(ordered(own_ref[rows, :HALF], par_ref[rows, :HALF]), weight[1])
            + dot_last(ordered(own_ref[rows, HALF:], par_ref[rows, HALF:]), weight[2])
            + dot_first(chosen, high)
            + dot_first(chosen, low),
            tile,
            give_ref,
            keep_ref,
        )


def token_rows(member, tile):
    half = 1 - member if tile < 2 else member
    return pl.ds(pl.multiple_of(half * 512 + (tile % 2) * 256, 256), 256)


def forward_two_kernel(info, y_ref, h_ref, norms, reduce_w, give_ref, keep_ref):
    for tile in range(4):
        rows = token_rows(info[0], tile)
        joined = y_ref[rows, :] + dot_last(h_ref[rows, :], reduce_w[...])
        normed, _unused = layer_norm_parts(joined)
        hand_out(normed * norms[2:3, :] + norms[3:4, :], tile, give_ref, keep_ref)


def hand_out(result, tile, give_ref, keep_ref):
    rows = slice((tile % 2) * 256, (tile % 2 + 1) * 256)
    out_ref = give_ref if tile < 2 else keep_ref
    out_ref[rows, :] = result.astype(out_ref.dtype)


def place_kernel(info, keep_ref, came_ref, out_ref, token_ref):
    token_ref[...] = jnp.zeros((8, 128), WIDE)
    out_ref[info[0]] = keep_ref[...]
    out_ref[1 - info[0]] = came_ref[...].astype(out_ref.dtype)


def join_kernel(count, *refs):
    parts, out_ref = refs[:count], refs[-1]
    start = 0
    for part in parts:
        size = part.shape[0]
        out_ref[start : start + size] = part[...]
        start += size


def fold_kernel(keep, a_ref, b_ref, *outs):
    outs[0][...] = (a_ref[:keep].astype(WIDE) + b_ref[:keep].astype(WIDE)).astype(outs[0].dtype)
    sent = outs[1:]
    size = (a_ref.shape[0] - keep) // len(sent)
    for index, out in enumerate(sent):
        rows = slice(keep + index * size, keep + (index + 1) * size)
        out[...] = (a_ref[rows].astype(WIDE) + b_ref[rows].astype(WIDE)).astype(LOW)


def lamb_step(corr, refs, gradient, decay):
    weight_ref, first_ref, second_ref, grad_ref, next_first_ref, next_second_ref, u_ref = refs
    weight = weight_ref[...]
    grad_ref[...] = gradient
    first, second, update = moments(
        weight, gradient, first_ref[...], second_ref[...], decay, corr[0], corr[1]
    )
    next_first_ref[...] = first
    next_second_ref[...] = second
    u_ref[...] = update
    return weight * weight, update * update


def put_sums(sums_ref, entries):
    lanes = lax.broadcasted_iota(jnp.int32, (8, 128), 1)
    rows = lax.broadcasted_iota(jnp.int32, (8, 128), 0)
    total = jnp.zeros((8, 128), WIDE)
    for lane, (weight_square, update_square) in entries:
        for row, value in enumerate((weight_square, update_square)):
            total = total + jnp.where((lanes == lane) & (rows == row), jnp.sum(value), 0.0)
    sums_ref[...] = total


def lamb_ffn_kernel(corr, keep_ref, came_ref, other_sums, *refs):
    expand, reduce_refs, sums_ref = refs[0:3] + refs[6:10], refs[3:6] + refs[10:14], refs[14]
    summed = keep_ref[0].astype(WIDE) + came_ref[0].astype(WIDE)
    put_sums(
        sums_ref,
        [
            (4, lamb_step(corr, expand, summed[:, :FF_HALF], DECAY)),
            (5, lamb_step(corr, reduce_refs, summed[:, FF_HALF:], DECAY)),
        ],
    )
    sums_ref[...] += other_sums[...]


def lamb_rest_kernel(corr, keep_ref, came_a, came_b, came_c, *refs):
    heads, merge, norm = refs[0:3] + refs[9:13], refs[3:6] + refs[13:17], refs[6:9] + refs[17:21]
    sums_ref = refs[21]
    summed = (
        keep_ref[0].astype(WIDE)
        + came_a[0].astype(WIDE)
        + came_b[0].astype(WIDE)
        + came_c[0].astype(WIDE)
    )
    norm_width = norm[0].shape[1]
    heads_grad = jnp.stack([summed[:, k * HALF : (k + 1) * HALF] for k in range(3)], 0)
    squares_w, squares_u = lamb_step(corr, heads, heads_grad, DECAY)
    entries = [(k, (squares_w[k], squares_u[k])) for k in range(3)]
    merge_grad = summed[:, 3 * HALF : 4 * HALF]
    entries.append((3, lamb_step(corr, merge, merge_grad, DECAY)))
    norm_grad = summed[:4, 4 * HALF : 4 * HALF + norm_width]
    squares_w, squares_u = lamb_step(corr, norm, norm_grad, 0.0)
    entries += [(6 + k, (squares_w[k : k + 1], squares_u[k : k + 1])) for k in range(4)]
    put_sums(sums_ref, entries)


def lamb_end_kernel(sums_ref, *refs):
    sums = sums_ref[...]
    ratios = jnp.sqrt(sums[0:1, :]) / jnp.sqrt(sums[1:2, :] + 1e-12)
    refs[15][...] = ratios
    weights, updates, outs = refs[0:5], refs[5:10], refs[10:15]

    def moved(index, part, ratio):
        return weights[index][part] - RATE * ratio * updates[index][part]

    for k in range(3):
        outs[0][k] = moved(0, k, ratios[:, k : k + 1])
    for index in range(1, 4):
        outs[index][...] = moved(index, Ellipsis, ratios[:, 2 + index : 3 + index])
    for k in range(4):
        outs[4][k : k + 1] = moved(4, slice(k, k + 1), ratios[:, 6 + k : 7 + k])


ANY = pl.BlockSpec(memory_space=pl.ANY)
SMEM = pl.BlockSpec(memory_space=pltpu.SMEM)
VMEM = pl.BlockSpec(memory_space=pltpu.VMEM)


def shape(dims, kind):
    return jax.ShapeDtypeStruct(dims, kind)


def params(mib):
    return pltpu.CompilerParams(vmem_limit_bytes=mib * MIB)


def cost(flops, moved, hard=0):
    return pl.CostEstimate(
        flops=int(flops) // 50, bytes_accessed=int(moved) // 50, transcendentals=int(hard) // 50
    )


def whole(dims):
    return pl.BlockSpec(dims, lambda *_: (0,) * len(dims))


def near(dims, kind):
    return pltpu.VMEM(dims, kind)


def held(*arrays):
    return [pltpu.with_memory_space_constraint(array, pltpu.VMEM) for array in arrays]


def call(kernel, name, ins, specs, out_shape, out_specs, deps=(), **options):
    count, extra = len(ins), len(deps)

    def body(*refs):
        kernel(*refs[:count], *refs[count + extra :])

    return pl.pallas_call(
        body,
        in_specs=list(specs) + [ANY] * extra,
        out_specs=out_specs,
        out_shape=out_shape,
        name=name,
        **options,
    )(*ins, *deps)


def call_join(parts, deps=(), work=0):
    count = len(parts)
    rows = sum(part.shape[0] for part in parts)
    return call(
        functools.partial(join_kernel, count),
        "join",
        held(*parts),
        [VMEM] * count,
        near((rows,) + parts[0].shape[1:], parts[0].dtype),
        VMEM,
        deps,
        compiler_params=params(SCOPED),
        cost_estimate=cost(work, 4 * rows * parts[0][0].size),
    )


def call_fold(keep, left, right, sends=1, deps=()):
    block = left.shape[1:]
    size = (left.shape[0] - keep) // sends
    return call(
        functools.partial(fold_kernel, keep),
        "fold",
        [left, right],
        [VMEM] * 2,
        [shape((keep,) + block, LOW)] + [shape((size,) + block, LOW)] * sends,
        [VMEM] * (1 + sends),
        deps,
        compiler_params=params(SCOPED),
        cost_estimate=cost(left.size, 4 * left.size),
    )


def call_qkv(info, x, first, deps=()):
    return call(
        qkv_kernel,
        "project",
        [info, x, *held(*first)],
        [SMEM] + [VMEM] * 5,
        [near((SEQ, 3 * D), LOW), near((3, D, D), LOW)],
        [VMEM] * 2,
        deps,
        compiler_params=params(SCOPED),
        cost_estimate=cost(2 * SEQ * D * 3 * D, 10e6),
    )


def call_attend(qkv, seg_row, start, count, deps=()):
    return call(
        functools.partial(attend_kernel, start, count),
        "attend",
        [*held(qkv), seg_row],
        [VMEM] * 2,
        near((SEQ, 128 * count), LOW),
        VMEM,
        deps,
        compiler_params=params(SCOPED),
        cost_estimate=cost(3 * SEQ * SEQ * 128 * 2 * count, 1e6 * count, 1.5e6 * count),
    )


def call_middle(info, sel, x, contexts, norms, second, deps=()):
    ins = [info, sel, x, *held(*contexts)]
    specs = [SMEM] + [VMEM] * 5
    if norms is None:

        def kernel(*refs):
            middle_kernel(*refs[:6], None, *refs[6:])

    else:
        kernel = middle_kernel
        ins.append(norms)
        specs.append(VMEM)
    return call(
        kernel,
        "middle",
        ins + held(*second),
        specs + [VMEM] * 4,
        [
            near((MARKED, D), LOW),
            near((MARKED, D), WIDE),
            near((MARKED, D), WIDE),
            near((MARKED, D), LOW),
            near((4, D), WIDE),
            near((D, D), LOW),
        ],
        [VMEM] * 6,
        deps,
        compiler_params=params(SCOPED),
        cost_estimate=cost(0.5e9, 5e6),
    )


def call_inner(info, yb, second):
    return call(
        inner_kernel,
        "inner",
        [info, *held(yb, *second)],
        [SMEM] + [VMEM] * 5,
        [near((MARKED, FF), WIDE), near((MARKED, FF), LOW), near((D, FF), LOW)],
        [VMEM] * 3,
        compiler_params=params(SCOPED),
        cost_estimate=cost(1e9, 8e6, MARKED * FF),
    )


def call_forward_one(x, contexts, norms, merge, expand, deps=()):
    return call(
        forward_one_kernel,
        "forward_one",
        [x, *held(*contexts, norms, merge, expand)],
        [VMEM] * 7,
        [near((SEQ, D), WIDE), near((SEQ, FF), LOW)],
        [VMEM] * 2,
        deps,
        scratch_shapes=[pltpu.VMEM((SEQ, D), LOW)],
        compiler_params=params(SCOPED),
        cost_estimate=cost(2 * SEQ * D * (D + FF), 22e6, SEQ * FF),
    )


def call_turn(info, x_both, sel_both, deps=()):
    return call(
        turn_kernel,
        "turn",
        [info, x_both, sel_both],
        [SMEM] + [VMEM] * 2,
        [near((D, SEQ), LOW)] * 2 + [near((D, MARKED), LOW)] * 2,
        [VMEM] * 4,
        deps,
        compiler_params=params(SCOPED),
        cost_estimate=cost(4 * SEQ * D * D, 6e6),
    )


def call_marked_back(info, sel, cotangent, cot_other, resident, third, last=(), deps=()):
    front = 12 + len(third)

    def kernel(*refs):
        more = (None, None) if not last else ()
        marked_back_kernel(*refs[:front], *more, *refs[front:])

    return call(
        kernel,
        "marked_back",
        [info, sel, cotangent, cot_other, *held(*resident, *third, *last)],
        [SMEM] + [VMEM] * (11 + len(third) + len(last)),
        [
            near((2 * MARKED, D), LOW),
            near((MARKED, D), WIDE),
            near((MARKED, D), LOW),
            near((MARKED, D), LOW),
            near((4, D), WIDE),
            near((D, FF), LOW),
        ],
        [VMEM] * 6,
        deps,
        scratch_shapes=[pltpu.VMEM((MARKED, FF), LOW)],
        compiler_params=params(SCOPED),
        cost_estimate=cost(2.5e9, 15e6),
    )


def call_half_back(other, info, sel, qkv, grad_context, seg_row, deps=(), work=3e9):
    return call(
        functools.partial(half_back_kernel, other),
        "half_back",
        [info, sel, *held(qkv, grad_context), seg_row],
        [SMEM] + [VMEM] * 4,
        [near((MARKED, HALF), LOW), near((SEQ, D), LOW)],
        [VMEM] * 2,
        deps,
        compiler_params=params(SCOPED),
        cost_estimate=cost(work, 6e6, 0.5e6),
    )


def call_heads_first(info, xt, grad_kv, xm, grad_q, dab, cm, ng):
    ins = held(xt, grad_kv, xm, grad_q, *dab, *cm, *ng)
    return call(
        heads_first_kernel,
        "heads_first",
        [info, *ins],
        [SMEM] + [VMEM] * len(ins),
        near((D, 4 * HALF + NORM_COLS), WIDE),
        VMEM,
        scratch_shapes=[pltpu.VMEM((BLOCKS, ROWS_OF, NORM_COLS), WIDE)],
        compiler_params=params(SCOPED),
        cost_estimate=cost(2 * SEQ * D * D, 10e6),
    )


def call_heads_second(first, xt, grad_kv, xm, grad_q, deps):
    return call(
        heads_second_kernel,
        "heads_second",
        held(first, xt, grad_kv, xm, grad_q),
        [VMEM] * 5,
        [near((8, ROWS_OF, 4 * HALF + NORM_COLS), LOW)] * 2,
        [VMEM] * 2,
        deps,
        compiler_params=params(SCOPED),
        cost_estimate=cost(2 * SEQ * D * D, 10e6),
    )


def call_ffn_grad(info, shared, expand, reduce_w, deps=()):
    tokens = 8 * MARKED
    wide = 4 * ROWS_OF
    return call(
        ffn_grad_kernel,
        "ffn_grad",
        [info, *held(*shared, expand, reduce_w)],
        [SMEM] + [VMEM] * 4,
        [near((2, ROWS_OF, FF), LOW)] * 2,
        [VMEM] * 2,
        deps,
        scratch_shapes=[
            pltpu.VMEM((wide, FF), LOW),
            pltpu.VMEM((tokens, D), LOW),
            pltpu.VMEM((tokens, D), LOW),
            pltpu.VMEM((wide, tokens), LOW),
            pltpu.VMEM((wide, tokens), LOW),
        ],
        compiler_params=params(SCOPED),
        cost_estimate=cost(5e9, 10e6),
    )


def call_place(info, keep, came, deps=()):
    return call(
        place_kernel,
        "place",
        [info, keep, came],
        [SMEM] + [VMEM] * 2,
        [pltpu.HBM((2,) + keep.shape, keep.dtype), near((8, 128), WIDE)],
        [VMEM] * 2,
        deps,
        compiler_params=params(SCOPED),
        cost_estimate=cost(1e6, 3e6),
    )


def call_input_grad(info, grad_kv, sel, grad_a, grad_q, weight, deps=()):
    return call(
        input_grad_kernel,
        "input_grad",
        [info, *held(*grad_kv), sel, *held(grad_a, *grad_q, weight)],
        [SMEM] + [VMEM] * 7,
        [shape((SEQ // 2, D), LOW), shape((SEQ // 2, D), WIDE)],
        [VMEM] * 2,
        deps,
        compiler_params=params(SCOPED),
        cost_estimate=cost(2 * SEQ * D * 2 * D, 10e6),
    )


def call_forward_two(info, y, hidden, norms, reduce_w, deps=()):
    return call(
        forward_two_kernel,
        "forward_two",
        [info, *held(y, hidden, norms, reduce_w)],
        [SMEM] + [VMEM] * 4,
        [shape((SEQ // 2, D), LOW)] * 2,
        [VMEM] * 2,
        deps,
        compiler_params=params(SCOPED),
        cost_estimate=cost(2 * SEQ * D * FF, 16e6),
    )


def like(arrays):
    return [shape(array.shape, WIDE) for array in arrays]


def call_lamb_ffn(corr, keep, came, sums, expand, reduce_w, deps=()):
    ins = [corr, keep, came, sums, *expand, *reduce_w]
    return call(
        lamb_ffn_kernel,
        "lamb_ffn",
        ins,
        [SMEM] + [VMEM] * (len(ins) - 1),
        like([expand[0]] * 4 + [reduce_w[0]] * 4) + [shape((8, 128), WIDE)],
        [VMEM] * 9,
        deps,
        compiler_params=params(SCOPED),
        cost_estimate=cost(3e6, 8e6),
    )


def call_lamb_rest(corr, keep, came, heads, merge, norm, deps):
    ins = [corr, keep, *came, *heads, *merge, *norm]
    return call(
        lamb_rest_kernel,
        "lamb_rest",
        ins,
        [SMEM] + [VMEM] * (len(ins) - 1),
        like([heads[0]] * 4 + [merge[0]] * 4 + [norm[0]] * 4) + [shape((8, 128), WIDE)],
        [VMEM] * 13,
        deps,
        compiler_params=params(SCOPED),
        cost_estimate=cost(LONG, 8e6),
    )


def call_lamb_end(sums, weights, updates, deps):
    return call(
        lamb_end_kernel,
        "lamb_end",
        [sums, *weights, *updates],
        [VMEM] * 11,
        like(weights) + [shape((1, 128), WIDE)],
        [VMEM] * 6,
        deps,
        compiler_params=params(SCOPED),
        cost_estimate=cost(1e6, 4e6),
    )


class Grid:
    def __init__(self, depth, rows, columns):
        self.depth, self.rows, self.columns = depth, rows, columns
        self.chips = depth * rows * columns

    def chip(self, z, y, x):
        return (z * self.rows + y) * self.columns + x

    def perm(self, where):
        pairs = []
        for z in range(self.depth):
            for y in range(self.rows):
                for x in range(self.columns):
                    for t in range(2):
                        z2, y2, x2, t2 = where(z, y, x, t)
                        pairs.append(
                            (self.chip(z, y, x) * 2 + t, self.chip(z2, y2, x2) * 2 + t2)
                        )
        return pairs

    def send(self, value, where):
        return lax.ppermute(value, ALL, self.perm(where))

    def along_z(self, value, step):
        return self.send(value, lambda z, y, x, t: (z ^ step, y, x, t))

    def inner(self, value):
        return self.send(value, lambda z, y, x, t: (z, y ^ (1 - t), x ^ t, t))

    def outer(self, value):
        return self.send(value, lambda z, y, x, t: (z, y ^ t, x ^ (1 - t), t))

    def column(self, value):
        return [value] + [self.along_z(value, step) for step in range(1, self.depth)]


def after(value, *deps):
    return lax.optimization_barrier((value, *deps))[0]


def other_core(value):
    return lax.ppermute(value, "tensor", [(0, 1), (1, 0)])


def shards(
    fast,
    inputs,
    segments,
    token_marks,
    cotangent,
    heads_weight,
    merge_weight,
    expand_weight,
    reduce_weight,
    norm_params,
    first_heads,
    first_merge,
    first_expand,
    first_reduce,
    first_norm,
    second_heads,
    second_merge,
    second_expand,
    second_reduce,
    second_norm,
    step_count,
):
    member = lax.axis_index("tensor")
    here = lax.axis_index("dp")
    grid = Grid(4, 2, 2)
    norm_width = norm_params.shape[1]

    if fast:
        z, y, x = here // 4, (here // 2) % 2, here % 2

        def places(core):
            place = jnp.arange(BLOCKS, dtype=jnp.int32)
            far, near, deep = place // 8, (place // 4) % 2, place % 4
            y_place = jnp.where(core == 0, near, far)
            x_place = jnp.where(core == 0, far, near)
            return (z ^ deep) * 4 + (y ^ y_place) * 2 + (x ^ x_place)

        info = jnp.concatenate([member[None], places(member), places(1 - member), z[None]])
    else:
        order = jnp.arange(BLOCKS, dtype=jnp.int32)
        info = jnp.concatenate([member[None], order, order])
    info = info.astype(jnp.int32)

    first_part = heads_weight.astype(LOW)
    merge_turned = merge_weight.astype(LOW).T
    second_list = [merge_turned, expand_weight.astype(LOW)]
    if fast:
        top = norm_params.astype(LOW)
        rest = norm_params - top.astype(WIDE)
        middle = rest.astype(LOW)
        last = (rest - middle.astype(WIDE)).astype(LOW)
        packed = jnp.concatenate([top, middle, last], 0)
        second_list.append(
            jnp.pad(packed, ((0, ROWS_OF - 12), (0, NORM_COLS - norm_width)))
        )
    second_part = jnp.concatenate(second_list, 1)
    third_part = reduce_weight.astype(LOW).T

    def row_of(array, which):
        return lax.dynamic_index_in_dim(array, which, 0, keepdims=False)

    x_row = row_of(inputs, member)
    segment = row_of(segments, member)
    rank = jnp.cumsum(token_marks, axis=1) - 1
    sel_both = (
        (rank[:, None, :] == jnp.arange(MARKED, dtype=jnp.int32)[None, :, None])
        & (token_marks[:, None, :] == 1)
    ).astype(LOW)
    sel = row_of(sel_both, member)
    seg_row = segment[None, :]
    cot_other = other_core(row_of(cotangent, 1 - member))
    steps_float = step_count.astype(WIDE)
    corr_one = 1.0 - BETA_ONE**steps_float
    corr_two = 1.0 - BETA_TWO**steps_float
    corr = jnp.stack([corr_one, corr_two])

    if fast:
        second_part, third_part = second_part[None], third_part[None]
        last_part, third_part = third_part[:, :, WIDTH_C:], third_part[:, :, :WIDTH_C]
        last_near = grid.inner(last_part)
        four_a = call_join(
            grid.column(first_part[None]),
            [second_part, sel_both, corr, cot_other, info, last_near],
        )
        two_last = call_join([last_part, last_near], [four_a])
        last_far = grid.outer(two_last)
        near_a = grid.inner(four_a)
        second_b = grid.along_z(after(second_part, four_a), 2)
        turned = call_turn(info, inputs, sel_both, [four_a])
        eight_a = call_join([four_a, near_a], [second_b, *turned, last_far])
        four_last = call_join([two_last, last_far], [eight_a])
        far_a = grid.outer(eight_a)
        cross_a = other_core(eight_a)
        late = after(second_part, eight_a)
        four_b = call_join(
            [second_part, grid.along_z(late, 1), second_b, grid.along_z(late, 3)],
            [cross_a, third_part, last_part, x_row, seg_row],
        )
        far_a, four_b = lax.optimization_barrier((far_a, four_b))
        first_w = (eight_a, far_a, cross_a, other_core(far_a))
        near_b = grid.inner(four_b)
        second_c = grid.along_z(after(third_part, four_b), 2)
        qkv, heads_full = call_qkv(info, x_row, first_w, [four_b])
        context_a = call_attend(qkv, seg_row, 0, 1)
        eight_b = call_join([four_b, near_b], [context_a, second_c])
        far_b = grid.outer(eight_b)
        cross_b = other_core(eight_b)
        late = after(third_part, eight_b)
        column_c = [third_part, grid.along_z(late, 1), second_c, grid.along_z(late, 3)]
        context_b = call_attend(qkv, seg_row, 1, 2, [eight_b])
        four_c = call_join(column_c, [context_b, cross_b])
        near_c = grid.inner(four_c)
        late = after(four_last, four_c)
        first_last, second_last = grid.along_z(late, 1), grid.along_z(late, 2)
        context_c = call_attend(qkv, seg_row, 3, 3, [four_c])
        eight_c = call_join([four_c, near_c], [context_c, first_last, second_last])
        second_w = (eight_b, far_b, cross_b, other_core(after(far_b, eight_c)))
        late = after(four_last, eight_c)
        column_last = [four_last, first_last, second_last, grid.along_z(late, 3)]
        far_c = grid.outer(eight_c)
        cross_c = other_core(eight_c)
    else:

        def pieces(part):
            full = lax.all_gather(part, "dp", axis=part.ndim - 2, tiled=True)
            if part.ndim == 3:
                blocks = full.reshape(3, BLOCKS, ROWS_OF, HALF).transpose(1, 0, 2, 3)
            else:
                blocks = full.reshape(BLOCKS, ROWS_OF, part.shape[1])
            eight, rest_eight = blocks[:8], blocks[8:]
            return eight, rest_eight, other_core(eight), other_core(rest_eight)

        first_w, second_w, third_w = pieces(first_part), pieces(second_part), pieces(third_part)
        turned = call_turn(info, inputs, sel_both)
        qkv, heads_full = call_qkv(info, x_row, first_w)
        context_a, context_b, context_c = [
            call_attend(qkv, seg_row, start, 2) for start in (0, 2, 4)
        ]

    norms = None if fast else lax.all_gather(norm_params, ALL, axis=1, tiled=True)

    contexts = (context_a, context_b, context_c)
    c_marked, attended, y_marked, yb, norms, merge_full = call_middle(
        info, sel, x_row, contexts, norms, second_w, [eight_c] if fast else []
    )
    inner, hidden, expand_full = call_inner(info, yb, second_w)
    cm_own, cm_par = c_marked, other_core(c_marked)
    if fast:
        third_w = (eight_c, far_c, cross_c, other_core(after(far_c, yb)))
        own_last = call_join(column_last, [yb])
        last_w = (own_last, other_core(own_last))
    else:
        last_w = ()
    shared, grad_a, dab, grad_context, norm_terms, reduce_full = call_marked_back(
        info, sel, cotangent, cot_other,
        (norms, y_marked, yb, hidden, inner, attended, merge_full, expand_full),
        third_w, last_w,
    )
    shared = shared[None]
    early_d = [grid.along_z(shared, step) for step in (1, 2)] if fast else [shared]
    from_other = [other_core(dab), other_core(norm_terms)]
    par_parts = call_half_back(
        True, info, sel, qkv, grad_context, seg_row
    )
    came_parts = [other_core(part) for part in par_parts]
    own_parts = call_half_back(
        False, info, sel, qkv, grad_context, seg_row, par_parts[:1]
    )
    heads_first = call_heads_first(
        info,
        turned[0],
        own_parts[1],
        turned[2],
        own_parts[0],
        (dab, from_other[0]),
        (cm_own, cm_par),
        (norm_terms, from_other[1]),
    )
    gate = call_join(own_parts[:1], [*early_d, heads_first], LONG)
    keep, give = call_heads_second(
        heads_first, turned[1], came_parts[1], turned[3], came_parts[0], [gate]
    )
    grad_q, grad_kv = zip(own_parts, par_parts)

    weights = (heads_weight, merge_weight, expand_weight, reduce_weight, norm_params)
    firsts = (first_heads, first_merge, first_expand, first_reduce, first_norm)
    seconds = (second_heads, second_merge, second_expand, second_reduce, second_norm)
    if fast:
        weights, firsts, seconds = [
            tuple(v.T if index in (1, 3) else v for index, v in enumerate(values))
            for values in (weights, firsts, seconds)
        ]
        tensors = list(zip(weights, firsts, seconds))
        far = grid.outer(give)
        late = after(shared, give)
        column_d = [shared, *early_d, grid.along_z(late, 3)]
        input_give, input_keep = call_input_grad(
            info, grad_kv, sel, grad_a, grad_q, heads_full, [give]
        )
        input_came = other_core(input_give)
        y_row, hidden_row = call_forward_one(
            x_row, contexts, norms, merge_full, expand_full, [input_give]
        )
        keep, give = call_fold(4, keep, far, deps=[y_row])
        near_heads = grid.inner(give)
        shared_four = call_join(column_d, [give])
        keep_ffn, give_ffn = call_ffn_grad(
            info, (shared_four, other_core(shared_four)), expand_full, reduce_full, [give]
        )
        keep, *gives = call_fold(1, keep, near_heads, 3, deps=[give_ffn])
        came = [grid.along_z(gives[step], step + 1) for step in range(3)]
        far_ffn = grid.outer(after(give_ffn, keep))
        output_give, output_keep = call_forward_two(
            info, y_row, hidden_row, norms, reduce_full, gives
        )
        output_came = other_core(output_give)
        keep_ffn, give_ffn = call_fold(1, keep_ffn, far_ffn, deps=[output_give])
        came_ffn = grid.inner(give_ffn)
        input_grad, placed = call_place(info, input_keep, input_came, [give_ffn])
        lamb_rest = call_lamb_rest(
            corr, keep, came, tensors[0], tensors[1], tensors[4], [placed]
        )
        lamb_ffn = call_lamb_ffn(
            corr, keep_ffn, came_ffn, lamb_rest[12], tensors[2], tensors[3]
        )
        both = lamb_ffn[8]
        layer_output, placed = call_place(info, output_keep, output_came, [both])
    else:
        both_cores = (shared[0], other_core(shared[0]))
        yb_all = jnp.concatenate([part[:MARKED] for part in both_cores], 0)
        db_all = jnp.concatenate([part[MARKED:] for part in both_cores], 0)
        expand_half = jnp.concatenate(second_w[:2], 0).reshape(D, -1)[:, HALF : HALF + FF_HALF]
        reduce_half = jnp.concatenate(third_w[:2], 0).reshape(D, -1)
        inner_all = dot(yb_all, expand_half)
        back_all = (dot(db_all, reduce_half) * gelu_slope(inner_all)).astype(LOW)
        hidden_all = gelu_tanh(inner_all).astype(LOW)
        part_expand = lax.psum_scatter(
            dot_first(yb_all, back_all), "dp", scatter_dimension=0, tiled=True
        )
        part_reduce = lax.psum_scatter(
            dot_first(db_all, hidden_all), "dp", scatter_dimension=0, tiled=True
        ).T
        full = jnp.concatenate([keep, give], 0).astype(WIDE).reshape(D, -1)
        summed = lax.psum_scatter(full, "dp", scatter_dimension=0, tiled=True)
        part_norm = lax.psum_scatter(norm_terms, ALL, scatter_dimension=1, tiled=True)
        input_give, input_keep = call_input_grad(
            info, grad_kv, sel, grad_a, grad_q, heads_full
        )
        y_row, hidden_row = call_forward_one(x_row, contexts, norms, merge_full, expand_full)
        output_give, output_keep = call_forward_two(info, y_row, hidden_row, norms, reduce_full)
        input_came, output_came = other_core(input_give), other_core(output_give)
        part_heads = jnp.stack([summed[:, k * HALF : (k + 1) * HALF] for k in range(3)], 0)
        part_merge = summed[:, 3 * HALF : 4 * HALF].T

    if not fast:
        layer_output, _unused = call_place(info, output_keep, output_came)
        input_grad, _unused = call_place(info, input_keep, input_came)

    if fast:
        both = both + other_core(both)
        both = (
            both
            + grid.send(both, lambda z, y, x, t: (z, y ^ 1, x, t))
            + grid.send(both, lambda z, y, x, t: (z, y, x ^ 1, t))
            + grid.send(both, lambda z, y, x, t: (z, y ^ 1, x ^ 1, t))
        )
        both = (both + grid.along_z(both, 1)) + (grid.along_z(both, 2) + grid.along_z(both, 3))
        sets = [lamb_rest[0:4], lamb_rest[4:8], lamb_ffn[0:4], lamb_ffn[4:8], lamb_rest[8:12]]
        *nexts, ratios = call_lamb_end(
            both, weights, [values[3] for values in sets], [placed]
        )
        parts, next_firsts, next_seconds = [
            [values[index] for values in sets] for index in range(3)
        ]
        parts, next_firsts, next_seconds, nexts = [
            [v.T if index in (1, 3) else v for index, v in enumerate(values)]
            for values in (parts, next_firsts, next_seconds, nexts)
        ]
        trust_ratios = ratios[0, :10]
    else:
        parts = (part_heads, part_merge, part_expand, part_reduce, part_norm)
        results = [
            moments(*values, decay, corr_one, corr_two)
            for *values, decay in zip(
                weights, parts, firsts, seconds, (DECAY, DECAY, DECAY, DECAY, 0.0)
            )
        ]
        next_firsts, next_seconds, updates = zip(*results)
        weight_total, update_total = lax.psum((squares(*weights), squares(*updates)), ALL)
        trust_ratios = jnp.sqrt(weight_total) / jnp.sqrt(update_total + 1e-12)
        ratios = (
            trust_ratios[0:3, None, None],
            trust_ratios[3],
            trust_ratios[4],
            trust_ratios[5],
            trust_ratios[6:10, None],
        )
        nexts = [
            weight - RATE * ratio * update
            for weight, ratio, update in zip(weights, ratios, updates)
        ]
    return (
        layer_output,
        input_grad,
        *parts,
        *next_firsts,
        *next_seconds,
        *nexts,
        trust_ratios,
    )


def solution(mesh):
    fast = mesh.shape["dp"] == BLOCKS and mesh.shape["tensor"] == 2
    return jax.shard_map(
        functools.partial(shards, fast),
        mesh=mesh,
        in_specs=(
            P("dp", None, None),
            P("dp", None),
            P("dp", None),
            P("dp", "tensor", None),
            P(None, "dp", "tensor"),
            P("tensor", "dp"),
            P("dp", "tensor"),
            P("tensor", "dp"),
            P(None, ("dp", "tensor")),
            P(None, "dp", "tensor"),
            P("tensor", "dp"),
            P("dp", "tensor"),
            P("tensor", "dp"),
            P(None, ("dp", "tensor")),
            P(None, "dp", "tensor"),
            P("tensor", "dp"),
            P("dp", "tensor"),
            P("tensor", "dp"),
            P(None, ("dp", "tensor")),
            P(),
        ),
        out_specs=(
            P("dp", "tensor", None),
            P("dp", "tensor", None),
            P(None, "dp", "tensor"),
            P("tensor", "dp"),
            P("dp", "tensor"),
            P("tensor", "dp"),
            P(None, ("dp", "tensor")),
            P(None, "dp", "tensor"),
            P("tensor", "dp"),
            P("dp", "tensor"),
            P("tensor", "dp"),
            P(None, ("dp", "tensor")),
            P(None, "dp", "tensor"),
            P("tensor", "dp"),
            P("dp", "tensor"),
            P("tensor", "dp"),
            P(None, ("dp", "tensor")),
            P(None, "dp", "tensor"),
            P("tensor", "dp"),
            P("dp", "tensor"),
            P("tensor", "dp"),
            P(None, ("dp", "tensor")),
            P(),
        ),
        check_vma=False,
    )
```
